32 devices in a mesh: batch: 8 (over z, x), chan: 4 (over y, core).
Axes of the slice: x: 2, y: 2, z: 4, core: 2. Of those that a mesh axis runs over, the one named last changes fastest.
Arguments:
- features: bfloat16 [192, 9, 9, 2048], P('batch', None, None, 'chan'), may hold values from -6 to 6
- w_reduce: bfloat16 [2048, 1024], P(None, 'chan'), may hold values from -0.125 to 0.125
- gain_one: float32 [1024], P('chan'), may hold values from 0.25 to 1.75
- shift_one: float32 [1024], P('chan'), may hold values from -1.5 to 1.5
- w_group: bfloat16 [3, 3, 32, 1024], P(None, None, None, 'chan'), may hold values from -0.375 to 0.375
- gain_two: float32 [1024], P('chan'), may hold values from 0.25 to 1.75
- shift_two: float32 [1024], P('chan'), may hold values from -1.5 to 1.5
- w_expand: bfloat16 [1024, 2048], P('chan'), may hold values from -0.1875 to 0.1875
- gain_three: float32 [2048], replicated, may hold values from 0.25 to 1.75
- shift_three: float32 [2048], replicated, may hold values from -1.5 to 1.5
- cotangent: bfloat16 [192, 9, 9, 2048], P('batch'), may hold values from -6 to 6
- resolution: int32 [8], P('batch'), may hold values from 5 to 9, as said below
- crop_count: int32 [8], P('batch'), may hold values from 18 to 24, as said below
Outputs:
- block_out: bfloat16 [192, 9, 9, 2048], P('batch', None, None, 'chan')
- features_grad: float32 [192, 9, 9, 2048], P('batch', None, None, 'chan')
- reduce_grad: float32 [2048, 1024], P(None, 'chan')
- gain_one_grad: float32 [1024], P('chan')
- shift_one_grad: float32 [1024], P('chan')
- group_grad: float32 [3, 3, 32, 1024], P(None, None, None, 'chan')
- gain_two_grad: float32 [1024], P('chan')
- shift_two_grad: float32 [1024], P('chan')
- expand_grad: float32 [1024, 2048], P('chan')
- gain_three_grad: float32 [2048], P('chan')
- shift_three_grad: float32 [2048], P('chan')
The draws below stay inside these ranges and needn't reach their ends.
Inputs may be any that keep to these rules, and one draw needn't show every extreme that they name: `resolution`: each entry is 5, 7 or 9, and some batch rank has 9 in every draw. `crop_count`: some batch rank uses all 24 slots in every draw.
All inputs are finite; a program needn't handle non-finite values.
Results may differ from the reference program's by a relative error of at most 0.018.
Values may be sent and summed in bfloat16 or wider, within the bound.
No kernel may reach another device: no remote copies, remote signals or barrier semaphores. Data moves between devices by JAX's collectives and lax.ppermute only.
A program may use at most 192 MiB of HBM per device.

```python
import jax
import jax.numpy as jnp
from jax import lax

CH = 2048
GROUPS = 32
GWIDTH = 32
SIDE = 9
CROPS = 24
WIDTH = 1024
CROPS_ALL = 192
N_BATCH = 8


def draw_resolution(key, part):
    key = jax.random.fold_in(key, 11)
    side_key, pick_key = jax.random.split(key)
    side_values = 5 + 2 * jax.random.randint(side_key, (N_BATCH,), 0, 3)
    chosen = jax.random.randint(pick_key, (), 0, N_BATCH)
    return jnp.where(jnp.arange(N_BATCH) == chosen, 9, side_values).astype(jnp.int32)


def draw_crop_count(key, part):
    key = jax.random.fold_in(key, 23)
    count_key, pick_key = jax.random.split(key)
    lowest = max(1, CROPS * 3 // 4)
    count_values = jax.random.randint(count_key, (N_BATCH,), lowest, CROPS + 1)
    chosen = jax.random.randint(pick_key, (), 0, N_BATCH)
    return jnp.where(jnp.arange(N_BATCH) == chosen, CROPS, count_values).astype(jnp.int32)


def block_scale(own_key, dims, pieces, least, high):
    loudness = 1.0
    for axis_at, parts in pieces:
        heights = jax.random.uniform(jax.random.fold_in(jax.random.fold_in(own_key, 6), axis_at), (parts,), jnp.float32, least / len(pieces), high / len(pieces))
        loudness = loudness * jnp.repeat(jnp.exp(heights), dims[axis_at] // parts).reshape((-1,) + (1,) * (len(dims) - 1 - axis_at))
    return loudness


def noise(stream_key, shape, width, most, cuts=(), kind=jnp.bfloat16):
    drawn = jax.random.normal(stream_key, shape, jnp.float32) * width
    if len(cuts) > 0:
        drawn = block_scale(stream_key, shape, cuts, -0.22, 0.18) * drawn
    return jnp.clip(drawn, min=-most, max=most).astype(kind)


def setup_inputs(seed: int = 0) -> dict:
    arg_keys = jax.random.split(jax.random.key(seed), 14)
    return {
        "features": noise(arg_keys[0], (CROPS_ALL, SIDE, SIDE, CH), 1.0, 6.0, ((0, 8), (3, 4))),
        "w_reduce": noise(arg_keys[1], (CH, WIDTH), CH ** -0.5, 0.125, ((1, 4),)),
        "gain_one": jnp.clip(1.0 + 0.15 * jax.random.normal(arg_keys[2], (WIDTH,), jnp.float32), 0.25, 1.75),
        "shift_one": noise(arg_keys[3], (WIDTH,), 0.3, 1.5, ((0, 4),), jnp.float32),
        "w_group": noise(arg_keys[4], (3, 3, GWIDTH, WIDTH), (9 * GWIDTH) ** -0.5, 0.375, ((3, 4),)),
        "gain_two": jnp.clip(1.0 + 0.15 * jax.random.normal(arg_keys[5], (WIDTH,), jnp.float32), 0.25, 1.75),
        "shift_two": noise(arg_keys[6], (WIDTH,), 0.3, 1.5, ((0, 4),), jnp.float32),
        "w_expand": noise(arg_keys[7], (WIDTH, CH), WIDTH ** -0.5, 0.1875, ((0, 4),)),
        "gain_three": jnp.clip(1.0 + 0.15 * jax.random.normal(arg_keys[8], (CH,), jnp.float32), 0.25, 1.75),
        "shift_three": noise(arg_keys[9], (CH,), 0.3, 1.5, (), jnp.float32),
        "cotangent": noise(arg_keys[10], (CROPS_ALL, SIDE, SIDE, CH), 1.0, 6.0, ((0, 8),)),
        "resolution": draw_resolution(jax.random.fold_in(arg_keys[13], 71), 0),
        "crop_count": draw_crop_count(jax.random.fold_in(arg_keys[13], 71), 0),
    }


EPSILON = 1e-05
PRECISE = lax.Precision.HIGHEST

@jax.custom_vjp
def low(v):
    return lax.optimization_barrier(v.astype(jnp.bfloat16)).astype(jnp.float32)

@jax.custom_vjp
def low_back(v):
    return v

def low_keep(v):
    return (low(v), None)

def low_pass(kept, grad):
    return (grad,)

def back_keep(v):
    return (v, None)

def back_low(kept, grad):
    return (low(grad),)
low.defvjp(low_keep, low_pass)
low_back.defvjp(back_keep, back_low)

def smooth(values):
    return jax.nn.gelu(values, approximate=True)

def crop_mask(resolution, crop_count):
    crop_index = jnp.arange(CROPS_ALL, dtype=jnp.int32)
    rank_index = (crop_index // CROPS).astype(jnp.int32)
    edge = resolution[rank_index]
    filled = crop_index % CROPS < crop_count[rank_index]
    position = jnp.arange(SIDE, dtype=jnp.int32)
    inside = filled[:, None, None] & (position[None, :, None] < edge[:, None, None]) & (position[None, None, :] < edge[:, None, None])
    return inside.astype(jnp.float32).reshape(CROPS_ALL * SIDE * SIDE, 1)

def batch_norm(inputs, gain, shift, live_mask, live_total):
    first_sum = lax.optimization_barrier(jnp.sum(live_mask * inputs, axis=0))
    second_sum = lax.optimization_barrier(jnp.sum(live_mask * inputs * inputs, axis=0))
    centre = first_sum / live_total
    spread = second_sum / live_total - centre * centre
    return (inputs - centre) * lax.rsqrt(spread + EPSILON) * gain + shift

def group_conv(hidden, weights):
    shaped = hidden.reshape(CROPS_ALL, SIDE, SIDE, GROUPS, GWIDTH)
    padded = jnp.pad(shaped, ((0, 0), (1, 1), (1, 1), (0, 0), (0, 0)))
    kernel = weights.reshape(3, 3, GWIDTH, GROUPS, GWIDTH)
    result = jnp.zeros((CROPS_ALL, SIDE, SIDE, GROUPS, GWIDTH), jnp.float32)
    for row_shift in range(3):
        for col_shift in range(3):
            window = padded[:, row_shift:row_shift + SIDE, col_shift:col_shift + SIDE]
            result = result + jnp.einsum('cijgk,kgl->cijgl', window, kernel[row_shift, col_shift], precision=PRECISE)
    return result.reshape(CROPS_ALL * SIDE * SIDE, WIDTH)

def reference(features, w_reduce, gain_one, shift_one, w_group, gain_two, shift_two, w_expand, gain_three, shift_three, cotangent, resolution, crop_count):
    live_mask = crop_mask(resolution, crop_count)
    live_total = jnp.sum(live_mask)
    pixel_rows = CROPS_ALL * SIDE * SIDE

    def forward(inputs, reduce_w, gain_a, shift_a, group_w, gain_b, shift_b, expand_w, gain_c, shift_c):
        reduced = low_back(jnp.dot(inputs, reduce_w, precision=PRECISE))
        hidden_one = low(live_mask * smooth(batch_norm(reduced, gain_a, shift_a, live_mask, live_total)))
        grouped = low_back(group_conv(hidden_one, group_w))
        hidden_two = low(live_mask * smooth(batch_norm(grouped, gain_b, shift_b, live_mask, live_total)))
        expanded = low_back(jnp.dot(hidden_two, expand_w, precision=PRECISE))
        pre_out = batch_norm(expanded, gain_c, shift_c, live_mask, live_total) + inputs
        return live_mask * smooth(pre_out)
    output, pull_back = jax.vjp(forward, features.reshape(pixel_rows, CH).astype(jnp.float32), w_reduce.astype(jnp.float32), gain_one, shift_one, w_group.astype(jnp.float32), gain_two, shift_two, w_expand.astype(jnp.float32), gain_three, shift_three)
    grads = pull_back(cotangent.reshape(pixel_rows, CH).astype(jnp.float32))
    return (output.astype(jnp.bfloat16).reshape(CROPS_ALL, SIDE, SIDE, CH), grads[0].reshape(CROPS_ALL, SIDE, SIDE, CH), grads[1], grads[2], grads[3], grads[4], grads[5], grads[6], grads[7], grads[8], grads[9])
```

```python
import jax
import jax.numpy as jnp
from jax import lax
from jax.sharding import PartitionSpec as P

EPSILON = 1e-05
ROOT = 0.7978845608028654
CUBE = 0.044715
F32 = jnp.float32
BF16 = jnp.bfloat16


def act(v):
    t = jnp.tanh(ROOT * (v + CUBE * v * v * v))
    return 0.5 * v * (1.0 + t)


def act_slope(v):
    t = jnp.tanh(ROOT * (v + CUBE * v * v * v))
    return 0.5 * (1.0 + t) + 0.5 * v * (1.0 - t * t) * (ROOT * (1.0 + 3.0 * CUBE * v * v))


def dot(a, b):
    return jnp.dot(a, b, preferred_element_type=F32)


def dot_tn(a, b):
    return lax.dot_general(a, b, (((0,), (0,)), ((), ())), preferred_element_type=F32)


def dot_nt(a, b):
    return lax.dot_general(a, b, (((1,), (1,)), ((), ())), preferred_element_type=F32)


def swap(v, axis, size, k):
    return lax.ppermute(v, axis, [(i, i ^ k) for i in range(size)])


def batch_sum(v, size):
    spread = jnp.broadcast_to(v[None], (size,) + v.shape)
    return jnp.sum(lax.all_to_all(spread, "batch", 0, 0), axis=0)


def gather_chan(v, size):
    blocks = [v]
    bits = [1 << b for b in range(size.bit_length() - 1)]
    held = {0: v}
    for bit in reversed(bits):
        held.update({k | bit: swap(b, "chan", size, bit) for k, b in list(held.items())})
    return [held[k] for k in range(size)]


def scatter_chan(parts, size):
    bits = [1 << b for b in range(size.bit_length() - 1)]
    held = dict(enumerate(parts))
    for bit in bits:
        sent = {k: swap(held[k].astype(BF16), "chan", size, bit) for k in held if k & bit}
        held = {k: held[k] + sent[k | bit].astype(F32) for k in held if not k & bit}
    return held[0]


def reduce_batch(v, size):
    me = lax.axis_index("batch")
    bit = 1
    while bit < size:
        half = v.shape[0] // 2
        mine = (me // bit) % 2
        keep = lax.dynamic_slice_in_dim(v, mine * half, half, 0)
        send = lax.dynamic_slice_in_dim(v, (1 - mine) * half, half, 0)
        v = keep.astype(F32) + swap(send.astype(BF16), "batch", size, bit).astype(F32)
        bit *= 2
    return v.astype(BF16)


def spread_batch(v, size):
    me = lax.axis_index("batch")
    bit = size // 2
    while bit:
        other = swap(v, "batch", size, bit)
        mine = (me // bit) % 2
        v = jnp.where(
            mine == 0, jnp.concatenate([v, other], 0), jnp.concatenate([other, v], 0)
        )
        bit //= 2
    return v


def in_order(blocks, me):
    stacked = jnp.stack(blocks)
    return [
        lax.dynamic_index_in_dim(stacked, me ^ j, 0, keepdims=False) for j in range(len(blocks))
    ]


def dense_taps(w_group, width, group_width):
    taps = w_group.reshape(9, group_width, width)
    tiled = jnp.tile(taps, (1, width // group_width, 1))
    rows = lax.broadcasted_iota(jnp.int32, (width, width), 0) // group_width
    cols = lax.broadcasted_iota(jnp.int32, (width, width), 1) // group_width
    return jnp.where((rows == cols)[None], tiled, jnp.zeros_like(tiled))


def moments(first, gain_sums, live_total):
    centre = gain_sums[0] / live_total
    spread = gain_sums[1] / live_total - centre * centre
    return centre, lax.rsqrt(spread + EPSILON)


def sums(live, a, b):
    la = live * a
    return jnp.stack([jnp.sum(la, axis=0), jnp.sum(la * b, axis=0)])


def norm_back(live, d, zhat, scale, gain, totals, live_total):
    shift_sum, gain_sum = totals[0], totals[1]
    return live * (scale * gain) * (d - shift_sum / live_total - zhat * (gain_sum / live_total))


def taps_of(array, side):
    slots, width = array.shape[0] // (side * side), array.shape[1]
    padded = jnp.pad(array.reshape(side, side, slots, width), ((1, 1), (1, 1), (0, 0), (0, 0)))
    return [
        padded[a : a + side, b : b + side].reshape(array.shape) for a in range(3) for b in range(3)
    ]


def shards(n_batch, n_chan, *args):
    (features, w_reduce, gain_one, shift_one, w_group, gain_two, shift_two, w_expand,
     gain_three, shift_three, cotangent, resolution, crop_count) = args
    slots, side, _, share = features.shape
    width = w_reduce.shape[1]
    group_width = w_group.shape[2]
    rows = slots * side * side
    me = lax.axis_index("chan")
    others = range(n_chan)

    feats = features.transpose(1, 2, 0, 3).reshape(rows, share)
    row = lax.broadcasted_iota(jnp.int32, (rows, 1), 0)
    crop, j, i = row % slots, (row // slots) % side, row // (slots * side)
    live = ((crop < crop_count[0]) & (i < resolution[0]) & (j < resolution[0])).astype(F32)

    w_red_blocks = w_reduce.reshape(n_chan, share, width)
    w_exp_blocks = w_expand.reshape(width, n_chan, share)
    pick_red = lambda k: lax.dynamic_index_in_dim(w_red_blocks, me ^ k, 0, keepdims=False)
    pick_exp = lambda k: lax.dynamic_index_in_dim(w_exp_blocks, me ^ k, 1, keepdims=False)

    whole = gather_chan(feats, n_chan)
    w_cols = [pick_exp(0)] + [swap(pick_exp(k), "chan", n_chan, k) for k in others if k]
    w_rows = [pick_red(0)] + [swap(pick_red(k), "chan", n_chan, k) for k in others if k]

    reduced = sum(dot(whole[k], pick_red(k)) for k in others)
    count = jnp.broadcast_to(jnp.sum(live), (1, width))
    got = batch_sum(jnp.concatenate([sums(live, reduced, reduced), count]), n_batch)
    live_total = got[2, 0]
    centre_one, scale_one = moments(None, got, live_total)
    zhat_one = (reduced - centre_one) * scale_one
    normed_one = zhat_one * gain_one + shift_one
    hidden_one = (live * act(normed_one)).astype(BF16)

    taps = dense_taps(w_group, width, group_width)
    windows = taps_of(hidden_one, side)
    grouped = sum(dot(windows[t], taps[t]) for t in range(9))
    got = batch_sum(sums(live, grouped, grouped), n_batch)
    centre_two, scale_two = moments(None, got, live_total)
    zhat_two = (grouped - centre_two) * scale_two
    normed_two = zhat_two * gain_two + shift_two
    hidden_two = (live * act(normed_two)).astype(BF16)

    hidden_all = gather_chan(hidden_two, n_chan)
    expanded = sum(dot(hidden_all[k], w_cols[k]) for k in others)
    got = batch_sum(sums(live, expanded, expanded), n_batch)
    centre_three, scale_three = moments(None, got, live_total)
    gain_c = lax.dynamic_slice_in_dim(gain_three, me * share, share)
    shift_c = lax.dynamic_slice_in_dim(shift_three, me * share, share)
    cot = lax.dynamic_slice_in_dim(
        cotangent.transpose(1, 2, 0, 3).reshape(rows, -1), me * share, share, 1
    ).astype(F32)
    zhat_three = (expanded - centre_three) * scale_three
    pre_out = zhat_three * gain_c + shift_c + feats.astype(F32)
    block_out = (live * act(pre_out)).astype(BF16)
    d_pre = live * cot * act_slope(pre_out)
    totals_three = batch_sum(sums(live, d_pre, zhat_three), n_batch)
    d_expanded = norm_back(
        live, d_pre, zhat_three, scale_three, gain_c, totals_three, live_total
    ).astype(BF16)

    d_hidden_two = scatter_chan([dot_nt(d_expanded, w_cols[k]) for k in others], n_chan)
    expand_parts = jnp.stack([dot_tn(hidden_all[k], d_expanded) for k in others])
    d_normed_two = live * d_hidden_two * act_slope(normed_two)
    totals_two = batch_sum(sums(live, d_normed_two, zhat_two), n_batch)
    d_grouped = norm_back(
        live, d_normed_two, zhat_two, scale_two, gain_two, totals_two, live_total
    ).astype(BF16)

    back = taps_of(d_grouped, side)
    d_hidden_one = sum(dot_nt(back[8 - t], taps[t]) for t in range(9))
    d_normed_one = live * d_hidden_one * act_slope(normed_one)
    totals_one = batch_sum(sums(live, d_normed_one, zhat_one), n_batch)
    d_reduced = norm_back(
        live, d_normed_one, zhat_one, scale_one, gain_one, totals_one, live_total
    ).astype(BF16)

    d_red_all = gather_chan(d_reduced, n_chan)
    reduce_parts = jnp.concatenate([dot_tn(whole[k], d_reduced) for k in others])
    features_grad = d_pre + sum(dot_nt(d_red_all[k], w_rows[k]) for k in others)

    group_dense = jnp.stack([dot_tn(windows[t], d_grouped) for t in range(9)])
    groups = width // group_width
    same = jnp.arange(groups)[:, None] == (jnp.arange(width) // group_width)[None]
    group_part = jnp.sum(
        jnp.where(same[None, :, None], group_dense.reshape(9, groups, group_width, width), 0.0),
        axis=1,
    ).reshape(9 * group_width, width)

    step = width // n_batch
    by_rank = expand_parts.reshape(n_chan, n_batch, step, share).transpose(1, 0, 2, 3)
    mine = reduce_batch(by_rank.reshape(n_batch * n_chan * step, share), n_batch)
    mine = mine.reshape(n_chan, step, share)
    cols = [mine[0]] + [swap(mine[k], "chan", n_chan, k) for k in others if k]
    cols = jnp.concatenate(in_order(cols, me), axis=1)
    expand_grad = spread_batch(cols, n_batch).astype(F32)

    tail = jnp.concatenate([reduce_parts, group_part])
    tail = spread_batch(reduce_batch(tail, n_batch), n_batch).astype(F32)
    reduce_grad = jnp.concatenate(
        in_order([tail[k * share : (k + 1) * share] for k in others], me)
    )
    group_grad = tail[n_chan * share :].reshape(3, 3, group_width, width)

    shaped = lambda v: v.reshape(side, side, slots, share).transpose(2, 0, 1, 3)
    return (
        shaped(block_out),
        shaped(features_grad),
        reduce_grad,
        totals_one[1],
        totals_one[0],
        group_grad,
        totals_two[1],
        totals_two[0],
        expand_grad,
        totals_three[1],
        totals_three[0],
    )


def solution(mesh):
    in_specs = (
        P("batch", None, None, "chan"),
        P(None, "chan"),
        P("chan"),
        P("chan"),
        P(None, None, None, "chan"),
        P("chan"),
        P("chan"),
        P("chan", None),
        P(),
        P(),
        P("batch", None, None, None),
        P("batch"),
        P("batch"),
    )
    out_specs = (
        P("batch", None, None, "chan"),
        P("batch", None, None, "chan"),
        P(None, "chan"),
        P("chan"),
        P("chan"),
        P(None, None, None, "chan"),
        P("chan"),
        P("chan"),
        P("chan", None),
        P("chan"),
        P("chan"),
    )
    n_batch, n_chan = mesh.shape["batch"], mesh.shape["chan"]

    def run(*args):
        return shards(n_batch, n_chan, *args)

    return jax.shard_map(run, mesh=mesh, in_specs=in_specs, out_specs=out_specs, check_vma=False)
```

```python
import functools

import jax
import jax.numpy as jnp
from jax import lax
from jax.experimental import pallas as pl
from jax.experimental.pallas import tpu as pltpu
from jax.sharding import PartitionSpec as P

EPSILON = 1e-05
ROOT = 0.7978845608028654
CUBE = 0.044715
F32 = jnp.float32
BF16 = jnp.bfloat16
STEP = 256
LANES = 128
TN = (((0,), (0,)), ((), ()))
NT = (((1,), (1,)), ((), ()))
VM = pl.BlockSpec(memory_space=pltpu.VMEM)
SM = pl.BlockSpec(memory_space=pltpu.SMEM)


def dot(a, b):
    return jnp.dot(a, b, preferred_element_type=F32)


def dot_tn(a, b):
    return lax.dot_general(a, b, TN, preferred_element_type=F32)


def dot_nt(a, b):
    return lax.dot_general(a, b, NT, preferred_element_type=F32)


def bend(v):
    return jnp.tanh(v * (ROOT + (ROOT * CUBE) * (v * v)))


def act(v):
    half = 0.5 * v
    return half + half * bend(v)


def act_slope(v):
    t = bend(v)
    inner = v * (0.5 * ROOT + (1.5 * ROOT * CUBE) * (v * v))
    return 0.5 + 0.5 * t + inner * (1.0 - t * t)


def chunks(total, body, step=STEP):
    full = total // step

    def go(c, carry):
        body(pl.multiple_of(c * step, step), step)
        return carry

    if full:
        lax.fori_loop(0, full, go, 0)
    if total % step:
        body(full * step, total % step)


def fold(v):
    return jnp.sum(v.reshape(v.shape[0] // 8, 8, v.shape[1]), axis=0)


def widen(live, width):
    return jnp.concatenate([live] * (width // LANES), axis=1) if width > LANES else live


def norm_of(got, counts):
    s = jnp.sum(got[...], axis=0)
    share_of = 1.0 / jnp.sum(counts[...], axis=0)[2:3, 0:1]
    mu = s[0:1] * share_of
    return mu, lax.rsqrt(s[1:2] * share_of - mu * mu + EPSILON), share_of


def send_sums(out, acc):
    out[...] = jnp.broadcast_to(jnp.sum(acc[...], axis=1)[None], out.shape)


def near_kernel(dims, *refs):
    *feats, w, out = refs
    share = feats[0].shape[1]
    me = dims[2]
    ws = [w[pl.ds(pl.multiple_of((me ^ k) * share, share), share), :] for k in range(len(feats))]

    def body(o, n):
        out[pl.ds(o, n), :] = sum(dot(f[pl.ds(o, n), :], wk) for f, wk in zip(feats, ws))

    chunks(out.shape[0], body)


def far_kernel(halves, dims, live, part, *refs):
    *feats, w, out, spread, acc = refs
    share = feats[0].shape[1]
    half = part.shape[0] // halves
    me = dims[2]
    acc[...] = jnp.zeros_like(acc)
    ks = range(len(feats) // halves)
    ws = [w[pl.ds(pl.multiple_of((me ^ (k + 2)) * share, share), share), :] for k in ks]
    for h in range(halves):

        def body(o, n, h=h):
            rows = pl.ds(h * half + o, n)
            z = part[rows, :] + sum(dot(feats[k * halves + h][pl.ds(o, n), :], ws[k]) for k in ks)
            out[rows, :] = z
            m = widen(live[rows, :], z.shape[1])
            mz = m * z
            acc[0] += fold(mz)
            acc[1] += fold(mz * z)
            acc[2] += fold(m)

        chunks(half, body)
    send_sums(spread, acc)


def pad_edges(pad, side, line, wide, slots):
    width = pad.shape[1]
    pad[0:wide] = jnp.zeros((wide, width), F32)
    pad[(side + 1) * wide : (side + 2) * wide] = jnp.zeros((wide, width), F32)


def pad_line(pad, i, value, line, wide, slots):
    o = pl.multiple_of((i + 1) * wide, 8)
    edge = jnp.zeros((slots, pad.shape[1]), F32)
    pad[pl.ds(o, slots), :] = edge
    pad[pl.ds(o + slots, line), :] = value
    pad[pl.ds(o + slots + line, slots), :] = edge


def conv_line(pad, i, taps, line, wide, slots, flip):
    total = None
    for t in range(9):
        a, b = divmod(t, 3)
        o = pl.multiple_of((i + a) * wide + b * slots, 8)
        d = dot(pad[pl.ds(o, line), :].astype(BF16), taps[8 - t if flip else t])
        total = d if total is None else total + d
    return total


def conv_kernel(side, slots, live, z, got, gain, shift, taps, hid, out, spread, pad, acc):
    line, wide = side * slots, (side + 2) * slots
    rows, width = z.shape
    mu, r, _ = norm_of(got, got)
    a = r * gain[...]
    b = shift[...] - mu * a
    pad_edges(pad, side, line, wide, slots)
    acc[...] = jnp.zeros_like(acc)

    def fill(i, carry):
        here = pl.ds(pl.multiple_of(i * line, 8), line)
        h = widen(live[here, :], width) * act(z[here, :] * a + b)
        h = h.astype(BF16).astype(F32)
        hid[here, :] = h
        pad_line(pad, i, h, line, wide, slots)
        return carry

    lax.fori_loop(0, side, fill, 0)

    def conv(i, carry):
        here = pl.ds(pl.multiple_of(i * line, 8), line)
        total = conv_line(pad, i, taps, line, wide, slots, False)
        out[here, :] = total
        m = widen(live[here, :], width) * total
        acc[0] += fold(m)
        acc[1] += fold(m * total)
        return carry

    lax.fori_loop(0, side, conv, 0)
    used = side * line
    out[used:rows] = jnp.zeros((rows - used, width), F32)
    hid[used:rows] = jnp.zeros((rows - used, width), F32)
    send_sums(spread, acc)


def hidden_kernel(live, z, counts, got, gain, shift, out):
    mu, r, _ = norm_of(got, counts)
    a = r * gain[...]
    b = shift[...] - mu * a

    def body(o, n):
        rows = pl.ds(o, n)
        m = widen(live[rows, :], z.shape[1])
        out[rows, :] = (m * act(z[rows, :] * a + b)).astype(BF16)

    chunks(z.shape[0], body)


def slope_kernel(live, z, counts, got, gain, shift, out):
    mu, r, _ = norm_of(got, counts)
    a = r * gain[...]
    b = shift[...] - mu * a

    def body(o, n):
        rows = pl.ds(o, n)
        out[rows, :] = widen(live[rows, :], z.shape[1]) * act_slope(z[rows, :] * a + b)

    chunks(z.shape[0], body)


def expand_near_kernel(*refs):
    *ins, out = refs
    k = len(ins) // 2
    hs, ws = ins[:k], ins[k:]

    def body(o, n):
        out[pl.ds(o, n), :] = sum(dot(h[pl.ds(o, n), :], w[...]) for h, w in zip(hs, ws))

    chunks(out.shape[0], body)


def expand_far_kernel(live, part, *refs):
    *ins, out, spread, acc = refs
    k = len(ins) // 2
    hs, ws = ins[:k], ins[k:]
    acc[...] = jnp.zeros_like(acc)

    def body(o, n):
        rows = pl.ds(o, n)
        e = part[rows, :] + sum(dot(h[rows, :], w[...]) for h, w in zip(hs, ws))
        out[rows, :] = e
        m = widen(live[rows, :], e.shape[1]) * e
        acc[0] += fold(m)
        acc[1] += fold(m * e)

    chunks(out.shape[0], body)
    send_sums(spread, acc)


def third_kernel(live, e, counts, got, gain, shift, feats, cot, d_pre, spread, acc):
    mu, r, _ = norm_of(got, counts)
    acc[...] = jnp.zeros_like(acc)

    def body(o, n):
        rows = pl.ds(o, n)
        zhat = (e[rows, :] - mu) * r
        v = zhat * gain[...] + shift[...] + feats[rows, :].astype(F32)
        m = widen(live[rows, :], v.shape[1])
        d = m * cot[rows, :].astype(F32) * act_slope(v)
        d_pre[rows, :] = d
        acc[0] += fold(d)
        acc[1] += fold(d * zhat)

    chunks(e.shape[0], body, 128)
    send_sums(spread, acc)


def block_kernel(live, e, counts, got, gain, shift, feats, out):
    mu, r, _ = norm_of(got, counts)

    def body(o, n):
        rows = pl.ds(o, n)
        v = (e[rows, :] - mu) * r * gain[...] + shift[...] + feats[rows, :].astype(F32)
        out[rows, :] = (widen(live[rows, :], v.shape[1]) * act(v)).astype(BF16)

    chunks(out.shape[0], body)


def d_expanded_kernel(live, e, d_pre, counts, got, totals, gain, *refs):
    k = (len(refs) - 1) // 2
    ws, d_exp, outs = refs[:k], refs[k], refs[k + 1 :]
    mu, r, share_of = norm_of(got, counts)
    t = jnp.sum(totals[...], axis=0) * share_of
    scale = r * gain[...]

    def body(o, n):
        rows = pl.ds(o, n)
        zhat = (e[rows, :] - mu) * r
        m = widen(live[rows, :], zhat.shape[1])
        d = (m * scale * (d_pre[rows, :] - t[0:1] - zhat * t[1:2])).astype(BF16)
        d_exp[rows, :] = d
        for w, out in zip(ws, outs):
            out[rows, :] = dot_nt(d, w[...]).astype(out.dtype)

    chunks(e.shape[0], body)


def back_expand_kernel(d_exp, *refs):
    k = len(refs) // 2
    ws, outs = refs[:k], refs[k:]

    def body(o, n):
        rows = pl.ds(o, n)
        for w, out in zip(ws, outs):
            out[rows, :] = dot_nt(d_exp[rows, :], w[...]).astype(out.dtype)

    chunks(d_exp.shape[0], body)


def expand_grad_kernel(d_exp, *refs):
    *hs, out = refs
    for k, h in enumerate(hs):
        out[k] = dot_tn(h[...], d_exp[...]).astype(BF16)


def d_two_kernel(slope, z, counts, got, *refs):
    *terms, d_out, spread, acc = refs
    mu, r, _ = norm_of(got, counts)
    acc[...] = jnp.zeros_like(acc)

    def body(o, n):
        rows = pl.ds(o, n)
        d = sum(t[rows, :].astype(F32) for t in terms) * slope[rows, :]
        d_out[rows, :] = d
        acc[0] += fold(d)
        acc[1] += fold(d * ((z[rows, :] - mu) * r))

    chunks(z.shape[0], body)
    send_sums(spread, acc)


def conv_back_kernel(
    side, slots, live, d_two, grouped, got_two, totals, gain, slope, z, got, taps,
    d_grouped, d_one, spread, pad, acc,
):
    line, wide = side * slots, (side + 2) * slots
    rows, width = z.shape
    mu_two, r_two, share_of = norm_of(got_two, got)
    mu, r, _ = norm_of(got, got)
    t = jnp.sum(totals[...], axis=0) * share_of
    scale = r_two * gain[...]
    pad_edges(pad, side, line, wide, slots)
    acc[...] = jnp.zeros_like(acc)

    def fill(i, carry):
        here = pl.ds(pl.multiple_of(i * line, 8), line)
        zhat = (grouped[here, :] - mu_two) * r_two
        m = widen(live[here, :], width)
        d = m * scale * (d_two[here, :] - t[0:1] - zhat * t[1:2])
        d = d.astype(BF16).astype(F32)
        d_grouped[here, :] = d
        pad_line(pad, i, d, line, wide, slots)
        return carry

    lax.fori_loop(0, side, fill, 0)

    def conv(i, carry):
        here = pl.ds(pl.multiple_of(i * line, 8), line)
        d = conv_line(pad, i, taps, line, wide, slots, True) * slope[here, :]
        d_one[here, :] = d
        acc[0] += fold(d)
        acc[1] += fold(d * ((z[here, :] - mu) * r))
        return carry

    lax.fori_loop(0, side, conv, 0)
    used = side * line
    d_one[used:rows] = jnp.zeros((rows - used, width), F32)
    d_grouped[used:rows] = jnp.zeros((rows - used, width), F32)
    send_sums(spread, acc)


def d_reduced_kernel(live, d_one, z, got, totals, gain, out):
    mu, r, share_of = norm_of(got, got)
    t = jnp.sum(totals[...], axis=0) * share_of
    scale = r * gain[...]

    def body(o, n):
        rows = pl.ds(o, n)
        zhat = (z[rows, :] - mu) * r
        m = widen(live[rows, :], zhat.shape[1])
        out[rows, :] = (m * scale * (d_one[rows, :] - t[0:1] - zhat * t[1:2])).astype(BF16)

    chunks(z.shape[0], body)


def group_grad_kernel(side, slots, group_width, hid, d_grouped, out, pad):
    line, wide = side * slots, (side + 2) * slots
    width = hid.shape[1]
    pad_edges(pad, side, line, wide, slots)

    def fill(i, carry):
        here = pl.ds(pl.multiple_of(i * line, 8), line)
        pad_line(pad, i, hid[here, :], line, wide, slots)
        return carry

    lax.fori_loop(0, side, fill, 0)
    d = d_grouped[0 : side * line].astype(BF16)
    ids = [lax.broadcasted_iota(jnp.int32, (width, width), b) // group_width for b in range(2)]
    same = ids[0] == ids[1]
    for t in range(9):
        a, b = divmod(t, 3)
        starts = [(i + a) * wide + b * slots for i in range(side)]
        x = jnp.concatenate([pad[o : o + line].astype(BF16) for o in starts], axis=0)
        dense = jnp.where(same, dot_tn(x, d), 0.0)
        picked = jnp.sum(dense.reshape(width // group_width, group_width, width), axis=0)
        out[t * group_width : (t + 1) * group_width] = picked.astype(BF16)
    used = 9 * group_width
    out[used:] = jnp.zeros((out.shape[0] - used, width), BF16)


def reduce_grad_kernel(halves, dims, d_red, group_part, *refs):
    *feats, out = refs
    share = feats[0].shape[1]
    me = dims[2]
    half = d_red.shape[0] // halves
    for k in range(2):
        rows = pl.ds(pl.multiple_of((me ^ k) * share, share), share)
        out[rows, :] = dot_tn(feats[k][...], d_red[...]).astype(BF16)
    far = feats[2:]
    for k in range(len(far) // halves):
        rows = pl.ds(pl.multiple_of((me ^ (k + 2)) * share, share), share)
        out[rows, :] = sum(
            dot_tn(far[k * halves + h][...], d_red[h * half : (h + 1) * half])
            for h in range(halves)
        ).astype(BF16)
    base = out.shape[0] - group_part.shape[0]
    out[base:] = group_part[...]


def features_grad_kernel(part, *refs):
    *ins, out = refs
    k = len(ins) // 2
    ds, ws = ins[:k], ins[k:]

    def body(o, n):
        rows = pl.ds(o, n)
        out[rows, :] = part[rows, :] + sum(dot_nt(d[rows, :], w[...]) for d, w in zip(ds, ws))

    chunks(out.shape[0], body)


def call(kernel, outs, ins, scratch=(), flops=0, name=None, smem=False):
    moved = sum(x.size * x.dtype.itemsize for x in ins)
    moved += sum(int(o.size) * o.dtype.itemsize for o in outs)
    specs = [VM] * len(ins)
    if smem:
        specs[0] = SM
    got = pl.pallas_call(
        kernel,
        out_shape=list(outs),
        in_specs=specs,
        out_specs=[VM] * len(outs),
        scratch_shapes=list(scratch),
        compiler_params=pltpu.CompilerParams(vmem_limit_bytes=32 << 20),
        cost_estimate=pl.CostEstimate(flops=flops, bytes_accessed=moved, transcendentals=0),
        name=name,
    )(*ins)
    return got[0] if len(outs) == 1 else got


def swap(v, axis, size, k):
    return lax.ppermute(v, axis, [(i, i ^ k) for i in range(size)])


def batch_sum(spread):
    return lax.all_to_all(spread, "batch", 0, 0)


def gather_chan(v, size):
    held = {0: v}
    bit = size // 2
    while bit:
        held.update({k | bit: swap(b, "chan", size, bit) for k, b in list(held.items())})
        bit //= 2
    return [held[k] for k in range(size)]


def scatter_chan(parts, size):
    def terms(k, below):
        got, bit = [parts[k]], 1
        while bit < below:
            inner = terms(k | bit, bit)
            total = sum(t.astype(F32) for t in inner) if len(inner) > 1 else inner[0]
            got.append(swap(total.astype(BF16), "chan", size, bit))
            bit *= 2
        return got

    return terms(0, size)


def reduce_batch(v, size, axis):
    me = lax.axis_index("batch")
    bit = 1
    while bit < size:
        half = v.shape[axis] // 2
        mine = (me // bit) % 2
        keep = lax.dynamic_slice_in_dim(v, mine * half, half, axis)
        send = lax.dynamic_slice_in_dim(v, (1 - mine) * half, half, axis)
        v = (keep.astype(F32) + swap(send, "batch", size, bit).astype(F32)).astype(BF16)
        bit *= 2
    return v


def spread_batch(v, size, axis):
    me = lax.axis_index("batch")
    bit = size // 2
    while bit:
        other = swap(v, "batch", size, bit)
        mine = (me // bit) % 2
        v = jnp.where(
            mine == 0, jnp.concatenate([v, other], axis), jnp.concatenate([other, v], axis)
        )
        bit //= 2
    return v


def dense_taps(w_group, width, group_width):
    taps = w_group.reshape(9, group_width, width)
    tiled = jnp.tile(taps, (1, width // group_width, 1))
    rows = lax.broadcasted_iota(jnp.int32, (width, width), 0) // group_width
    cols = lax.broadcasted_iota(jnp.int32, (width, width), 1) // group_width
    return jnp.where((rows == cols)[None], tiled, jnp.zeros_like(tiled))


def shards(n_batch, n_chan, *args):
    (features, w_reduce, gain_one, shift_one, w_group, gain_two, shift_two, w_expand,
     gain_three, shift_three, cotangent, resolution, crop_count) = args
    slots, side, _, share = features.shape
    width = w_reduce.shape[1]
    group_width = w_group.shape[2]
    rows = slots * side * side
    padded = -(-rows // 32) * 32
    half = padded // 2
    halves = 2
    line, wide = side * slots, (side + 2) * slots
    me = lax.axis_index("chan")
    others = range(n_chan)
    shape = jax.ShapeDtypeStruct
    acc = lambda n, c: pltpu.VMEM((n, 8, c), F32)
    tall = pltpu.VMEM(((side + 2) * wide, width), F32)
    mm = 2 * padded * share * width

    feats = features.transpose(1, 2, 0, 3).reshape(rows, share)
    ends = ((0, padded - rows), (0, 0))
    pieces = [feats[:half], jnp.pad(feats[half:], ends)]
    moved = [gather_far(p, n_chan) for p in pieces]
    own = jnp.pad(feats, ends)
    beside = swap(own, "chan", n_chan, 1)
    far = [moved[h][k] for k in others if k > 1 for h in range(halves)]

    dims = jnp.stack([resolution[0], crop_count[0], me.astype(jnp.int32)])
    row = lax.broadcasted_iota(jnp.int32, (padded, LANES), 0)
    crop, j, i = row % slots, (row // slots) % side, row // line
    live = ((crop < crop_count[0]) & (i < resolution[0]) & (j < resolution[0])).astype(F32)
    cot = lax.dynamic_slice_in_dim(
        cotangent.transpose(1, 2, 0, 3).reshape(rows, -1), me * share, share, 1
    )
    cot = jnp.pad(cot, ends)
    taps = dense_taps(w_group, width, group_width)
    taps_back = taps.transpose(0, 2, 1)
    line_of = lambda v: v.reshape(1, -1)
    gain_one, shift_one, gain_two, shift_two = map(
        line_of, (gain_one, shift_one, gain_two, shift_two)
    )
    gain_c = line_of(lax.dynamic_slice_in_dim(gain_three, me * share, share))
    shift_c = line_of(lax.dynamic_slice_in_dim(shift_three, me * share, share))

    part = call(
        near_kernel, [shape((padded, width), F32)], [dims, own, beside, w_reduce],
        flops=2 * mm, name="near", smem=True,
    )
    z, spread = call(
        functools.partial(far_kernel, halves),
        [shape((padded, width), F32), shape((n_batch, 3, width), F32)],
        [dims, live, part, *far, w_reduce], [acc(3, width)],
        flops=(n_chan - 2) * mm, name="far", smem=True,
    )
    got_one = batch_sum(spread)

    w_red_blocks = w_reduce.reshape(n_chan, share, width)
    w_exp_blocks = w_expand.reshape(width, n_chan, share)
    pick_red = lambda k: lax.dynamic_index_in_dim(w_red_blocks, me ^ k, 0, keepdims=False)
    pick_exp = lambda k: lax.dynamic_index_in_dim(w_exp_blocks, me ^ k, 1, keepdims=False)
    w_cols = [pick_exp(0)] + [swap(pick_exp(k), "chan", n_chan, k) for k in others if k]
    w_rows = [pick_red(0)] + [swap(pick_red(k), "chan", n_chan, k) for k in others if k]

    hid, grouped, spread = call(
        functools.partial(conv_kernel, side, slots),
        [shape((padded, width), F32)] * 2 + [shape((n_batch, 2, width), F32)],
        [live, z, got_one, gain_one, shift_one, taps], [tall, acc(2, width)],
        flops=18 * padded * width * width, name="conv",
    )
    got_two = batch_sum(spread)
    hidden_two = call(
        hidden_kernel, [shape((padded, width), BF16)],
        [live, grouped, got_one, got_two, gain_two, shift_two], flops=mm, name="hidden",
    )
    hidden_all = gather_chan(hidden_two, n_chan)
    slope_two = call(
        slope_kernel, [shape((padded, width), F32)],
        [live, grouped, got_one, got_two, gain_two, shift_two], flops=mm, name="slope_two",
    )
    slope_one = call(
        slope_kernel, [shape((padded, width), F32)],
        [live, z, got_one, got_one, gain_one, shift_one], flops=mm, name="slope_one",
    )
    part = call(
        expand_near_kernel, [shape((padded, share), F32)], [*hidden_all[:2], *w_cols[:2]],
        flops=2 * mm, name="expand_near",
    )
    expanded, spread = call(
        expand_far_kernel, [shape((padded, share), F32), shape((n_batch, 2, share), F32)],
        [live, part, *hidden_all[2:], *w_cols[2:]], [acc(2, share)],
        flops=(n_chan - 2) * mm, name="expand_far",
    )
    got_three = batch_sum(spread)
    d_pre, spread = call(
        third_kernel, [shape((padded, share), F32), shape((n_batch, 2, share), F32)],
        [live, expanded, got_one, got_three, gain_c, shift_c, own, cot], [acc(2, share)],
        flops=4 * mm, name="third",
    )
    totals_three = batch_sum(spread)
    block_out = call(
        block_kernel, [shape((rows, share), BF16)],
        [live, expanded, got_one, got_three, gain_c, shift_c, own], flops=2 * mm, name="block",
    )

    odd = [k for k in reversed(others) if k % 2]
    even = [k for k in reversed(others) if k % 2 == 0]
    d_expanded, *sent = call(
        d_expanded_kernel,
        [shape((padded, share), BF16)] + [shape((padded, width), BF16)] * len(odd),
        [live, expanded, d_pre, got_one, got_three, totals_three, gain_c]
        + [w_cols[k] for k in odd],
        flops=(1 + len(odd)) * mm, name="d_expanded",
    )
    kept = call(
        back_expand_kernel, [shape((padded, width), F32)] * len(even),
        [d_expanded] + [w_cols[k] for k in even], flops=len(even) * mm, name="back_expand",
    )
    parts = dict(zip(odd, sent)) | dict(zip(even, kept))
    terms = scatter_chan(parts, n_chan)
    expand_part = call(
        expand_grad_kernel, [shape((n_chan, width, share), BF16)], [d_expanded, *hidden_all],
        flops=n_chan * mm, name="expand_grad",
    )
    d_two, spread = call(
        d_two_kernel, [shape((padded, width), F32), shape((n_batch, 2, width), F32)],
        [slope_two, grouped, got_one, got_two, *terms], [acc(2, width)], flops=mm, name="d_two",
    )
    totals_two = batch_sum(spread)
    d_grouped, d_one, spread = call(
        functools.partial(conv_back_kernel, side, slots),
        [shape((padded, width), F32)] * 2 + [shape((n_batch, 2, width), F32)],
        [live, d_two, grouped, got_two, totals_two, gain_two, slope_one, z, got_one, taps_back],
        [tall, acc(2, width)], flops=18 * padded * width * width, name="conv_back",
    )
    totals_one = batch_sum(spread)
    group_rows = -(-9 * group_width // 128) * 128
    group_part = call(
        functools.partial(group_grad_kernel, side, slots, group_width),
        [shape((group_rows, width), BF16)], [hid, d_grouped], [tall],
        flops=18 * padded * width * width, name="group_grad",
    )
    d_reduced = call(
        d_reduced_kernel, [shape((padded, width), BF16)],
        [live, d_one, z, got_one, totals_one, gain_one], flops=mm, name="d_reduced",
    )
    d_red_all = gather_chan(d_reduced, n_chan)
    tail = call(
        functools.partial(reduce_grad_kernel, halves),
        [shape((n_chan * share + group_rows, width), BF16)],
        [dims, d_reduced, group_part, own, beside, *far],
        flops=n_chan * mm, name="reduce_grad", smem=True,
    )
    part = call(
        features_grad_kernel, [shape((padded, share), F32)],
        [d_pre, *d_red_all[:2], *w_rows[:2]], flops=2 * mm, name="input_near",
    )
    features_grad = call(
        features_grad_kernel, [shape((rows, share), F32)],
        [part, *d_red_all[2:], *w_rows[2:]], flops=(n_chan - 2) * mm, name="input_far",
    )

    mine = reduce_batch(expand_part, n_batch, 1)
    cols = [mine[0]] + [swap(mine[k], "chan", n_chan, k) for k in others if k]
    stacked = jnp.stack(cols)
    cols = [lax.dynamic_index_in_dim(stacked, me ^ k, 0, keepdims=False) for k in others]
    expand_grad = spread_batch(jnp.concatenate(cols, axis=1), n_batch, 0).astype(F32)

    tail = spread_batch(reduce_batch(tail, n_batch, 0), n_batch, 0)
    reduce_grad = tail[: n_chan * share].astype(F32)
    group_grad = tail[n_chan * share : n_chan * share + 9 * group_width].astype(F32)

    total = lambda v: jnp.sum(v, axis=0)
    totals_one, totals_two, totals_three = map(total, (totals_one, totals_two, totals_three))
    shaped = lambda v: v.reshape(side, side, slots, share).transpose(2, 0, 1, 3)
    return (
        shaped(block_out),
        shaped(features_grad),
        reduce_grad,
        totals_one[1],
        totals_one[0],
        group_grad.reshape(3, 3, group_width, width),
        totals_two[1],
        totals_two[0],
        expand_grad,
        totals_three[1],
        totals_three[0],
    )


def gather_far(v, size):
    held = {0: v}
    bit = size // 2
    while bit > 1:
        held.update({k | bit: swap(b, "chan", size, bit) for k, b in list(held.items())})
        bit //= 2
    far = {k: b for k, b in held.items() if k}
    far.update({k | 1: swap(b, "chan", size, 1) for k, b in list(far.items())})
    return far


def solution(mesh):
    in_specs = (
        P("batch", None, None, "chan"),
        P(None, "chan"),
        P("chan"),
        P("chan"),
        P(None, None, None, "chan"),
        P("chan"),
        P("chan"),
        P("chan", None),
        P(),
        P(),
        P("batch", None, None, None),
        P("batch"),
        P("batch"),
    )
    out_specs = (
        P("batch", None, None, "chan"),
        P("batch", None, None, "chan"),
        P(None, "chan"),
        P("chan"),
        P("chan"),
        P(None, None, None, "chan"),
        P("chan"),
        P("chan"),
        P("chan", None),
        P("chan"),
        P("chan"),
    )
    n_batch, n_chan = mesh.shape["batch"], mesh.shape["chan"]

    def run(*args):
        return shards(n_batch, n_chan, *args)

    return jax.shard_map(run, mesh=mesh, in_specs=in_specs, out_specs=out_specs, check_vma=False)
```

```python
import functools

import jax
import jax.numpy as jnp
from jax import lax
from jax.experimental import pallas as pl
from jax.experimental.pallas import tpu as pltpu
from jax.sharding import PartitionSpec as P

EPSILON = 1e-05
ROOT = 0.7978845608028654
CUBE = 0.044715
F32 = jnp.float32
BF16 = jnp.bfloat16
STEP = 256
LANES = 128
LINES = 3
STEPS = 4
TN = (((0,), (0,)), ((), ()))
NT = (((1,), (1,)), ((), ()))
VM = pl.BlockSpec(memory_space=pltpu.VMEM)
SM = pl.BlockSpec(memory_space=pltpu.SMEM)


def dot(a, b):
    return jnp.dot(a, b, preferred_element_type=F32)


def dot_tn(a, b):
    return lax.dot_general(a, b, TN, preferred_element_type=F32)


def dot_nt(a, b):
    return lax.dot_general(a, b, NT, preferred_element_type=F32)


def bend(v):
    return jnp.tanh(v * (ROOT + (ROOT * CUBE) * (v * v)))


def act(v):
    half = 0.5 * v
    return half + half * bend(v)


def act_slope(v):
    t = bend(v)
    inner = v * (0.5 * ROOT + (1.5 * ROOT * CUBE) * (v * v))
    return 0.5 + 0.5 * t + inner * (1.0 - t * t)


def chunks(total, body, step=STEP):
    full = total // step

    def go(c, carry):
        body(pl.multiple_of(c * step, step), step)
        return carry

    if full:
        lax.fori_loop(0, full, go, 0)
    if total % step:
        body(full * step, total % step)


def fold(v):
    return jnp.sum(v.reshape(v.shape[0] // 8, 8, v.shape[1]), axis=0)


def widen(live, width):
    return jnp.concatenate([live] * (width // LANES), axis=1) if width > LANES else live


def norm_of(got, counts):
    s = jnp.sum(got[...], axis=0)
    share_of = 1.0 / jnp.sum(counts[...], axis=0)[2:3, 0:1]
    mu = s[0:1] * share_of
    return mu, lax.rsqrt(s[1:2] * share_of - mu * mu + EPSILON), share_of


def send_sums(out, acc):
    out[...] = jnp.broadcast_to(jnp.sum(acc[...], axis=1)[None], out.shape)


def start_sums(acc):
    @pl.when(pl.program_id(0) == 0)
    def _():
        acc[...] = jnp.zeros_like(acc)


def end_sums(out, acc):
    @pl.when(pl.program_id(0) == pl.num_programs(0) - 1)
    def _():
        send_sums(out, acc)


def near_kernel(dims, *refs):
    *feats, w, out = refs
    share = feats[0].shape[1]
    me = dims[2]
    ws = [w[pl.ds(pl.multiple_of((me ^ k) * share, share), share), :] for k in range(len(feats))]
    out[...] = sum(dot(f[...], wk) for f, wk in zip(feats, ws))


def far_kernel(dims, live, part, *refs):
    *feats, w, out, spread, acc = refs
    share = feats[0].shape[1]
    me = dims[2]
    start_sums(acc)
    z = part[...]
    for k, f in enumerate(feats, 2):
        z += dot(f[...], w[pl.ds(pl.multiple_of((me ^ k) * share, share), share), :])
    m = widen(live[...], z.shape[1])
    z = jnp.where(m > 0.0, z, 0.0)
    out[...] = z
    acc[0] += fold(z)
    acc[1] += fold(z * z)
    acc[2] += fold(m)
    end_sums(spread, acc)


def pad_edges(pad, side, line, wide, slots):
    width = pad.shape[1]
    pad[0:wide] = jnp.zeros((wide, width), F32)
    pad[(side + 1) * wide : (side + 2) * wide] = jnp.zeros((wide, width), F32)


def pad_line(pad, i, value, line, wide, slots):
    o = pl.multiple_of((i + 1) * wide, 8)
    edge = jnp.zeros((slots, pad.shape[1]), F32)
    pad[pl.ds(o, slots), :] = edge
    pad[pl.ds(o + slots, line), :] = value
    pad[pl.ds(o + slots + line, slots), :] = edge


def conv_lines(pad, first, count, taps, line, wide, slots, flip):
    total = None
    for t in range(9):
        a, b = divmod(t, 3)
        starts = [(first + i + a) * wide + b * slots for i in range(count)]
        x = jnp.concatenate([pad[o : o + line].astype(BF16) for o in starts], axis=0)
        d = dot_nt(x, taps[8 - t]) if flip else dot(x, taps[t])
        total = d if total is None else total + d
    return total


def taps_kernel(w, out):
    width, group_width = w.shape[2], w.shape[1]
    ids = [lax.broadcasted_iota(jnp.int32, (width, width), b) // group_width for b in range(2)]
    same = ids[0] == ids[1]
    for t in range(9):
        tiled = jnp.concatenate([w[t].astype(F32)] * (width // group_width), axis=0)
        out[t] = jnp.where(same, tiled, 0.0).astype(BF16)


def conv_kernel(side, slots, live, z, got, gain, shift, taps, hid, out, spread, pad, acc):
    line, wide = side * slots, (side + 2) * slots
    rows, width = z.shape
    mu, r, _ = norm_of(got, got)
    a = r * gain[...]
    b = shift[...] - mu * a
    pad_edges(pad, side, line, wide, slots)
    acc[...] = jnp.zeros_like(acc)

    def fill(i, carry):
        here = pl.ds(pl.multiple_of(i * line, 8), line)
        h = widen(live[here, :], width) * act(z[here, :] * a + b)
        h = h.astype(BF16).astype(F32)
        hid[here, :] = h
        pad_line(pad, i, h, line, wide, slots)
        return carry

    lax.fori_loop(0, side, fill, 0)

    for first in range(0, side, LINES):
        count = min(LINES, side - first)
        here = slice(first * line, (first + count) * line)
        total = conv_lines(pad, first, count, taps, line, wide, slots, False)
        out[here] = total
        m = widen(live[here], width) * total
        acc[0] += fold(m)
        acc[1] += fold(m * total)
    used = side * line
    out[used:rows] = jnp.zeros((rows - used, width), F32)
    hid[used:rows] = jnp.zeros((rows - used, width), F32)
    send_sums(spread, acc)


def hidden_kernel(live, z, counts, got, gain, shift, out):
    mu, r, _ = norm_of(got, counts)
    a = r * gain[...]
    b = shift[...] - mu * a
    m = widen(live[...], z.shape[1])
    out[...] = (m * act(z[...] * a + b)).astype(BF16)


def slope_kernel(live, z, counts, got, gain, shift, out):
    mu, r, _ = norm_of(got, counts)
    a = r * gain[...]
    b = shift[...] - mu * a
    out[...] = widen(live[...], z.shape[1]) * act_slope(z[...] * a + b)


def expand_near_kernel(*refs):
    *ins, out = refs
    k = len(ins) // 2
    out[...] = sum(dot(h[...], w[...]) for h, w in zip(ins[:k], ins[k:]))


def expand_far_kernel(live, part, *refs):
    *ins, out, spread, acc = refs
    k = len(ins) // 2
    start_sums(acc)
    e = part[...] + sum(dot(h[...], w[...]) for h, w in zip(ins[:k], ins[k:]))
    out[...] = e
    m = widen(live[...], e.shape[1]) * e
    acc[0] += fold(m)
    acc[1] += fold(m * e)
    end_sums(spread, acc)


def third_kernel(live, e, counts, got, gain, shift, feats, cot, d_pre, spread, acc):
    mu, r, _ = norm_of(got, counts)
    start_sums(acc)
    zhat = (e[...] - mu) * r
    v = zhat * gain[...] + shift[...] + feats[...].astype(F32)
    m = widen(live[...], v.shape[1])
    d = m * cot[...].astype(F32) * act_slope(v)
    d_pre[...] = d
    acc[0] += fold(d)
    acc[1] += fold(d * zhat)
    end_sums(spread, acc)


def block_kernel(live, e, counts, got, gain, shift, feats, out):
    mu, r, _ = norm_of(got, counts)
    v = (e[...] - mu) * r * gain[...] + shift[...] + feats[...].astype(F32)
    out[...] = (widen(live[...], v.shape[1]) * act(v)).astype(BF16)


def d_expanded_kernel(live, e, d_pre, counts, got, totals, gain, w, d_exp, out, sums):
    mu, r, share_of = norm_of(got, counts)
    t = jnp.sum(totals[...], axis=0)
    sums[...] = t
    t = t * share_of
    scale = r * gain[...]
    zhat = (e[...] - mu) * r
    m = widen(live[...], zhat.shape[1])
    d = (m * scale * (d_pre[...] - t[0:1] - zhat * t[1:2])).astype(BF16)
    d_exp[...] = d
    out[...] = dot_nt(d, w[...]).astype(BF16)


def back_expand_kernel(d_exp, *refs):
    k = len(refs) // 2
    for w, out in zip(refs[:k], refs[k:]):
        out[...] = dot_nt(d_exp[...], w[...]).astype(out.dtype)


def merge_kernel(d_exp, w, *refs):
    *got, out = refs
    total = dot_nt(d_exp[...], w[...]) + sum(g[...].astype(F32) for g in got)
    out[...] = total.astype(BF16)


def expand_grad_kernel(d_exp, *refs):
    *hs, out = refs
    for k, h in enumerate(hs):
        out[k] = dot_tn(h[...], d_exp[...]).astype(BF16)


def d_two_kernel(slope, z, counts, got, *refs):
    *terms, d_out, spread, acc = refs
    mu, r, _ = norm_of(got, counts)
    start_sums(acc)
    d = sum(t[...].astype(F32) for t in terms) * slope[...]
    d_out[...] = d
    acc[0] += fold(d)
    acc[1] += fold(d * ((z[...] - mu) * r))
    end_sums(spread, acc)


def conv_back_kernel(
    side, slots, live, d_two, grouped, got_two, totals, gain, slope, z, got, taps,
    d_grouped, d_one, spread, sums, pad, acc,
):
    line, wide = side * slots, (side + 2) * slots
    rows, width = z.shape
    mu_two, r_two, share_of = norm_of(got_two, got)
    mu, r, _ = norm_of(got, got)
    t = jnp.sum(totals[...], axis=0)
    sums[...] = t
    t = t * share_of
    scale = r_two * gain[...]
    pad_edges(pad, side, line, wide, slots)
    acc[...] = jnp.zeros_like(acc)

    def fill(i, carry):
        here = pl.ds(pl.multiple_of(i * line, 8), line)
        zhat = (grouped[here, :] - mu_two) * r_two
        m = widen(live[here, :], width)
        d = m * scale * (d_two[here, :] - t[0:1] - zhat * t[1:2])
        d = d.astype(BF16).astype(F32)
        d_grouped[here, :] = d
        pad_line(pad, i, d, line, wide, slots)
        return carry

    lax.fori_loop(0, side, fill, 0)

    for first in range(0, side, LINES):
        count = min(LINES, side - first)
        here = slice(first * line, (first + count) * line)
        d = conv_lines(pad, first, count, taps, line, wide, slots, True) * slope[here]
        d_one[here] = d
        acc[0] += fold(d)
        acc[1] += fold(d * ((z[here] - mu) * r))
    used = side * line
    d_one[used:rows] = jnp.zeros((rows - used, width), F32)
    d_grouped[used:rows] = jnp.zeros((rows - used, width), F32)
    send_sums(spread, acc)


def d_reduced_kernel(live, d_one, z, got, totals, gain, out, sums):
    mu, r, share_of = norm_of(got, got)
    t = jnp.sum(totals[...], axis=0)
    sums[...] = t
    t = t * share_of
    zhat = (z[...] - mu) * r
    m = widen(live[...], zhat.shape[1])
    out[...] = (m * (r * gain[...]) * (d_one[...] - t[0:1] - zhat * t[1:2])).astype(BF16)


def group_grad_kernel(side, slots, group_width, hid, d_grouped, out, pad):
    line, wide = side * slots, (side + 2) * slots
    width = hid.shape[1]
    pad_edges(pad, side, line, wide, slots)

    def fill(i, carry):
        here = pl.ds(pl.multiple_of(i * line, 8), line)
        pad_line(pad, i, hid[here, :], line, wide, slots)
        return carry

    lax.fori_loop(0, side, fill, 0)
    d = d_grouped[0 : side * line].astype(BF16)
    ids = [lax.broadcasted_iota(jnp.int32, (width, width), b) // group_width for b in range(2)]
    same = ids[0] == ids[1]
    for t in range(9):
        a, b = divmod(t, 3)
        starts = [(i + a) * wide + b * slots for i in range(side)]
        x = jnp.concatenate([pad[o : o + line].astype(BF16) for o in starts], axis=0)
        dense = jnp.where(same, dot_tn(x, d), 0.0)
        picked = jnp.sum(dense.reshape(width // group_width, group_width, width), axis=0)
        out[t * group_width : (t + 1) * group_width] = picked.astype(BF16)


def reduce_grad_kernel(dims, d_red, *refs):
    *feats, out = refs
    share = feats[0].shape[1]
    me = dims[2]
    for k, f in enumerate(feats):
        rows = pl.ds(pl.multiple_of((me ^ k) * share, share), share)
        out[rows, :] = dot_tn(f[...], d_red[0 : f.shape[0]]).astype(BF16)


def features_grad_kernel(part, *refs):
    *ins, out = refs
    k = len(ins) // 2
    out[...] = part[...] + sum(dot_nt(d[...], w[...]) for d, w in zip(ins[:k], ins[k:]))


def pick_kernel(dims, w_expand, w_reduce, gain, shift, cot, *outs):
    me = dims[2]
    n = (len(outs) - 3) // 2
    cols, rows, rest = outs[:n], outs[n : 2 * n], outs[2 * n :]
    share = rows[0].shape[0]

    @pl.when(pl.program_id(0) == 0)
    def _():
        for k in range(n):
            at = pl.ds(pl.multiple_of((me ^ k) * share, share), share)
            cols[k][...] = w_expand[:, at]
            rows[k][...] = w_reduce[at, :]
        at = pl.ds(pl.multiple_of(me * share, share), share)
        rest[0][...] = gain[:, at]
        rest[1][...] = shift[:, at]

    at = pl.ds(pl.multiple_of(me * share, share), share)
    first = pl.program_id(0) * cot.shape[0]
    row = lax.broadcasted_iota(jnp.int32, (cot.shape[0], share), 0) + first
    rest[2][...] = jnp.where(row < dims[4], cot[:, at].astype(F32), 0.0).astype(BF16)


def bit_of(v, bit):
    return lax.bitwise_and(lax.shift_right_logical(v, bit), 1)


def send_kernel(step, last, dims, *refs):
    *terms, out = refs
    total = None
    for first, term in enumerate(terms):
        rows, at = term.shape[-2], 0
        for t in range(first, step + (not last)):
            rows //= 2
            side = bit_of(dims[3], t)
            at += rows * (side if t < step else 1 - side)
        here = pl.ds(at if isinstance(at, int) else pl.multiple_of(at, 16), rows)
        v = term[:, here, :] if len(term.shape) == 3 else term[here, :]
        total = v.astype(F32) if total is None else total + v.astype(F32)
    out[...] = total.astype(BF16)


def arrange_kernel(dims, *refs):
    *cols, out = refs
    share = cols[0].shape[1]
    for k, c in enumerate(cols):
        out[:, pl.ds(pl.multiple_of((dims[2] ^ k) * share, share), share)] = c[...]


def double_kernel(bit, dims, mine, *refs):
    *other, out = refs
    n = mine.shape[0]
    upper = bit_of(dims[3], bit)
    out[pl.ds(pl.multiple_of(upper * n, 16), n), :] = mine[...].astype(out.dtype)
    at = (1 - upper) * n
    for v in other:
        out[pl.ds(pl.multiple_of(at, 16), v.shape[0]), :] = v[...].astype(out.dtype)
        at += v.shape[0]


def split_kernel(a, b, *outs):
    for k, out in enumerate(outs):
        out[...] = (a[k].astype(F32) + b[k].astype(F32)).astype(BF16)


def add_kernel(a, b, out):
    out[...] = (a[...].astype(F32) + b[...].astype(F32)).astype(out.dtype)


def input_far_kernel(part, *refs):
    *ins, out = refs
    n = len(ins) // (STEPS + 1)
    ds, ws = ins[: n * STEPS], ins[n * STEPS :]
    for step in range(STEPS):

        @pl.when(pl.program_id(0) == step)
        def _(step=step):
            got = sum(dot_nt(ds[k * STEPS + step][...], w[...]) for k, w in enumerate(ws))
            out[...] = part[...] + got


def call(kernel, outs, ins, scratch=(), flops=0, name=None, smem=False, steps=0):
    moved = sum(x.size * x.dtype.itemsize for x in ins)
    moved += sum(int(o.size) * o.dtype.itemsize for o in outs)
    block = -(-max(o.shape[0] for o in outs) // (16 * steps)) * 16 if steps else 0

    most = max(o.shape[0] for o in outs)

    def spec(x):
        if not steps:
            return VM
        if len(x.shape) == 2 and most - block < x.shape[0] <= steps * block:
            return pl.BlockSpec((block, x.shape[1]), lambda s: (s, 0))
        return pl.BlockSpec(x.shape, lambda s: (0,) * len(x.shape))

    specs = [spec(x) for x in ins]
    if smem:
        specs[0] = SM
    got = pl.pallas_call(
        kernel,
        out_shape=list(outs),
        grid=(steps,) if steps else (),
        in_specs=specs,
        out_specs=[spec(o) for o in outs],
        scratch_shapes=list(scratch),
        compiler_params=pltpu.CompilerParams(vmem_limit_bytes=32 << 20),
        cost_estimate=pl.CostEstimate(flops=flops, bytes_accessed=moved, transcendentals=0),
        name=name,
    )(*ins)
    return got[0] if len(outs) == 1 else got


def after(v, *others):
    return lax.optimization_barrier((v, *others))[0]


def swap(v, axis, size, k):
    return lax.ppermute(v, axis, [(i, i ^ k) for i in range(size)])


def batch_sum(spread):
    return lax.all_to_all(spread, "batch", 0, 0)


def pair_kernel(a, b, out):
    out[0:1] = a[...]
    out[1:2] = b[...]


def sum_kernel(*refs):
    *terms, out = refs
    out[...] = sum(t[...] for t in terms)


def batch_sum_stepwise(v, size):
    shape = jax.ShapeDtypeStruct(v.shape, v.dtype)
    got = [swap(v, "batch", size, k) for k in range(2, size, 2)]
    v = call(sum_kernel, [shape], [v, *got], name="sum")
    both = jax.ShapeDtypeStruct((2, *v.shape[1:]), v.dtype)
    return call(pair_kernel, [both], [v, swap(v, "batch", size, 1)], name="pair")


def gather_chan(v, size):
    held = {0: v}
    bit = size // 2
    while bit:
        held.update({k | bit: swap(b, "chan", size, bit) for k, b in list(held.items())})
        bit //= 2
    return [held[k] for k in range(size)]


def send_of(dims, terms, step, last=False):
    shape = list(terms[0].shape)
    shape[-2] >>= step + (not last)
    return call(
        functools.partial(send_kernel, step, last), [jax.ShapeDtypeStruct(tuple(shape), BF16)],
        [dims, *terms], name="send", smem=True,
    )


def double(dims, mine, other, bit, dtype=BF16):
    other = other if isinstance(other, list) else [other]
    shape = (2 * mine.shape[0], mine.shape[1])
    return call(
        functools.partial(double_kernel, bit), [jax.ShapeDtypeStruct(shape, dtype)],
        [dims, mine, *other], name="double", smem=True,
    )


def add(a, b, dtype=BF16):
    return call(add_kernel, [jax.ShapeDtypeStruct(a.shape, dtype)], [a, b], name="add")


def shards(n_batch, n_chan, *args):
    (features, w_reduce, gain_one, shift_one, w_group, gain_two, shift_two, w_expand,
     gain_three, shift_three, cotangent, resolution, crop_count) = args
    slots, side, _, share = features.shape
    width = w_reduce.shape[1]
    group_width = w_group.shape[2]
    rows = slots * side * side
    unit = 16 * STEPS
    padded = -(-rows // unit) * unit
    line, wide = side * slots, (side + 2) * slots
    me = lax.axis_index("chan")
    others = range(n_chan)
    shape = jax.ShapeDtypeStruct
    acc = lambda n, c: pltpu.VMEM((n, 8, c), F32)
    tall = pltpu.VMEM(((side + 2) * wide, width), F32)
    mm = 2 * padded * share * width

    feats = features.transpose(1, 2, 0, 3).reshape(rows, share)
    ends = ((0, padded - rows), (0, 0))
    first = gather_y(feats, n_chan)
    own = jnp.pad(feats, ends)
    beside = swap(own, "chan", n_chan, 1)

    dims = jnp.stack(
        [resolution[0], crop_count[0], me, lax.axis_index("batch"), jnp.int32(rows)]
    )
    row = lax.broadcasted_iota(jnp.int32, (padded, LANES), 0)
    crop, j, i = row % slots, (row // slots) % side, row // line
    live = ((crop < crop_count[0]) & (i < resolution[0]) & (j < resolution[0])).astype(F32)
    taps = call(
        taps_kernel, [shape((9, width, width), BF16)], [w_group.reshape(9, group_width, width)],
        flops=mm, name="taps",
    )
    line_of = lambda v: v.reshape(1, -1)
    gain_one, shift_one, gain_two, shift_two = map(
        line_of, (gain_one, shift_one, gain_two, shift_two)
    )

    *picked, gain_c, shift_c, cot = call(
        pick_kernel,
        [shape((width, share), BF16)] * n_chan + [shape((share, width), BF16)] * n_chan
        + [shape((1, share), F32)] * 2 + [shape((padded, share), BF16)],
        [dims, w_expand, w_reduce, line_of(gain_three), line_of(shift_three),
         cotangent.transpose(1, 2, 0, 3).reshape(rows, -1)],
        flops=mm, name="pick", smem=True, steps=STEPS,
    )

    part = call(
        near_kernel, [shape((padded, width), F32)], [dims, own, beside, w_reduce],
        flops=2 * mm, name="near", steps=STEPS, smem=True,
    )
    w_cols = [picked[0], swap(after(picked[1], part), "chan", n_chan, 1)]
    w_rows = [picked[n_chan], swap(after(picked[n_chan + 1], part), "chan", n_chan, 1)]
    ready = (part, live, cot, taps, gain_c, shift_c, w_cols[1], w_rows[1], *picked)
    first = {k: after(v, *ready) for k, v in first.items()}
    w_cols += [swap(after(picked[k], *first.values()), "chan", n_chan, k) for k in others[2:]]
    first = gather_core(first, n_chan)
    far = [first[k] for k in others[2:]]
    z, spread = call(
        far_kernel,
        [shape((padded, width), F32), shape((1, 3, width), F32)],
        [dims, live, part, *far, w_reduce], [acc(3, width)],
        flops=(n_chan - 2) * mm, name="far", steps=STEPS, smem=True,
    )
    got_one = batch_sum_stepwise(spread, n_batch)

    hid, grouped, spread = call(
        functools.partial(conv_kernel, side, slots),
        [shape((padded, width), F32)] * 2 + [shape((n_batch, 2, width), F32)],
        [live, z, got_one, gain_one, shift_one, taps], [tall, acc(2, width)],
        flops=18 * padded * width * width, name="conv",
    )
    got_two = batch_sum(after(spread, *w_cols))
    hidden_two = call(
        hidden_kernel, [shape((padded, width), BF16)],
        [live, grouped, got_one, got_two, gain_two, shift_two], flops=mm, name="hidden", steps=STEPS,
    )
    first = gather_y(hidden_two, n_chan)
    beside_two = swap(hidden_two, "chan", n_chan, 1)
    slope_two = call(
        slope_kernel, [shape((padded, width), F32)],
        [live, grouped, got_one, got_two, gain_two, shift_two], flops=mm, name="slope_two", steps=STEPS,
    )
    slope_one = call(
        slope_kernel, [shape((padded, width), F32)],
        [live, z, got_one, got_one, gain_one, shift_one], flops=mm, name="slope_one", steps=STEPS,
    )
    part = call(
        expand_near_kernel, [shape((padded, share), F32)], [hidden_two, beside_two, *w_cols[:2]],
        flops=2 * mm, name="expand_near", steps=STEPS,
    )
    first = {k: after(v, part, slope_one, slope_two, *w_cols) for k, v in first.items()}
    w_rows += [
        swap(after(picked[n_chan + k], *first.values()), "chan", n_chan, k) for k in others[2:]
    ]
    first = gather_core(first, n_chan)
    hidden_all = [hidden_two, beside_two] + [first[k] for k in others if k > 1]
    expanded, spread = call(
        expand_far_kernel, [shape((padded, share), F32), shape((n_batch, 2, share), F32)],
        [live, part, *hidden_all[2:], *w_cols[2:]], [acc(2, share)],
        flops=(n_chan - 2) * mm, name="expand_far", steps=STEPS,
    )
    got_three = batch_sum(spread)
    d_pre, spread = call(
        third_kernel, [shape((padded, share), F32), shape((n_batch, 2, share), F32)],
        [live, expanded, got_one, got_three, gain_c, shift_c, own, cot], [acc(2, share)],
        flops=4 * mm, name="third", steps=STEPS,
    )
    totals_three = batch_sum(after(spread, *w_rows))
    top = n_chan - 1
    d_expanded, sent, sums_three = call(
        d_expanded_kernel,
        [shape((padded, share), BF16), shape((padded, width), BF16), shape((2, share), F32)],
        [live, expanded, d_pre, got_one, got_three, totals_three, gain_c]
        + [w_cols[top]],
        flops=2 * mm, name="d_expanded", steps=STEPS,
    )
    early = [0, 1]
    d_zero, d_near = call(
        back_expand_kernel, [shape((padded, width), F32), shape((padded, width), BF16)],
        [after(d_expanded, sent)] + [w_cols[k] for k in early], flops=2 * mm,
        name="back_expand", steps=STEPS,
    )

    def part_sum(k, below):
        if k == top:
            return sent
        if k == 1:
            return d_near
        got, bit = [], 1
        while bit < below:
            got.append(swap(part_sum(k | bit, bit), "chan", n_chan, bit))
            bit *= 2
        if k == 0:
            return [d_zero, *got]
        return call(
            merge_kernel, [shape((padded, width), BF16)],
            [after(d_expanded, d_near), w_cols[k], *got], flops=mm, name="merge", steps=STEPS,
        )

    far_sum = part_sum(n_chan // 2, n_chan // 2)
    terms = [d_zero]
    bit = 1
    while bit < n_chan:
        mine = far_sum if bit == n_chan // 2 else part_sum(bit, bit)
        terms.append(swap(mine, "chan", n_chan, bit))
        bit *= 2
    expand_part = call(
        expand_grad_kernel, [shape((n_chan, width, share), BF16)],
        [after(d_expanded, far_sum), *hidden_all], flops=n_chan * mm, name="expand_grad",
    )
    block_out = call(
        block_kernel, [shape((rows, share), BF16)],
        [live, after(expanded, expand_part), got_one, got_three, gain_c, shift_c, own],
        flops=2 * mm, name="block", steps=STEPS,
    )
    expand_terms = [expand_part]
    bits = n_batch.bit_length() - 1
    for s in range(2):
        send = send_of(dims, expand_terms, s)
        expand_terms.append(swap(send, "batch", n_batch, 1 << s))
    for t in range(2, bits - 1):
        expand_send = send_of(dims, expand_terms, t)
        expand_terms.append(swap(expand_send, "batch", n_batch, 1 << t))
    mine = send_of(dims, expand_terms, bits - 1, True)
    expand_other = swap(mine, "batch", n_batch, 1 << (bits - 1))
    terms[0] = after(d_zero, mine, block_out)
    d_two, spread = call(
        d_two_kernel, [shape((padded, width), F32), shape((n_batch, 2, width), F32)],
        [slope_two, grouped, got_one, got_two, *terms], [acc(2, width)], flops=mm, name="d_two", steps=STEPS,
    )
    totals_two = batch_sum(spread)
    d_grouped, d_one, spread, sums_two = call(
        functools.partial(conv_back_kernel, side, slots),
        [shape((padded, width), F32)] * 2 + [shape((n_batch, 2, width), F32), shape((2, width), F32)],
        [live, d_two, grouped, got_two, totals_two, gain_two, slope_one, z, got_one, taps],
        [tall, acc(2, width)], flops=18 * padded * width * width, name="conv_back",
    )
    parts = call(
        split_kernel, [shape(mine.shape[1:], BF16)] * n_chan,
        [mine, after(expand_other, d_one)], name="split",
    )
    totals_one = batch_sum(after(spread, *parts))
    d_reduced, sums_one = call(
        d_reduced_kernel, [shape((padded, width), BF16), shape((2, width), F32)],
        [live, d_one, z, got_one, totals_one, gain_one], flops=mm, name="d_reduced", steps=STEPS,
    )
    tail = call(
        reduce_grad_kernel,
        [shape((n_chan * share, width), BF16)], [dims, d_reduced, own, beside, *far],
        flops=n_chan * mm, name="reduce_grad", smem=True,
    )
    d_beside = swap(d_reduced, "chan", n_chan, 1)
    tail_terms = [after(tail, d_beside)]
    quarter = padded // STEPS
    d_far = []

    def next_far(*ready):
        at = len(d_far) * quarter
        if d_far and len(d_far[-1]) < n_chan - 2:
            last = {k: after(v, *ready) for k, v in d_far[-1].items()}
            d_far[-1] = gather_core(last, n_chan)
        if at < padded:
            piece = after(d_reduced, *ready)[at : at + quarter]
            d_far.append(gather_y(piece, n_chan))
        return [v for d in d_far for v in d.values()]

    top = bits - 1
    for s in range(top):
        send = send_of(dims, tail_terms, s)
        got = swap(send, "batch", n_batch, 1 << s)
        if s == 0:
            cols = [parts[0]]
            cols += [swap(after(parts[k], send), "chan", n_chan, k) for k in others if k]
            group_part = call(
                functools.partial(group_grad_kernel, side, slots, group_width),
                [shape((9 * group_width, width), BF16)], [hid, after(d_grouped, *parts)],
                [tall], flops=mm, name="group_grad",
            )
            group_other = swap(group_part, "batch", n_batch, 2)
            cols[1] = after(cols[1], group_part)
            cols = call(
                arrange_kernel, [shape((mine.shape[1], n_chan * share), BF16)], [dims, *cols],
                name="arrange", smem=True,
            )
            for t in reversed(range(1, top)):
                other = swap(cols, "batch", n_batch, 1 << t)
                if t == 1:
                    group_part = add(group_part, after(group_other, cols))
                    other = after(other, group_part)
                cols = double(dims, cols, other, t)
            got = after(got, cols)
        elif s == 1:
            split = cols.shape[0] // 2
            others_cols = [swap(after(cols, send)[:split], "batch", n_batch, 1)]
            got = after(got, *others_cols, *next_far(send))
        tail_terms.append(got)
    mine = send_of(dims, tail_terms, top, True)
    other = swap(mine, "batch", n_batch, 1 << top)
    part = call(
        features_grad_kernel, [shape((padded, share), F32)],
        [d_pre, after(d_reduced, mine), d_beside, *w_rows[:2]], flops=2 * mm,
        name="input_near", steps=STEPS,
    )
    others_cols.append(swap(after(cols, part)[split:], "batch", n_batch, 1))
    moved = next_far(part)
    others_cols[0] = after(others_cols[0], part)
    expand_grad = double(dims, cols, others_cols, 0, F32)
    group_other = swap(after(group_part, part), "batch", n_batch, 1)
    group_part = add(group_part, after(group_other, expand_grad))
    moved = next_far(part)
    tail = add(mine, after(other, group_part, *moved))
    for s in reversed(range(top)):
        got = swap(tail, "batch", n_batch, 1 << s)
        before = next_far(tail)
        if s == 0:
            for t in range(2, bits):
                group_part = after(group_part, tail)
                group_other = swap(group_part, "batch", n_batch, 1 << t)
                group_part = add(group_part, group_other, BF16 if t + 1 < bits else F32)
            features_grad = call(
                input_far_kernel, [shape((rows, share), F32)],
                [after(part, tail), *[d[k] for k in others[2:] for d in d_far], *w_rows[2:]],
                flops=(n_chan - 2) * mm, name="input_far", steps=STEPS,
            )
            before = (features_grad, group_part)
        tail = double(dims, tail, after(got, *before), s, BF16 if s else F32)
    reduce_grad, group_grad = tail, group_part

    shaped = lambda v: v.reshape(side, side, slots, share).transpose(2, 0, 1, 3)
    return (
        shaped(block_out),
        shaped(features_grad),
        reduce_grad,
        sums_one[1],
        sums_one[0],
        group_grad.reshape(3, 3, group_width, width),
        sums_two[1],
        sums_two[0],
        expand_grad,
        sums_three[1],
        sums_three[0],
    )


def gather_y(v, size):
    held = {0: v}
    bit = size // 2
    while bit > 1:
        held.update({k | bit: swap(b, "chan", size, bit) for k, b in list(held.items())})
        bit //= 2
    return {k: b for k, b in held.items() if k}


def gather_core(held, size):
    return held | {k | 1: swap(b, "chan", size, 1) for k, b in held.items()}


def solution(mesh):
    in_specs = (
        P("batch", None, None, "chan"),
        P(None, "chan"),
        P("chan"),
        P("chan"),
        P(None, None, None, "chan"),
        P("chan"),
        P("chan"),
        P("chan", None),
        P(),
        P(),
        P("batch", None, None, None),
        P("batch"),
        P("batch"),
    )
    out_specs = (
        P("batch", None, None, "chan"),
        P("batch", None, None, "chan"),
        P(None, "chan"),
        P("chan"),
        P("chan"),
        P(None, None, None, "chan"),
        P("chan"),
        P("chan"),
        P("chan", None),
        P("chan"),
        P("chan"),
    )
    n_batch, n_chan = mesh.shape["batch"], mesh.shape["chan"]

    def run(*args):
        return shards(n_batch, n_chan, *args)

    return jax.shard_map(run, mesh=mesh, in_specs=in_specs, out_specs=out_specs, check_vma=False)
```

```python
import functools

import jax
import jax.numpy as jnp
from jax import lax
from jax.experimental import pallas as pl
from jax.experimental.pallas import tpu as pltpu
from jax.sharding import PartitionSpec as P

EPSILON = 1e-05
ROOT = 0.7978845608028654
CUBE = 0.044715
F32 = jnp.float32
BF16 = jnp.bfloat16
STEP = 256
LANES = 128
LINES = 3
STEPS = 4
TN = (((0,), (0,)), ((), ()))
NT = (((1,), (1,)), ((), ()))
VM = pl.BlockSpec(memory_space=pltpu.VMEM)
SM = pl.BlockSpec(memory_space=pltpu.SMEM)


def dot(a, b):
    return jnp.dot(a, b, preferred_element_type=F32)


def dot_tn(a, b):
    return lax.dot_general(a, b, TN, preferred_element_type=F32)


def dot_nt(a, b):
    return lax.dot_general(a, b, NT, preferred_element_type=F32)


def bend(v):
    return jnp.tanh(v * (ROOT + (ROOT * CUBE) * (v * v)))


def act(v):
    half = 0.5 * v
    return half + half * bend(v)


def act_slope(v):
    t = bend(v)
    inner = v * (0.5 * ROOT + (1.5 * ROOT * CUBE) * (v * v))
    return 0.5 + 0.5 * t + inner * (1.0 - t * t)


def chunks(total, body, step=STEP):
    full = total // step

    def go(c, carry):
        body(pl.multiple_of(c * step, step), step)
        return carry

    if full:
        lax.fori_loop(0, full, go, 0)
    if total % step:
        body(full * step, total % step)


def fold(v):
    return jnp.sum(v.reshape(v.shape[0] // 8, 8, v.shape[1]), axis=0)


def widen(live, width):
    return jnp.concatenate([live] * (width // LANES), axis=1) if width > LANES else live


def norm_of(got, counts):
    s = jnp.sum(got[...], axis=0)
    share_of = 1.0 / jnp.sum(counts[...], axis=0)[2:3, 0:1]
    mu = s[0:1] * share_of
    return mu, lax.rsqrt(s[1:2] * share_of - mu * mu + EPSILON), share_of


def send_sums(out, acc):
    out[...] = jnp.broadcast_to(jnp.sum(acc[...], axis=1)[None], out.shape)


def start_sums(acc):
    @pl.when(pl.program_id(0) == 0)
    def _():
        acc[...] = jnp.zeros_like(acc)


def end_sums(out, acc):
    @pl.when(pl.program_id(0) == pl.num_programs(0) - 1)
    def _():
        send_sums(out, acc)


def near_kernel(dims, *refs):
    *feats, w, out = refs
    share = feats[0].shape[1]
    me = dims[2]
    ws = [w[pl.ds(pl.multiple_of((me ^ k) * share, share), share), :] for k in range(len(feats))]
    out[...] = sum(dot(f[...], wk) for f, wk in zip(feats, ws))


def part_far_kernel(dims, own, beside, *refs):
    n = len(refs) // 4
    ws, outs, rows, passed = (refs[i * n : (i + 1) * n] for i in range(4))
    share = own.shape[1]
    core = lax.bitwise_and(dims[2], 1)
    mine = pl.ds(pl.multiple_of(core * share, share), share)
    other = pl.ds(pl.multiple_of((1 - core) * share, share), share)
    for w, out in zip(ws, outs):
        out[...] = (dot(own[...], w[mine, :]) + dot(beside[...], w[other, :])).astype(BF16)

    @pl.when(pl.program_id(0) == 0)
    def _():
        for w, row, pass_on in zip(ws, rows, passed):
            row[...] = w[mine, :]
            pass_on[...] = w[other, :]


def far_kernel(live, part, *refs):
    *got, out, spread, acc = refs
    start_sums(acc)
    z = part[...] + sum(g[...].astype(F32) for g in got)
    m = widen(live[...], z.shape[1])
    z = jnp.where(m > 0.0, z, 0.0)
    out[...] = z
    acc[0] += fold(z)
    acc[1] += fold(z * z)
    acc[2] += fold(m)
    end_sums(spread, acc)


def pad_edges(pad, side, line, wide, slots):
    width = pad.shape[1]
    pad[0:wide] = jnp.zeros((wide, width), F32)
    pad[(side + 1) * wide : (side + 2) * wide] = jnp.zeros((wide, width), F32)


def pad_line(pad, i, value, line, wide, slots):
    o = pl.multiple_of((i + 1) * wide, 8)
    edge = jnp.zeros((slots, pad.shape[1]), F32)
    pad[pl.ds(o, slots), :] = edge
    pad[pl.ds(o + slots, line), :] = value
    pad[pl.ds(o + slots + line, slots), :] = edge


def conv_lines(pad, first, count, taps, line, wide, slots, flip):
    total = None
    for t in range(9):
        a, b = divmod(t, 3)
        starts = [(first + i + a) * wide + b * slots for i in range(count)]
        x = jnp.concatenate([pad[o : o + line].astype(BF16) for o in starts], axis=0)
        d = dot_nt(x, taps[8 - t]) if flip else dot(x, taps[t])
        total = d if total is None else total + d
    return total


def taps_kernel(w, out):
    width, group_width = w.shape[2], w.shape[1]
    ids = [lax.broadcasted_iota(jnp.int32, (width, width), b) // group_width for b in range(2)]
    same = ids[0] == ids[1]
    for t in range(9):
        tiled = jnp.concatenate([w[t].astype(F32)] * (width // group_width), axis=0)
        out[t] = jnp.where(same, tiled, 0.0).astype(BF16)


def conv_kernel(side, slots, live, z, got, gain, shift, taps, hid, out, spread, pad, acc):
    line, wide = side * slots, (side + 2) * slots
    rows, width = z.shape
    mu, r, _ = norm_of(got, got)
    a = r * gain[...]
    b = shift[...] - mu * a
    pad_edges(pad, side, line, wide, slots)
    acc[...] = jnp.zeros_like(acc)

    def fill(i, carry):
        here = pl.ds(pl.multiple_of(i * line, 8), line)
        h = widen(live[here, :], width) * act(z[here, :] * a + b)
        h = h.astype(BF16).astype(F32)
        hid[here, :] = h
        pad_line(pad, i, h, line, wide, slots)
        return carry

    lax.fori_loop(0, side, fill, 0)

    for first in range(0, side, LINES):
        count = min(LINES, side - first)
        here = slice(first * line, (first + count) * line)
        total = conv_lines(pad, first, count, taps, line, wide, slots, False)
        out[here] = total
        m = widen(live[here], width) * total
        acc[0] += fold(m)
        acc[1] += fold(m * total)
    used = side * line
    out[used:rows] = jnp.zeros((rows - used, width), F32)
    hid[used:rows] = jnp.zeros((rows - used, width), F32)
    send_sums(spread, acc)


def hidden_kernel(live, z, counts, got, gain, shift, out):
    mu, r, _ = norm_of(got, counts)
    a = r * gain[...]
    b = shift[...] - mu * a
    m = widen(live[...], z.shape[1])
    out[...] = (m * act(z[...] * a + b)).astype(BF16)


def slope_kernel(live, z, counts, got, gain, shift, out):
    mu, r, _ = norm_of(got, counts)
    a = r * gain[...]
    b = shift[...] - mu * a
    out[...] = widen(live[...], z.shape[1]) * act_slope(z[...] * a + b)


def expand_near_kernel(*refs):
    *ins, out = refs
    k = len(ins) // 2
    out[...] = sum(dot(h[...], w[...]) for h, w in zip(ins[:k], ins[k:]))


def expand_far_kernel(live, part, *refs):
    *ins, out, spread, acc = refs
    k = len(ins) // 2
    start_sums(acc)
    e = part[...] + sum(dot(h[...], w[...]) for h, w in zip(ins[:k], ins[k:]))
    out[...] = e
    m = widen(live[...], e.shape[1]) * e
    acc[0] += fold(m)
    acc[1] += fold(m * e)
    end_sums(spread, acc)


def third_kernel(live, e, counts, got, gain, shift, feats, cot, d_pre, spread, acc):
    mu, r, _ = norm_of(got, counts)
    start_sums(acc)
    zhat = (e[...] - mu) * r
    v = zhat * gain[...] + shift[...] + feats[...].astype(F32)
    m = widen(live[...], v.shape[1])
    d = m * cot[...].astype(F32) * act_slope(v)
    d_pre[...] = d
    acc[0] += fold(d)
    acc[1] += fold(d * zhat)
    end_sums(spread, acc)


def block_kernel(live, e, counts, got, gain, shift, feats, out):
    mu, r, _ = norm_of(got, counts)
    v = (e[...] - mu) * r * gain[...] + shift[...] + feats[...].astype(F32)
    out[...] = (widen(live[...], v.shape[1]) * act(v)).astype(BF16)


def d_expanded_kernel(live, e, d_pre, counts, got, totals, gain, w, d_exp, out, sums):
    mu, r, share_of = norm_of(got, counts)
    t = jnp.sum(totals[...], axis=0)
    sums[...] = t
    t = t * share_of
    scale = r * gain[...]
    zhat = (e[...] - mu) * r
    m = widen(live[...], zhat.shape[1])
    d = (m * scale * (d_pre[...] - t[0:1] - zhat * t[1:2])).astype(BF16)
    d_exp[...] = d
    out[...] = dot_nt(d, w[...]).astype(BF16)


def back_expand_kernel(d_exp, *refs):
    k = len(refs) // 2
    for w, out in zip(refs[:k], refs[k:]):
        out[...] = dot_nt(d_exp[...], w[...]).astype(out.dtype)


def merge_kernel(d_exp, w, *refs):
    *got, out = refs
    total = dot_nt(d_exp[...], w[...]) + sum(g[...].astype(F32) for g in got)
    out[...] = total.astype(BF16)


def expand_grad_kernel(d_exp, *refs):
    *hs, out = refs
    for k, h in enumerate(hs):
        out[k] = dot_tn(h[...], d_exp[...]).astype(BF16)


def d_two_kernel(slope, z, counts, got, *refs):
    *terms, d_out, spread, acc = refs
    mu, r, _ = norm_of(got, counts)
    start_sums(acc)
    d = sum(t[...].astype(F32) for t in terms) * slope[...]
    d_out[...] = d
    acc[0] += fold(d)
    acc[1] += fold(d * ((z[...] - mu) * r))
    end_sums(spread, acc)


def conv_back_kernel(
    side, slots, live, d_two, grouped, got_two, totals, gain, slope, z, got, taps,
    d_grouped, d_one, spread, sums, pad, acc,
):
    line, wide = side * slots, (side + 2) * slots
    rows, width = z.shape
    mu_two, r_two, share_of = norm_of(got_two, got)
    mu, r, _ = norm_of(got, got)
    t = jnp.sum(totals[...], axis=0)
    sums[...] = t
    t = t * share_of
    scale = r_two * gain[...]
    pad_edges(pad, side, line, wide, slots)
    acc[...] = jnp.zeros_like(acc)

    def fill(i, carry):
        here = pl.ds(pl.multiple_of(i * line, 8), line)
        zhat = (grouped[here, :] - mu_two) * r_two
        m = widen(live[here, :], width)
        d = m * scale * (d_two[here, :] - t[0:1] - zhat * t[1:2])
        d = d.astype(BF16).astype(F32)
        d_grouped[here, :] = d
        pad_line(pad, i, d, line, wide, slots)
        return carry

    lax.fori_loop(0, side, fill, 0)

    for first in range(0, side, LINES):
        count = min(LINES, side - first)
        here = slice(first * line, (first + count) * line)
        d = conv_lines(pad, first, count, taps, line, wide, slots, True) * slope[here]
        d_one[here] = d
        acc[0] += fold(d)
        acc[1] += fold(d * ((z[here] - mu) * r))
    used = side * line
    d_one[used:rows] = jnp.zeros((rows - used, width), F32)
    d_grouped[used:rows] = jnp.zeros((rows - used, width), F32)
    send_sums(spread, acc)


def d_reduced_kernel(live, d_one, z, got, totals, gain, out, sums):
    mu, r, share_of = norm_of(got, got)
    t = jnp.sum(totals[...], axis=0)
    sums[...] = t
    t = t * share_of
    zhat = (z[...] - mu) * r
    m = widen(live[...], zhat.shape[1])
    out[...] = (m * (r * gain[...]) * (d_one[...] - t[0:1] - zhat * t[1:2])).astype(BF16)


def group_grad_kernel(side, slots, group_width, hid, d_grouped, out, pad):
    line, wide = side * slots, (side + 2) * slots
    width = hid.shape[1]
    pad_edges(pad, side, line, wide, slots)

    def fill(i, carry):
        here = pl.ds(pl.multiple_of(i * line, 8), line)
        pad_line(pad, i, hid[here, :], line, wide, slots)
        return carry

    lax.fori_loop(0, side, fill, 0)
    d = d_grouped[0 : side * line].astype(BF16)
    ids = [lax.broadcasted_iota(jnp.int32, (width, width), b) // group_width for b in range(2)]
    same = ids[0] == ids[1]
    for t in range(9):
        a, b = divmod(t, 3)
        starts = [(i + a) * wide + b * slots for i in range(side)]
        x = jnp.concatenate([pad[o : o + line].astype(BF16) for o in starts], axis=0)
        dense = jnp.where(same, dot_tn(x, d), 0.0)
        picked = jnp.sum(dense.reshape(width // group_width, group_width, width), axis=0)
        out[t * group_width : (t + 1) * group_width] = picked.astype(BF16)


def reduce_grad_kernel(dims, d_red, *refs):
    *feats, out, rest = refs
    share = feats[0].shape[1]
    me = dims[2]
    for k in range(2):
        rows = pl.ds(pl.multiple_of((me ^ k) * share, share), share)
        out[rows, :] = dot_tn(feats[k][...], d_red[...]).astype(BF16)
    for k, f in enumerate(feats[2:]):
        rest[k] = dot_tn(f[...], d_red[0 : f.shape[0]])


def reduce_grad_rest_kernel(dims, d_red, near, rest, *refs):
    *feats, out = refs
    share = feats[0].shape[1]
    me = dims[2]
    for k in range(2):
        rows = pl.ds(pl.multiple_of((me ^ k) * share, share), share)
        out[rows, :] = near[rows, :]
    for k, f in enumerate(feats):
        rows = pl.ds(pl.multiple_of((me ^ (k + 2)) * share, share), share)
        first = d_red.shape[0] - f.shape[0]
        out[rows, :] = (rest[k] + dot_tn(f[...], d_red[first:])).astype(BF16)


def features_grad_kernel(part, *refs):
    *ins, out = refs
    k = len(ins) // 2
    out[...] = part[...] + sum(dot_nt(d[...], w[...]) for d, w in zip(ins[:k], ins[k:]))


def pick_kernel(dims, w_expand, w_reduce, gain, shift, cot, *outs):
    me = dims[2]
    n = len(outs) - 5
    cols, rows, rest = outs[:n], outs[n : n + 2], outs[n + 2 :]
    share = rows[0].shape[0]

    @pl.when(pl.program_id(0) == 0)
    def _():
        for k in range(n):
            at = pl.ds(pl.multiple_of((me ^ k) * share, share), share)
            cols[k][...] = w_expand[:, at]
            if k < 2:
                rows[k][...] = w_reduce[at, :]
        at = pl.ds(pl.multiple_of(me * share, share), share)
        rest[0][...] = gain[:, at]
        rest[1][...] = shift[:, at]

    at = pl.ds(pl.multiple_of(me * share, share), share)
    first = pl.program_id(0) * cot.shape[0]
    row = lax.broadcasted_iota(jnp.int32, (cot.shape[0], share), 0) + first
    rest[2][...] = jnp.where(row < dims[4], cot[:, at].astype(F32), 0.0).astype(BF16)


def bit_of(v, bit):
    return lax.bitwise_and(lax.shift_right_logical(v, bit), 1)


def send_kernel(step, last, dims, *refs):
    *terms, out = refs
    total = None
    for first, term in enumerate(terms):
        rows, at = term.shape[-2], 0
        for t in range(first, step + (not last)):
            rows //= 2
            side = bit_of(dims[3], t)
            at += rows * (side if t < step else 1 - side)
        here = pl.ds(at if isinstance(at, int) else pl.multiple_of(at, 16), rows)
        v = term[:, here, :] if len(term.shape) == 3 else term[here, :]
        total = v.astype(F32) if total is None else total + v.astype(F32)
    out[...] = total.astype(BF16)


def arrange_kernel(dims, *refs):
    *cols, out = refs
    share = cols[0].shape[1]
    for k, c in enumerate(cols):
        out[:, pl.ds(pl.multiple_of((dims[2] ^ k) * share, share), share)] = c[...]


def double_kernel(bit, dims, mine, *refs):
    *other, out = refs
    n = mine.shape[0]
    upper = bit_of(dims[3], bit)
    out[pl.ds(pl.multiple_of(upper * n, 16), n), :] = mine[...].astype(out.dtype)
    at = (1 - upper) * n
    for v in other:
        out[pl.ds(pl.multiple_of(at, 16), v.shape[0]), :] = v[...].astype(out.dtype)
        at += v.shape[0]


def split_kernel(a, b, *outs):
    for k, out in enumerate(outs):
        out[...] = (a[k].astype(F32) + b[k].astype(F32)).astype(BF16)


def add_kernel(a, b, out):
    out[...] = (a[...].astype(F32) + b[...].astype(F32)).astype(out.dtype)


def input_far_kernel(part, *refs):
    *ins, out = refs
    n = len(ins) // (STEPS + 1)
    ds, ws = ins[: n * STEPS], ins[n * STEPS :]
    for step in range(STEPS):

        @pl.when(pl.program_id(0) == step)
        def _(step=step):
            got = sum(dot_nt(ds[k * STEPS + step][...], w[...]) for k, w in enumerate(ws))
            out[...] = part[...] + got


def call(kernel, outs, ins, scratch=(), flops=0, name=None, smem=False, steps=0):
    moved = sum(x.size * x.dtype.itemsize for x in ins)
    moved += sum(int(o.size) * o.dtype.itemsize for o in outs)
    block = -(-max(o.shape[0] for o in outs) // (16 * steps)) * 16 if steps else 0

    most = max(o.shape[0] for o in outs)

    def spec(x):
        if not steps:
            return VM
        if len(x.shape) == 2 and most - block < x.shape[0] <= steps * block:
            return pl.BlockSpec((block, x.shape[1]), lambda s: (s, 0))
        return pl.BlockSpec(x.shape, lambda s: (0,) * len(x.shape))

    specs = [spec(x) for x in ins]
    if smem:
        specs[0] = SM
    got = pl.pallas_call(
        kernel,
        out_shape=list(outs),
        grid=(steps,) if steps else (),
        in_specs=specs,
        out_specs=[spec(o) for o in outs],
        scratch_shapes=list(scratch),
        compiler_params=pltpu.CompilerParams(vmem_limit_bytes=32 << 20),
        cost_estimate=pl.CostEstimate(flops=flops, bytes_accessed=moved, transcendentals=0),
        name=name,
    )(*ins)
    return got[0] if len(outs) == 1 else got


def after(v, *others):
    return lax.optimization_barrier((v, *others))[0]


def swap(v, axis, size, k):
    return lax.ppermute(v, axis, [(i, i ^ k) for i in range(size)])


def batch_sum(spread):
    return lax.all_to_all(spread, "batch", 0, 0)


def pair_kernel(a, b, out):
    out[0:1] = a[...]
    out[1:2] = b[...]


def sum_kernel(*refs):
    *terms, out = refs
    out[...] = sum(t[...] for t in terms)


def batch_sum_stepwise(v, size):
    shape = jax.ShapeDtypeStruct(v.shape, v.dtype)
    got = [swap(v, "batch", size, k) for k in range(2, size, 2)]
    v = call(sum_kernel, [shape], [v, *got], name="sum")
    both = jax.ShapeDtypeStruct((2, *v.shape[1:]), v.dtype)
    return call(pair_kernel, [both], [v, swap(v, "batch", size, 1)], name="pair")


def gather_chan(v, size):
    held = {0: v}
    bit = size // 2
    while bit:
        held.update({k | bit: swap(b, "chan", size, bit) for k, b in list(held.items())})
        bit //= 2
    return [held[k] for k in range(size)]


def send_of(dims, terms, step, last=False):
    shape = list(terms[0].shape)
    shape[-2] >>= step + (not last)
    return call(
        functools.partial(send_kernel, step, last), [jax.ShapeDtypeStruct(tuple(shape), BF16)],
        [dims, *terms], name="send", smem=True,
    )


def double(dims, mine, other, bit, dtype=BF16):
    other = other if isinstance(other, list) else [other]
    shape = (2 * mine.shape[0], mine.shape[1])
    return call(
        functools.partial(double_kernel, bit), [jax.ShapeDtypeStruct(shape, dtype)],
        [dims, mine, *other], name="double", smem=True,
    )


def add(a, b, dtype=BF16):
    return call(add_kernel, [jax.ShapeDtypeStruct(a.shape, dtype)], [a, b], name="add")


def shards(n_batch, n_chan, *args):
    (features, w_reduce, gain_one, shift_one, w_group, gain_two, shift_two, w_expand,
     gain_three, shift_three, cotangent, resolution, crop_count) = args
    slots, side, _, share = features.shape
    width = w_reduce.shape[1]
    group_width = w_group.shape[2]
    rows = slots * side * side
    unit = 16 * STEPS
    padded = -(-rows // unit) * unit
    line, wide = side * slots, (side + 2) * slots
    me = lax.axis_index("chan")
    others = range(n_chan)
    shape = jax.ShapeDtypeStruct
    acc = lambda n, c: pltpu.VMEM((n, 8, c), F32)
    tall = pltpu.VMEM(((side + 2) * wide, width), F32)
    mm = 2 * padded * share * width

    feats = features.transpose(1, 2, 0, 3).reshape(rows, share)
    ends = ((0, padded - rows), (0, 0))
    even = [k for k in others[2:] if k % 2 == 0]
    at = [lax.bitwise_and(me ^ k, n_chan - 2) * share for k in even]
    w_far = [lax.dynamic_slice_in_dim(w_reduce, o, 2 * share, 0) for o in at]
    w_far = [swap(w, "chan", n_chan, k) for k, w in zip(even, w_far)]
    own = jnp.pad(feats, ends)
    beside = swap(own, "chan", n_chan, 1)

    dims = jnp.stack(
        [resolution[0], crop_count[0], me, lax.axis_index("batch"), jnp.int32(rows)]
    )
    row = lax.broadcasted_iota(jnp.int32, (padded, LANES), 0)
    crop, j, i = row % slots, (row // slots) % side, row // line
    live = ((crop < crop_count[0]) & (i < resolution[0]) & (j < resolution[0])).astype(F32)
    taps = call(
        taps_kernel, [shape((9, width, width), BF16)], [w_group.reshape(9, group_width, width)],
        flops=mm, name="taps",
    )
    line_of = lambda v: v.reshape(1, -1)
    gain_one, shift_one, gain_two, shift_two = map(
        line_of, (gain_one, shift_one, gain_two, shift_two)
    )

    got = call(
        part_far_kernel,
        [shape((padded, width), BF16)] * len(even) + [shape((share, width), BF16)] * 2 * len(even),
        [dims, own, beside, *w_far],
        flops=2 * len(even) * mm, name="part_far", steps=STEPS, smem=True,
    )
    parts, rows_far, passed = (got[i * len(even) : (i + 1) * len(even)] for i in range(3))
    got = [swap(p, "chan", n_chan, k) for k, p in zip(even, parts)]

    *picked, gain_c, shift_c, cot = call(
        pick_kernel,
        [shape((width, share), BF16)] * n_chan + [shape((share, width), BF16)] * 2
        + [shape((1, share), F32)] * 2 + [shape((padded, share), BF16)],
        [dims, after(w_expand, *parts), w_reduce, line_of(gain_three), line_of(shift_three),
         cotangent.transpose(1, 2, 0, 3).reshape(rows, -1)],
        flops=mm, name="pick", smem=True, steps=STEPS,
    )
    part = call(
        near_kernel, [shape((padded, width), F32)], [dims, after(own, *parts), beside, w_reduce],
        flops=2 * mm, name="near", steps=STEPS, smem=True,
    )
    w_cols = [picked[0], swap(after(picked[1], part), "chan", n_chan, 1)]
    w_rows = [picked[n_chan], swap(after(picked[n_chan + 1], part), "chan", n_chan, 1)]
    for row, pass_on in zip(rows_far, passed):
        w_rows += [row, swap(after(pass_on, part), "chan", n_chan, 1)]
    ready = (part, live, cot, taps, gain_c, shift_c, w_cols[1], *w_rows, *picked)
    got = [after(v, *ready) for v in got]
    w_cols += [swap(after(picked[k], *got), "chan", n_chan, k) for k in others[2:]]
    z, spread = call(
        far_kernel, [shape((padded, width), F32), shape((1, 3, width), F32)],
        [live, part, *got], [acc(3, width)], flops=mm, name="far", steps=STEPS,
    )
    got_one = batch_sum_stepwise(spread, n_batch)

    hid, grouped, spread = call(
        functools.partial(conv_kernel, side, slots),
        [shape((padded, width), F32)] * 2 + [shape((n_batch, 2, width), F32)],
        [live, z, got_one, gain_one, shift_one, taps], [tall, acc(2, width)],
        flops=18 * padded * width * width, name="conv",
    )
    got_two = batch_sum(after(spread, *w_cols))
    hidden_two = call(
        hidden_kernel, [shape((padded, width), BF16)],
        [live, grouped, got_one, got_two, gain_two, shift_two], flops=mm, name="hidden", steps=STEPS,
    )
    first = gather_y(hidden_two, n_chan)
    beside_two = swap(hidden_two, "chan", n_chan, 1)
    slope_two = call(
        slope_kernel, [shape((padded, width), F32)],
        [live, grouped, got_one, got_two, gain_two, shift_two], flops=mm, name="slope_two", steps=STEPS,
    )
    slope_one = call(
        slope_kernel, [shape((padded, width), F32)],
        [live, z, got_one, got_one, gain_one, shift_one], flops=mm, name="slope_one", steps=STEPS,
    )
    part = call(
        expand_near_kernel, [shape((padded, share), F32)], [hidden_two, beside_two, *w_cols[:2]],
        flops=2 * mm, name="expand_near", steps=STEPS,
    )
    first = {k: after(v, part, slope_one, slope_two, *w_cols) for k, v in first.items()}
    half = padded * 42 // 64 // 16 * 16
    far_halves = [gather_y(after(own, *first.values())[:half], n_chan)]
    first = gather_core(first, n_chan)
    hidden_all = [hidden_two, beside_two] + [first[k] for k in others if k > 1]
    expanded, spread = call(
        expand_far_kernel, [shape((padded, share), F32), shape((n_batch, 2, share), F32)],
        [live, part, *hidden_all[2:], *w_cols[2:]], [acc(2, share)],
        flops=(n_chan - 2) * mm, name="expand_far", steps=STEPS,
    )
    got_three = batch_sum(spread)
    d_pre, spread = call(
        third_kernel, [shape((padded, share), F32), shape((n_batch, 2, share), F32)],
        [live, expanded, got_one, got_three, gain_c, shift_c, own, cot], [acc(2, share)],
        flops=4 * mm, name="third", steps=STEPS,
    )
    totals_three = batch_sum(spread)
    top = n_chan - 1
    d_expanded, sent, sums_three = call(
        d_expanded_kernel,
        [shape((padded, share), BF16), shape((padded, width), BF16), shape((2, share), F32)],
        [live, expanded, d_pre, got_one, got_three, totals_three, gain_c]
        + [w_cols[top]],
        flops=2 * mm, name="d_expanded", steps=STEPS,
    )
    early = [0, 1]
    far_halves[0] = {k: after(v, d_expanded) for k, v in far_halves[0].items()}
    d_zero, d_near = call(
        back_expand_kernel, [shape((padded, width), F32), shape((padded, width), BF16)],
        [after(d_expanded, sent, *far_halves[0].values())] + [w_cols[k] for k in early], flops=2 * mm,
        name="back_expand", steps=STEPS,
    )

    def part_sum(k, below):
        if k == top:
            return sent
        if k == 1:
            return d_near
        got, bit = [], 1
        while bit < below:
            got.append(swap(part_sum(k | bit, bit), "chan", n_chan, bit))
            bit *= 2
        if k == 0:
            return [d_zero, *got]
        return call(
            merge_kernel, [shape((padded, width), BF16)],
            [after(d_expanded, d_near), w_cols[k], *got], flops=mm, name="merge", steps=STEPS,
        )

    far_sum = part_sum(n_chan // 2, n_chan // 2)
    terms = [d_zero]
    bit = 1
    while bit < n_chan:
        mine = far_sum if bit == n_chan // 2 else part_sum(bit, bit)
        terms.append(swap(mine, "chan", n_chan, bit))
        bit *= 2
    expand_part = call(
        expand_grad_kernel, [shape((n_chan, width, share), BF16)],
        [after(d_expanded, far_sum), *hidden_all], flops=n_chan * mm, name="expand_grad",
    )
    expand_terms = [expand_part]
    bits = n_batch.bit_length() - 1
    send = send_of(dims, expand_terms, 0)
    got = swap(send, "batch", n_batch, 1)
    block_out = call(
        block_kernel, [shape((rows, share), BF16)],
        [live, after(expanded, send), got_one, got_three, gain_c, shift_c, own],
        flops=2 * mm, name="block", steps=STEPS,
    )
    expand_terms.append(after(got, block_out))
    send = send_of(dims, expand_terms, 1)
    expand_terms.append(swap(send, "batch", n_batch, 2))
    for t in range(2, bits - 1):
        expand_send = send_of(dims, expand_terms, t)
        expand_terms.append(swap(expand_send, "batch", n_batch, 1 << t))
    mine = send_of(dims, expand_terms, bits - 1, True)
    expand_other = swap(mine, "batch", n_batch, 1 << (bits - 1))
    far_halves[0] = gather_core({k: after(v, far_sum) for k, v in far_halves[0].items()}, n_chan)
    terms[0] = after(d_zero, *far_halves[0].values())
    far_halves.append(gather_y(after(own, terms[-1], mine)[half:], n_chan))
    d_two, spread = call(
        d_two_kernel, [shape((padded, width), F32), shape((n_batch, 2, width), F32)],
        [slope_two, grouped, got_one, got_two, *terms], [acc(2, width)], flops=mm, name="d_two", steps=STEPS,
    )
    totals_two = batch_sum(spread)
    d_grouped, d_one, spread, sums_two = call(
        functools.partial(conv_back_kernel, side, slots),
        [shape((padded, width), F32)] * 2 + [shape((n_batch, 2, width), F32), shape((2, width), F32)],
        [live, d_two, grouped, got_two, totals_two, gain_two, slope_one, z, got_one, taps],
        [tall, acc(2, width)], flops=18 * padded * width * width, name="conv_back",
    )
    parts = call(
        split_kernel, [shape(mine.shape[1:], BF16)] * n_chan,
        [mine, after(expand_other, d_one)], name="split",
    )
    far_halves[1] = {k: after(v, d_one) for k, v in far_halves[1].items()}
    totals_one = batch_sum(after(spread, *parts, *far_halves[1].values()))
    d_reduced, sums_one = call(
        d_reduced_kernel, [shape((padded, width), BF16), shape((2, width), F32)],
        [live, d_one, z, got_one, totals_one, gain_one], flops=mm, name="d_reduced", steps=STEPS,
    )
    far_halves[1] = gather_core(far_halves[1], n_chan)
    firsts, lasts = ([far_halves[h][k] for k in others[2:]] for h in range(2))
    tail, rest = call(
        reduce_grad_kernel,
        [shape((n_chan * share, width), BF16), shape((n_chan - 2, share, width), F32)],
        [dims, d_reduced, own, beside, *firsts], flops=n_chan * mm, name="reduce_grad", smem=True,
    )
    tail = call(
        reduce_grad_rest_kernel, [shape((n_chan * share, width), BF16)],
        [dims, d_reduced, tail, rest, *lasts], flops=mm, name="reduce_grad_rest", smem=True,
    )
    d_beside = swap(d_reduced, "chan", n_chan, 1)
    tail_terms = [after(tail, d_beside)]
    quarter = padded // STEPS
    d_far = []

    def next_far(*ready):
        at = len(d_far) * quarter
        if d_far and len(d_far[-1]) < n_chan - 2:
            last = {k: after(v, *ready) for k, v in d_far[-1].items()}
            d_far[-1] = gather_core(last, n_chan)
        if at < padded:
            piece = after(d_reduced, *ready)[at : at + quarter]
            d_far.append(gather_y(piece, n_chan))
        return [v for d in d_far for v in d.values()]

    top = bits - 1
    for s in range(top):
        send = send_of(dims, tail_terms, s)
        got = swap(send, "batch", n_batch, 1 << s)
        if s == 0:
            cols = [parts[0]]
            cols += [swap(after(parts[k], send), "chan", n_chan, k) for k in others if k]
            group_part = call(
                functools.partial(group_grad_kernel, side, slots, group_width),
                [shape((9 * group_width, width), BF16)], [hid, after(d_grouped, *parts)],
                [tall], flops=mm, name="group_grad",
            )
            cols[1] = after(cols[1], group_part)
            cols = call(
                arrange_kernel, [shape((mine.shape[1], n_chan * share), BF16)], [dims, *cols],
                name="arrange", smem=True,
            )
            for t in reversed(range(1, top)):
                other = swap(cols, "batch", n_batch, 1 << t)
                cols = double(dims, cols, other, t)
            got = after(got, cols)
        elif s == 1:
            split = cols.shape[0] // 2
            others_cols = [swap(after(cols, send)[:split], "batch", n_batch, 1)]
            got = after(got, *others_cols, *next_far(send))
        tail_terms.append(got)
    mine = send_of(dims, tail_terms, top, True)
    other = swap(mine, "batch", n_batch, 1 << top)
    others_cols.append(swap(after(cols, mine)[split:], "batch", n_batch, 1))
    moved = next_far(mine)
    expand_grad = double(dims, cols, others_cols, 0, F32)
    group_other = swap(after(group_part, mine), "batch", n_batch, 1)
    group_part = add(group_part, after(group_other, expand_grad))
    moved = next_far(expand_grad)
    tail = add(mine, after(other, group_part, *moved))
    for s in reversed(range(top)):
        got = swap(tail, "batch", n_batch, 1 << s)
        before = next_far(tail)
        if s == top - 1:
            group_other = swap(after(group_part, tail), "batch", n_batch, 2)
            part = call(
                features_grad_kernel, [shape((padded, share), F32)],
                [d_pre, after(d_reduced, tail), d_beside, *w_rows[:2]], flops=2 * mm,
                name="input_near", steps=STEPS,
            )
            group_part = add(group_part, after(group_other, part))
            before = (group_part, *before)
        if s == 0:
            features_grad = call(
                input_far_kernel, [shape((rows, share), F32)],
                [after(part, tail), *[d[k] for k in others[2:] for d in d_far], *w_rows[2:]],
                flops=(n_chan - 2) * mm, name="input_far", steps=STEPS,
            )
            for t in range(2, bits):
                group_part = after(group_part, tail)
                group_other = swap(group_part, "batch", n_batch, 1 << t)
                group_other = after(group_other, features_grad)
                group_part = add(group_part, group_other, BF16 if t + 1 < bits else F32)
            before = (group_part,)
        tail = double(dims, tail, after(got, *before), s, BF16 if s else F32)
    reduce_grad, group_grad = tail, group_part

    shaped = lambda v: v.reshape(side, side, slots, share).transpose(2, 0, 1, 3)
    return (
        shaped(block_out),
        shaped(features_grad),
        reduce_grad,
        sums_one[1],
        sums_one[0],
        group_grad.reshape(3, 3, group_width, width),
        sums_two[1],
        sums_two[0],
        expand_grad,
        sums_three[1],
        sums_three[0],
    )


def gather_y(v, size):
    held = {0: v}
    bit = size // 2
    while bit > 1:
        held.update({k | bit: swap(b, "chan", size, bit) for k, b in list(held.items())})
        bit //= 2
    return {k: b for k, b in held.items() if k}


def gather_core(held, size):
    return held | {k | 1: swap(b, "chan", size, 1) for k, b in held.items()}


def solution(mesh):
    in_specs = (
        P("batch", None, None, "chan"),
        P(None, "chan"),
        P("chan"),
        P("chan"),
        P(None, None, None, "chan"),
        P("chan"),
        P("chan"),
        P("chan", None),
        P(),
        P(),
        P("batch", None, None, None),
        P("batch"),
        P("batch"),
    )
    out_specs = (
        P("batch", None, None, "chan"),
        P("batch", None, None, "chan"),
        P(None, "chan"),
        P("chan"),
        P("chan"),
        P(None, None, None, "chan"),
        P("chan"),
        P("chan"),
        P("chan", None),
        P("chan"),
        P("chan"),
    )
    n_batch, n_chan = mesh.shape["batch"], mesh.shape["chan"]

    def run(*args):
        return shards(n_batch, n_chan, *args)

    return jax.shard_map(run, mesh=mesh, in_specs=in_specs, out_specs=out_specs, check_vma=False)
```

```python
import functools

import jax
import jax.numpy as jnp
from jax import lax
from jax.experimental import pallas as pl
from jax.experimental.pallas import tpu as pltpu
from jax.sharding import PartitionSpec as P

EPSILON = 1e-05
ROOT = 0.7978845608028654
CUBE = 0.044715
F32 = jnp.float32
BF16 = jnp.bfloat16
STEP = 256
LANES = 128
LINES = 3
STEPS = 4
PIECES = 2
TN = (((0,), (0,)), ((), ()))
NT = (((1,), (1,)), ((), ()))
VM = pl.BlockSpec(memory_space=pltpu.VMEM)
SM = pl.BlockSpec(memory_space=pltpu.SMEM)


def dot(a, b):
    return jnp.dot(a, b, preferred_element_type=F32)


def dot_tn(a, b):
    return lax.dot_general(a, b, TN, preferred_element_type=F32)


def dot_nt(a, b):
    return lax.dot_general(a, b, NT, preferred_element_type=F32)


def bend(v):
    return jnp.tanh(v * (ROOT + (ROOT * CUBE) * (v * v)))


def act(v):
    half = 0.5 * v
    return half + half * bend(v)


def act_slope(v):
    t = bend(v)
    inner = v * (0.5 * ROOT + (1.5 * ROOT * CUBE) * (v * v))
    return 0.5 + 0.5 * t + inner * (1.0 - t * t)


def chunks(total, body, step=STEP):
    full = total // step

    def go(c, carry):
        body(pl.multiple_of(c * step, step), step)
        return carry

    if full:
        lax.fori_loop(0, full, go, 0)
    if total % step:
        body(full * step, total % step)


def fold(v):
    return jnp.sum(v.reshape(v.shape[0] // 8, 8, v.shape[1]), axis=0)


def widen(live, width):
    return jnp.concatenate([live] * (width // LANES), axis=1) if width > LANES else live


def norm_of(got, counts):
    s = jnp.sum(got[...], axis=0)
    share_of = 1.0 / jnp.sum(counts[...], axis=0)[2:3, 0:1]
    mu = s[0:1] * share_of
    return mu, lax.rsqrt(s[1:2] * share_of - mu * mu + EPSILON), share_of


def send_sums(out, acc):
    out[...] = jnp.broadcast_to(jnp.sum(acc[...], axis=1)[None], out.shape)


def start_sums(acc):
    @pl.when(pl.program_id(0) == 0)
    def _():
        acc[...] = jnp.zeros_like(acc)


def end_sums(out, acc):
    @pl.when(pl.program_id(0) == pl.num_programs(0) - 1)
    def _():
        send_sums(out, acc)


def near_kernel(dims, *refs):
    *feats, w, out = refs
    share = feats[0].shape[1]
    me = dims[2]
    ws = [w[pl.ds(pl.multiple_of((me ^ k) * share, share), share), :] for k in range(len(feats))]
    out[...] = sum(dot(f[...], wk) for f, wk in zip(feats, ws))


def part_far_kernel(dims, own, beside, *refs):
    n = len(refs) // 2
    share = own.shape[1]
    core = lax.bitwise_and(dims[2], 1)
    mine = pl.ds(pl.multiple_of(core * share, share), share)
    other = pl.ds(pl.multiple_of((1 - core) * share, share), share)
    for w, out in zip(refs[:n], refs[n:]):
        out[...] = (dot(own[...], w[mine, :]) + dot(beside[...], w[other, :])).astype(BF16)


def rows_kernel(dims, *refs):
    n = len(refs) // 3
    ws, rows, passed = (refs[i * n : (i + 1) * n] for i in range(3))
    share = rows[0].shape[0]
    core = lax.bitwise_and(dims[2], 1)
    for w, row, pass_on in zip(ws, rows, passed):
        row[...] = w[pl.ds(pl.multiple_of(core * share, share), share), :]
        pass_on[...] = w[pl.ds(pl.multiple_of((1 - core) * share, share), share), :]


def far_kernel(live, part, *refs):
    *got, out, spread, acc = refs
    start_sums(acc)
    z = part[...] + sum(g[...].astype(F32) for g in got)
    m = widen(live[...], z.shape[1])
    z = jnp.where(m > 0.0, z, 0.0)
    out[...] = z
    acc[0] += fold(z)
    acc[1] += fold(z * z)
    acc[2] += fold(m)
    end_sums(spread, acc)


def pad_edges(pad, side, line, wide, slots):
    width = pad.shape[1]
    pad[0:wide] = jnp.zeros((wide, width), F32)
    pad[(side + 1) * wide : (side + 2) * wide] = jnp.zeros((wide, width), F32)


def pad_line(pad, i, value, line, wide, slots):
    o = pl.multiple_of((i + 1) * wide, 8)
    edge = jnp.zeros((slots, pad.shape[1]), F32)
    pad[pl.ds(o, slots), :] = edge
    pad[pl.ds(o + slots, line), :] = value
    pad[pl.ds(o + slots + line, slots), :] = edge


def conv_lines(pad, first, count, taps, line, wide, slots, flip):
    total = None
    for t in range(9):
        a, b = divmod(t, 3)
        starts = [(first + i + a) * wide + b * slots for i in range(count)]
        x = jnp.concatenate([pad[o : o + line].astype(BF16) for o in starts], axis=0)
        d = dot_nt(x, taps[8 - t]) if flip else dot(x, taps[t])
        total = d if total is None else total + d
    return total


def taps_kernel(w, out):
    width, group_width = w.shape[2], w.shape[1]
    ids = [lax.broadcasted_iota(jnp.int32, (width, width), b) // group_width for b in range(2)]
    same = ids[0] == ids[1]
    for t in range(9):
        tiled = jnp.concatenate([w[t].astype(F32)] * (width // group_width), axis=0)
        out[t] = jnp.where(same, tiled, 0.0).astype(BF16)


def conv_kernel(side, slots, live, z, got, gain, shift, taps, out, spread, pad, acc):
    line, wide = side * slots, (side + 2) * slots
    rows, width = z.shape
    mu, r, _ = norm_of(got, got)
    a = r * gain[...]
    b = shift[...] - mu * a
    pad_edges(pad, side, line, wide, slots)
    acc[...] = jnp.zeros_like(acc)

    def fill(i, carry):
        here = pl.ds(pl.multiple_of(i * line, 8), line)
        h = widen(live[here, :], width) * act(z[here, :] * a + b)
        pad_line(pad, i, h.astype(BF16).astype(F32), line, wide, slots)
        return carry

    lax.fori_loop(0, side, fill, 0)

    for first in range(0, side, LINES):
        count = min(LINES, side - first)
        here = slice(first * line, (first + count) * line)
        total = conv_lines(pad, first, count, taps, line, wide, slots, False)
        out[here] = total
        m = widen(live[here], width) * total
        acc[0] += fold(m)
        acc[1] += fold(m * total)
    used = side * line
    out[used:rows] = jnp.zeros((rows - used, width), F32)
    send_sums(spread, acc)


def hidden_kernel(live, z, counts, got, gain, shift, out):
    mu, r, _ = norm_of(got, counts)
    a = r * gain[...]
    b = shift[...] - mu * a
    m = widen(live[...], z.shape[1])
    out[...] = (m * act(z[...] * a + b)).astype(BF16)


def slope_kernel(live, z, counts, got, gain, shift, out):
    mu, r, _ = norm_of(got, counts)
    a = r * gain[...]
    b = shift[...] - mu * a
    out[...] = widen(live[...], z.shape[1]) * act_slope(z[...] * a + b)


def expand_near_kernel(*refs):
    *ins, out = refs
    k = len(ins) // 2
    out[...] = sum(dot(h[...], w[...]) for h, w in zip(ins[:k], ins[k:]))


def expand_far_kernel(live, part, *refs):
    *ins, out, spread, acc = refs
    k = len(ins) // 2
    start_sums(acc)
    e = part[...] + sum(dot(h[...], w[...]) for h, w in zip(ins[:k], ins[k:]))
    out[...] = e
    m = widen(live[...], e.shape[1]) * e
    acc[0] += fold(m)
    acc[1] += fold(m * e)
    end_sums(spread, acc)


def third_kernel(live, e, counts, got, gain, shift, feats, cot, d_pre, spread, acc):
    mu, r, _ = norm_of(got, counts)
    start_sums(acc)
    zhat = (e[...] - mu) * r
    v = zhat * gain[...] + shift[...] + feats[...].astype(F32)
    m = widen(live[...], v.shape[1])
    d = m * cot[...].astype(F32) * act_slope(v)
    d_pre[...] = d
    acc[0] += fold(d)
    acc[1] += fold(d * zhat)
    end_sums(spread, acc)


def block_kernel(live, e, counts, got, gain, shift, feats, out):
    mu, r, _ = norm_of(got, counts)
    v = (e[...] - mu) * r * gain[...] + shift[...] + feats[...].astype(F32)
    out[...] = (widen(live[...], v.shape[1]) * act(v)).astype(BF16)


def d_expanded_kernel(live, e, d_pre, counts, got, totals, gain, w, d_exp, out, sums):
    mu, r, share_of = norm_of(got, counts)
    t = jnp.sum(totals[...], axis=0)
    sums[...] = t
    t = t * share_of
    scale = r * gain[...]
    zhat = (e[...] - mu) * r
    m = widen(live[...], zhat.shape[1])
    d = (m * scale * (d_pre[...] - t[0:1] - zhat * t[1:2])).astype(BF16)
    d_exp[...] = d
    out[...] = dot_nt(d, w[...]).astype(BF16)


def back_expand_kernel(d_exp, *refs):
    k = len(refs) // 2
    for w, out in zip(refs[:k], refs[k:]):
        out[...] = dot_nt(d_exp[...], w[...]).astype(out.dtype)


def merge_kernel(d_exp, w, *refs):
    *got, out = refs
    total = dot_nt(d_exp[...], w[...]) + sum(g[...].astype(F32) for g in got)
    out[...] = total.astype(BF16)


def expand_grad_kernel(d_exp, *refs):
    *hs, out = refs
    for k, h in enumerate(hs):
        out[k] = dot_tn(h[...], d_exp[...]).astype(BF16)


def d_two_kernel(slope, z, counts, got, *refs):
    *terms, d_out, spread, acc = refs
    mu, r, _ = norm_of(got, counts)
    start_sums(acc)
    d = sum(t[...].astype(F32) for t in terms) * slope[...]
    d_out[...] = d
    acc[0] += fold(d)
    acc[1] += fold(d * ((z[...] - mu) * r))
    end_sums(spread, acc)


def conv_back_kernel(
    side, slots, live, d_two, grouped, got_two, totals, gain, slope, z, got, taps,
    d_grouped, d_one, spread, sums, pad, acc,
):
    line, wide = side * slots, (side + 2) * slots
    rows, width = z.shape
    mu_two, r_two, share_of = norm_of(got_two, got)
    mu, r, _ = norm_of(got, got)
    t = jnp.sum(totals[...], axis=0)
    sums[...] = t
    t = t * share_of
    scale = r_two * gain[...]
    pad_edges(pad, side, line, wide, slots)
    acc[...] = jnp.zeros_like(acc)

    def fill(i, carry):
        here = pl.ds(pl.multiple_of(i * line, 8), line)
        zhat = (grouped[here, :] - mu_two) * r_two
        m = widen(live[here, :], width)
        d = m * scale * (d_two[here, :] - t[0:1] - zhat * t[1:2])
        d = d.astype(BF16).astype(F32)
        d_grouped[here, :] = d
        pad_line(pad, i, d, line, wide, slots)
        return carry

    lax.fori_loop(0, side, fill, 0)

    for first in range(0, side, LINES):
        count = min(LINES, side - first)
        here = slice(first * line, (first + count) * line)
        d = conv_lines(pad, first, count, taps, line, wide, slots, True) * slope[here]
        d_one[here] = d
        acc[0] += fold(d)
        acc[1] += fold(d * ((z[here] - mu) * r))
    used = side * line
    d_one[used:rows] = jnp.zeros((rows - used, width), F32)
    d_grouped[used:rows] = jnp.zeros((rows - used, width), F32)
    send_sums(spread, acc)


def d_reduced_kernel(live, d_one, z, got, totals, gain, out, sums):
    mu, r, share_of = norm_of(got, got)
    t = jnp.sum(totals[...], axis=0)
    sums[...] = t
    t = t * share_of
    zhat = (z[...] - mu) * r
    m = widen(live[...], zhat.shape[1])
    out[...] = (m * (r * gain[...]) * (d_one[...] - t[0:1] - zhat * t[1:2])).astype(BF16)


def group_grad_kernel(side, slots, group_width, live, z, got, gain, shift, d_grouped, out, pad):
    line, wide = side * slots, (side + 2) * slots
    width = z.shape[1]
    mu, r, _ = norm_of(got, got)
    scale = r * gain[...]
    offset = shift[...] - mu * scale
    pad_edges(pad, side, line, wide, slots)

    def fill(i, carry):
        here = pl.ds(pl.multiple_of(i * line, 8), line)
        h = widen(live[here, :], width) * act(z[here, :] * scale + offset)
        pad_line(pad, i, h.astype(BF16).astype(F32), line, wide, slots)
        return carry

    lax.fori_loop(0, side, fill, 0)
    d = d_grouped[0 : side * line].astype(BF16)
    ids = [lax.broadcasted_iota(jnp.int32, (width, width), b) // group_width for b in range(2)]
    same = ids[0] == ids[1]
    for t in range(9):
        a, b = divmod(t, 3)
        starts = [(i + a) * wide + b * slots for i in range(side)]
        x = jnp.concatenate([pad[o : o + line].astype(BF16) for o in starts], axis=0)
        dense = jnp.where(same, dot_tn(x, d), 0.0)
        picked = jnp.sum(dense.reshape(width // group_width, group_width, width), axis=0)
        out[t * group_width : (t + 1) * group_width] = picked.astype(BF16)


def reduce_grad_kernel(dims, d_red, *refs):
    *feats, out, rest = refs
    share = feats[0].shape[1]
    me = dims[2]
    for k in range(2):
        rows = pl.ds(pl.multiple_of((me ^ k) * share, share), share)
        out[rows, :] = dot_tn(feats[k][...], d_red[...]).astype(BF16)
    for k, f in enumerate(feats[2:]):
        rest[k] = dot_tn(f[...], d_red[0 : f.shape[0]])


def reduce_grad_rest_kernel(dims, d_red, near, rest, *refs):
    *feats, out = refs
    share = feats[0].shape[1]
    me = dims[2]
    for k in range(2):
        rows = pl.ds(pl.multiple_of((me ^ k) * share, share), share)
        out[rows, :] = near[rows, :]
    for k, f in enumerate(feats):
        rows = pl.ds(pl.multiple_of((me ^ (k + 2)) * share, share), share)
        first = d_red.shape[0] - f.shape[0]
        out[rows, :] = (rest[k] + dot_tn(f[...], d_red[first:])).astype(BF16)


def features_grad_kernel(part, *refs):
    *ins, out = refs
    k = len(ins) // 2
    out[...] = part[...] + sum(dot_nt(d[...], w[...]) for d, w in zip(ins[:k], ins[k:]))


def pick_kernel(dims, w_expand, w_reduce, gain, shift, cot, *outs):
    me = dims[2]
    n = len(outs) - 5
    cols, rows, rest = outs[:n], outs[n : n + 2], outs[n + 2 :]
    share = rows[0].shape[0]

    @pl.when(pl.program_id(0) == 0)
    def _():
        for k in range(n):
            at = pl.ds(pl.multiple_of((me ^ k) * share, share), share)
            cols[k][...] = w_expand[:, at]
            if k < 2:
                rows[k][...] = w_reduce[at, :]
        at = pl.ds(pl.multiple_of(me * share, share), share)
        rest[0][...] = gain[:, at]
        rest[1][...] = shift[:, at]

    at = pl.ds(pl.multiple_of(me * share, share), share)
    first = pl.program_id(0) * cot.shape[0]
    row = lax.broadcasted_iota(jnp.int32, (cot.shape[0], share), 0) + first
    rest[2][...] = jnp.where(row < dims[4], cot[:, at].astype(F32), 0.0).astype(BF16)


def bit_of(v, bit):
    return lax.bitwise_and(lax.shift_right_logical(v, bit), 1)


def add_terms(b, terms, order, step, last, base):
    total = None
    for first, (term, size) in enumerate(terms):
        rows, at = size, base if first == 0 else 0
        for t in range(first, step + (not last)):
            rows //= 2
            side = bit_of(b, order[t])
            at += rows * (side if t < step else 1 - side)
        here = pl.ds(at if isinstance(at, int) else pl.multiple_of(at, 16), rows)
        v = term[:, here, :] if len(term.shape) == 3 else term[here, :]
        total = v.astype(F32) if total is None else total + v.astype(F32)
    return total.astype(BF16)


def send_kernel(step, last, dims, *refs):
    *terms, out = refs
    sized = [(t, t.shape[-2]) for t in terms]
    out[...] = add_terms(dims[3], sized, range(step + 1), step, last, 0)


def send_both_kernel(step, last, orders, dims, whole, *refs):
    half = whole.shape[0] // 2
    n = step
    outs = refs[2 * n :]
    for i, order in enumerate(orders):
        terms = [(whole, half)] + [(r, r.shape[0]) for r in refs[i * n : (i + 1) * n]]
        total = add_terms(dims[3], terms, order, step, last, i * half)
        if last:
            outs[0][i * total.shape[0] : (i + 1) * total.shape[0]] = total
        else:
            outs[i][...] = total


def double_pair_kernel(bits, dims, sums, *refs):
    *ins, a, b = refs
    n = ins[0].shape[0]
    for i, (bit, out) in enumerate(zip(bits, (a, b))):
        mine = sums[i * n : (i + 1) * n] if len(ins) == 2 else (sums, ins[0])[i][...]
        other = ins[i] if len(ins) == 2 else ins[i + 1]
        upper = bit_of(dims[3], bit)
        out[pl.ds(pl.multiple_of(upper * n, 16), n), :] = mine
        out[pl.ds(pl.multiple_of((1 - upper) * n, 16), n), :] = other[...]


def finish_kernel(bits, dims, a, b, other_a, other_b, out):
    n = a.shape[0]
    for i, (bit, mine, other) in enumerate(zip(bits, (a, b), (other_a, other_b))):
        upper = bit_of(dims[3], bit)
        at = 2 * i * n
        out[pl.ds(pl.multiple_of(at + upper * n, 16), n), :] = mine[...].astype(F32)
        out[pl.ds(pl.multiple_of(at + (1 - upper) * n, 16), n), :] = other[...].astype(F32)


def arrange_kernel(dims, *refs):
    *cols, out = refs
    share = cols[0].shape[1]
    for k, c in enumerate(cols):
        out[:, pl.ds(pl.multiple_of((dims[2] ^ k) * share, share), share)] = c[...]


def double_kernel(bit, dims, mine, *refs):
    *other, out = refs
    n = mine.shape[0]
    upper = bit_of(dims[3], bit)
    out[pl.ds(pl.multiple_of(upper * n, 16), n), :] = mine[...].astype(out.dtype)
    at = (1 - upper) * n
    for v in other:
        out[pl.ds(pl.multiple_of(at, 16), v.shape[0]), :] = v[...].astype(out.dtype)
        at += v.shape[0]


def split_kernel(a, b, *outs):
    for k, out in enumerate(outs):
        out[...] = (a[k].astype(F32) + b[k].astype(F32)).astype(BF16)


def add_kernel(a, b, out):
    out[...] = (a[...].astype(F32) + b[...].astype(F32)).astype(out.dtype)


def input_far_kernel(part, *refs):
    *ins, out = refs
    n = len(ins) // (PIECES + 1)
    ds, ws = ins[: n * PIECES], ins[n * PIECES :]
    for step in range(PIECES):

        @pl.when(pl.program_id(0) == step)
        def _(step=step):
            got = sum(dot_nt(ds[k * PIECES + step][...], w[...]) for k, w in enumerate(ws))
            out[...] = part[...] + got


def call(kernel, outs, ins, scratch=(), flops=0, name=None, smem=False, steps=0, size=0):
    moved = sum(x.size * x.dtype.itemsize for x in ins)
    moved += sum(int(o.size) * o.dtype.itemsize for o in outs)
    size = size or max(o.shape[0] for o in outs)
    block = -(-size // (16 * steps)) * 16 if steps else 0

    def spec(x):
        if not steps:
            return VM
        if len(x.shape) == 2 and steps * block - 64 < x.shape[0] <= steps * block:
            return pl.BlockSpec((block, x.shape[1]), lambda s: (s, 0))
        return pl.BlockSpec(x.shape, lambda s: (0,) * len(x.shape))

    specs = [spec(x) for x in ins]
    if smem:
        specs[0] = SM
    got = pl.pallas_call(
        kernel,
        out_shape=list(outs),
        grid=(steps,) if steps else (),
        in_specs=specs,
        out_specs=[spec(o) for o in outs],
        scratch_shapes=list(scratch),
        compiler_params=pltpu.CompilerParams(vmem_limit_bytes=16 << 20),
        cost_estimate=pl.CostEstimate(flops=flops, bytes_accessed=moved, transcendentals=0),
        name=name,
    )(*ins)
    return got[0] if len(outs) == 1 else got


def after(v, *others):
    return lax.optimization_barrier((v, *others))[0]


def swap(v, axis, size, k):
    return lax.ppermute(v, axis, [(i, i ^ k) for i in range(size)])


def batch_sum(spread):
    return lax.all_to_all(spread, "batch", 0, 0)


def pair_kernel(a, b, out):
    out[0:1] = a[...]
    out[1:2] = b[...]


def sum_kernel(*refs):
    *terms, out = refs
    out[...] = sum(t[...] for t in terms)


def batch_sum_stepwise(v, size):
    shape = jax.ShapeDtypeStruct(v.shape, v.dtype)
    got = [swap(v, "batch", size, k) for k in range(2, size, 2)]
    v = call(sum_kernel, [shape], [v, *got], name="sum")
    both = jax.ShapeDtypeStruct((2, *v.shape[1:]), v.dtype)
    return call(pair_kernel, [both], [v, swap(v, "batch", size, 1)], name="pair")


def gather_chan(v, size):
    held = {0: v}
    bit = size // 2
    while bit:
        held.update({k | bit: swap(b, "chan", size, bit) for k, b in list(held.items())})
        bit //= 2
    return [held[k] for k in range(size)]


def send_of(dims, terms, step, last=False):
    shape = list(terms[0].shape)
    shape[-2] >>= step + (not last)
    return call(
        functools.partial(send_kernel, step, last), [jax.ShapeDtypeStruct(tuple(shape), BF16)],
        [dims, *terms], name="send", smem=True,
    )


def double(dims, mine, other, bit, dtype=BF16):
    other = other if isinstance(other, list) else [other]
    shape = (2 * mine.shape[0], mine.shape[1])
    return call(
        functools.partial(double_kernel, bit), [jax.ShapeDtypeStruct(shape, dtype)],
        [dims, mine, *other], name="double", smem=True,
    )


def add(a, b, dtype=BF16):
    return call(add_kernel, [jax.ShapeDtypeStruct(a.shape, dtype)], [a, b], name="add")


def shards(n_batch, n_chan, *args):
    (features, w_reduce, gain_one, shift_one, w_group, gain_two, shift_two, w_expand,
     gain_three, shift_three, cotangent, resolution, crop_count) = args
    slots, side, _, share = features.shape
    width = w_reduce.shape[1]
    group_width = w_group.shape[2]
    rows = slots * side * side
    unit = 16 * STEPS
    padded = -(-rows // unit) * unit
    line, wide = side * slots, (side + 2) * slots
    me = lax.axis_index("chan")
    others = range(n_chan)
    shape = jax.ShapeDtypeStruct
    acc = lambda n, c: pltpu.VMEM((n, 8, c), F32)
    tall = pltpu.VMEM(((side + 2) * wide, width), F32)
    mm = 2 * padded * share * width

    feats = features.transpose(1, 2, 0, 3).reshape(rows, share)
    ends = ((0, padded - rows), (0, 0))
    even = [k for k in others[2:] if k % 2 == 0]
    at = [lax.bitwise_and(me ^ k, n_chan - 2) * share for k in even]
    w_far = [lax.dynamic_slice_in_dim(w_reduce, o, 2 * share, 0) for o in at]
    own = jnp.pad(after(feats, *w_far), ends)
    w_far = [swap(w, "chan", n_chan, k) for k, w in zip(even, w_far)]
    beside = swap(own, "chan", n_chan, 1)

    dims = jnp.stack(
        [resolution[0], crop_count[0], me, lax.axis_index("batch"), jnp.int32(rows)]
    )
    row = lax.broadcasted_iota(jnp.int32, (padded, LANES), 0)
    crop, j, i = row % slots, (row // slots) % side, row // line
    live = ((crop < crop_count[0]) & (i < resolution[0]) & (j < resolution[0])).astype(F32)
    taps = call(
        taps_kernel, [shape((9, width, width), BF16)], [w_group.reshape(9, group_width, width)],
        flops=mm, name="taps",
    )
    line_of = lambda v: v.reshape(1, -1)
    gain_one, shift_one, gain_two, shift_two = map(
        line_of, (gain_one, shift_one, gain_two, shift_two)
    )

    parts = call(
        part_far_kernel, [shape((padded, width), BF16)] * len(even), [dims, own, beside, *w_far],
        flops=2 * len(even) * mm, name="part_far", steps=2, smem=True,
    )
    parts = parts if len(even) > 1 else [parts]
    got = call(
        rows_kernel, [shape((share, width), BF16)] * 2 * len(even),
        [dims, *[after(w, *parts) for w in w_far]], name="rows", smem=True,
    )
    rows_far, passed = got[: len(even)], got[len(even) :]
    got = [swap(p, "chan", n_chan, k) for k, p in zip(even, parts)]

    *picked, gain_c, shift_c, cot = call(
        pick_kernel,
        [shape((width, share), BF16)] * n_chan + [shape((share, width), BF16)] * 2
        + [shape((1, share), F32)] * 2 + [shape((padded, share), BF16)],
        [dims, after(w_expand, *parts), w_reduce, line_of(gain_three), line_of(shift_three),
         cotangent.transpose(1, 2, 0, 3).reshape(rows, -1)],
        flops=mm, name="pick", smem=True, steps=STEPS,
    )
    part = call(
        near_kernel, [shape((padded, width), F32)], [dims, after(own, *parts), beside, w_reduce],
        flops=2 * mm, name="near", steps=STEPS, smem=True,
    )
    w_cols = [picked[0], swap(after(picked[1], part), "chan", n_chan, 1)]
    w_rows = [picked[n_chan], swap(after(picked[n_chan + 1], part), "chan", n_chan, 1)]
    for row, pass_on in zip(rows_far, passed):
        w_rows += [row, swap(after(pass_on, part), "chan", n_chan, 1)]
    ready = (part, live, cot, taps, gain_c, shift_c, w_cols[1], *w_rows, *picked)
    got = [after(v, *ready) for v in got]
    w_cols += [swap(after(picked[k], *got), "chan", n_chan, k) for k in others[2:]]
    z, spread = call(
        far_kernel, [shape((padded, width), F32), shape((1, 3, width), F32)],
        [live, part, *got], [acc(3, width)], flops=mm, name="far", steps=STEPS,
    )
    got_one = batch_sum_stepwise(spread, n_batch)

    grouped, spread = call(
        functools.partial(conv_kernel, side, slots),
        [shape((padded, width), F32), shape((n_batch, 2, width), F32)],
        [live, z, got_one, gain_one, shift_one, taps], [tall, acc(2, width)],
        flops=18 * padded * width * width, name="conv",
    )
    got_two = batch_sum(after(spread, *w_cols))
    hidden_two = call(
        hidden_kernel, [shape((padded, width), BF16)],
        [live, grouped, got_one, got_two, gain_two, shift_two], flops=mm, name="hidden", steps=STEPS,
    )
    half = padded * 42 // 64 // 16 * 16
    own_first = after(own, hidden_two)[:half]
    first = gather_y(hidden_two, n_chan)
    beside_two = swap(hidden_two, "chan", n_chan, 1)
    slope_two = call(
        slope_kernel, [shape((padded, width), F32)],
        [live, grouped, got_one, got_two, gain_two, shift_two], flops=mm, name="slope_two", steps=STEPS,
    )
    slope_one = call(
        slope_kernel, [shape((padded, width), F32)],
        [live, z, got_one, got_one, gain_one, shift_one], flops=mm, name="slope_one", steps=STEPS,
    )
    part = call(
        expand_near_kernel, [shape((padded, share), F32)], [hidden_two, beside_two, *w_cols[:2]],
        flops=2 * mm, name="expand_near", steps=2,
    )
    first = {k: after(v, part, slope_one, slope_two, own_first, *w_cols) for k, v in first.items()}
    far_halves = [gather_y(after(own_first, *first.values()), n_chan)]
    first = gather_core(first, n_chan)
    hidden_all = [hidden_two, beside_two] + [first[k] for k in others if k > 1]
    expanded, spread = call(
        expand_far_kernel, [shape((padded, share), F32), shape((n_batch, 2, share), F32)],
        [live, part, *hidden_all[2:], *w_cols[2:]], [acc(2, share)],
        flops=(n_chan - 2) * mm, name="expand_far", steps=STEPS,
    )
    got_three = batch_sum(spread)
    d_pre, spread = call(
        third_kernel, [shape((padded, share), F32), shape((n_batch, 2, share), F32)],
        [live, expanded, got_one, got_three, gain_c, shift_c, own, cot], [acc(2, share)],
        flops=4 * mm, name="third", steps=STEPS,
    )
    totals_three = batch_sum(spread)
    top = n_chan - 1
    d_expanded, sent, sums_three = call(
        d_expanded_kernel,
        [shape((padded, share), BF16), shape((padded, width), BF16), shape((2, share), F32)],
        [live, expanded, d_pre, got_one, got_three, totals_three, gain_c]
        + [w_cols[top]],
        flops=2 * mm, name="d_expanded", steps=STEPS,
    )
    early = [0, 1]
    far_halves[0] = {k: after(v, d_expanded) for k, v in far_halves[0].items()}
    d_zero, d_near = call(
        back_expand_kernel, [shape((padded, width), F32), shape((padded, width), BF16)],
        [after(d_expanded, sent, *far_halves[0].values())] + [w_cols[k] for k in early], flops=2 * mm,
        name="back_expand", steps=2,
    )

    def part_sum(k, below):
        if k == top:
            return sent
        if k == 1:
            return d_near
        got, bit = [], 1
        while bit < below:
            got.append(swap(part_sum(k | bit, bit), "chan", n_chan, bit))
            bit *= 2
        if k == 0:
            return [d_zero, *got]
        return call(
            merge_kernel, [shape((padded, width), BF16)],
            [after(d_expanded, d_near), w_cols[k], *got], flops=mm, name="merge", steps=2,
        )

    far_sum = part_sum(n_chan // 2, n_chan // 2)
    terms = [d_zero]
    bit = 1
    while bit < n_chan:
        mine = far_sum if bit == n_chan // 2 else part_sum(bit, bit)
        terms.append(swap(mine, "chan", n_chan, bit))
        bit *= 2
    expand_part = call(
        expand_grad_kernel, [shape((n_chan, width, share), BF16)],
        [after(d_expanded, far_sum), *hidden_all], flops=n_chan * mm, name="expand_grad",
    )
    expand_terms = [expand_part]
    bits = n_batch.bit_length() - 1
    send = send_of(dims, expand_terms, 0)
    got = swap(send, "batch", n_batch, 1)
    block_out = call(
        block_kernel, [shape((rows, share), BF16)],
        [live, after(expanded, send), got_one, got_three, gain_c, shift_c, own],
        flops=2 * mm, name="block", steps=STEPS,
    )
    expand_terms.append(after(got, block_out))
    send = send_of(dims, expand_terms, 1)
    expand_terms.append(swap(send, "batch", n_batch, 2))
    for t in range(2, bits - 1):
        expand_send = send_of(dims, expand_terms, t)
        expand_terms.append(swap(expand_send, "batch", n_batch, 1 << t))
    mine = send_of(dims, expand_terms, bits - 1, True)
    expand_other = swap(mine, "batch", n_batch, 1 << (bits - 1))
    far_halves[0] = gather_core({k: after(v, far_sum) for k, v in far_halves[0].items()}, n_chan)
    terms[0] = after(d_zero, *far_halves[0].values())
    far_halves.append(gather_y(after(own, terms[-1], mine)[half:], n_chan))
    d_two, spread = call(
        d_two_kernel, [shape((padded, width), F32), shape((n_batch, 2, width), F32)],
        [slope_two, grouped, got_one, got_two, *terms], [acc(2, width)], flops=mm, name="d_two", steps=STEPS,
    )
    totals_two = batch_sum(spread)
    d_grouped, d_one, spread, sums_two = call(
        functools.partial(conv_back_kernel, side, slots),
        [shape((padded, width), F32)] * 2 + [shape((n_batch, 2, width), F32), shape((2, width), F32)],
        [live, d_two, grouped, got_two, totals_two, gain_two, slope_one, z, got_one, taps],
        [tall, acc(2, width)], flops=18 * padded * width * width, name="conv_back",
    )
    parts = call(
        split_kernel, [shape(mine.shape[1:], BF16)] * n_chan,
        [mine, after(expand_other, d_one)], name="split",
    )
    far_halves[1] = {k: after(v, d_one) for k, v in far_halves[1].items()}
    totals_one = batch_sum(after(spread, *parts, *far_halves[1].values()))
    d_reduced, sums_one = call(
        d_reduced_kernel, [shape((padded, width), BF16), shape((2, width), F32)],
        [live, d_one, z, got_one, totals_one, gain_one], flops=mm, name="d_reduced", steps=STEPS,
    )
    far_halves[1] = gather_core(far_halves[1], n_chan)
    firsts, lasts = ([far_halves[h][k] for k in others[2:]] for h in range(2))
    tail, rest = call(
        reduce_grad_kernel,
        [shape((n_chan * share, width), BF16), shape((n_chan - 2, share, width), F32)],
        [dims, d_reduced, own, beside, *firsts], flops=n_chan * mm, name="reduce_grad", smem=True,
    )
    tail = call(
        reduce_grad_rest_kernel, [shape((n_chan * share, width), BF16)],
        [dims, d_reduced, tail, rest, *lasts], flops=mm, name="reduce_grad_rest", smem=True,
    )
    d_beside = swap(d_reduced, "chan", n_chan, 1)
    tail = after(tail, d_beside)
    piece_rows = padded // PIECES
    d_far = []

    def far_rows(at, *ready):
        piece = after(d_reduced, *ready)[at * piece_rows : (at + 1) * piece_rows]
        d_far.append(gather_y(piece, n_chan))
        return list(d_far[at].values())

    def pass_on(at, *ready):
        d_far[at] = gather_core({k: after(v, *ready) for k, v in d_far[at].items()}, n_chan)
        return list(d_far[at].values())

    top = bits - 1
    orders = [list(range(top)), [1, 0, *range(2, top)]]
    got = [[], []]
    for s in range(top):
        rows_here = n_chan * share >> (s + 2)
        send = call(
            functools.partial(send_both_kernel, s, False, orders),
            [shape((rows_here, width), BF16)] * 2, [dims, tail, *got[0], *got[1]],
            name="send_both", smem=True,
        )
        new = [swap(send[i], "batch", n_batch, 1 << orders[i][s]) for i in range(2)]
        ties = []
        if s == 0:
            cols = [parts[0]]
            cols += [swap(after(parts[k], send[0]), "chan", n_chan, k) for k in others if k]
            cols = call(
                arrange_kernel, [shape((mine.shape[1], n_chan * share), BF16)], [dims, *cols],
                name="arrange", smem=True,
            )
            group_part = call(
                functools.partial(group_grad_kernel, side, slots, group_width),
                [shape((9 * group_width, width), BF16)],
                [live, z, got_one, gain_one, shift_one, after(d_grouped, cols)],
                [tall], flops=mm, name="group_grad",
            )
            far_rows(0, cols)
            ties = [group_part]
        elif s == 1:
            group_other = swap(after(group_part, send[0]), "batch", n_batch, 1)
            for t in reversed(range(1, top)):
                other = swap(after(cols, send[0]), "batch", n_batch, 1 << t)
                cols = double(dims, cols, other, t)
            group_part = add(group_part, after(group_other, cols))
            ties += [group_part, *d_far[0].values()]
            ties.append(cols)
        new = [after(v, *ties) for v in new]
        got = [got[i] + [new[i]] for i in range(2)]
    sums = call(
        functools.partial(send_both_kernel, top, True, orders),
        [shape((n_chan * share >> top, width), BF16)], [dims, tail, *got[0], *got[1]],
        name="send_both", smem=True,
    )
    other = swap(sums, "batch", n_batch, 1 << top)
    cols_other = swap(after(cols, sums), "batch", n_batch, 1)
    moved = [*far_rows(1, sums), *pass_on(0, sums)]
    part = call(
        features_grad_kernel, [shape((padded, share), F32)],
        [d_pre, after(d_reduced, sums), d_beside, *w_rows[:2]], flops=2 * mm,
        name="input_near", steps=STEPS,
    )
    expand_grad = double(dims, cols, after(cols_other, part), 0, F32)
    sums = add(sums, after(other, expand_grad, *moved))
    pair = [sums]
    for s in reversed(range(top)):
        n = pair[0].shape[0] // (2 if len(pair) == 1 else 1)
        cut = [sums[:n], sums[n:]] if len(pair) == 1 else pair
        new = [swap(cut[i], "batch", n_batch, 1 << orders[i][s]) for i in range(2)]
        if s == top - 1:
            group_other = swap(after(group_part, sums), "batch", n_batch, 2)
            group_part = add(group_part, group_other)
            before = (group_part, *pass_on(1, sums))
        if s == 0:
            for t in range(2, bits):
                group_part = after(group_part, cut[0])
                group_other = swap(group_part, "batch", n_batch, 1 << t)
                if t == 2:
                    features_grad = call(
                        input_far_kernel, [shape((rows, share), F32)],
                        [after(part, cut[0]), *[d[k] for k in others[2:] for d in d_far], *w_rows[2:]],
                        flops=(n_chan - 2) * mm, name="input_far", steps=PIECES, size=padded,
                    )
                    group_other = after(group_other, features_grad)
                group_part = add(group_part, group_other, BF16 if t + 1 < bits else F32)
            before = (group_part,)
        new = [after(v, *before) for v in new]
        if s:
            pair = call(
                functools.partial(double_pair_kernel, [o[s] for o in orders]),
                [shape((2 * n, width), BF16)] * 2, [dims, *pair, *new], name="double_pair",
                smem=True,
            )
    tail = call(
        functools.partial(finish_kernel, [o[0] for o in orders]),
        [shape((n_chan * share, width), F32)], [dims, *pair, *new], name="finish", smem=True,
    )
    reduce_grad, group_grad = tail, group_part

    shaped = lambda v: v.reshape(side, side, slots, share).transpose(2, 0, 1, 3)
    return (
        shaped(block_out),
        shaped(features_grad),
        reduce_grad,
        sums_one[1],
        sums_one[0],
        group_grad.reshape(3, 3, group_width, width),
        sums_two[1],
        sums_two[0],
        expand_grad,
        sums_three[1],
        sums_three[0],
    )


def gather_y(v, size):
    held = {0: v}
    bit = size // 2
    while bit > 1:
        held.update({k | bit: swap(b, "chan", size, bit) for k, b in list(held.items())})
        bit //= 2
    return {k: b for k, b in held.items() if k}


def gather_core(held, size):
    return held | {k | 1: swap(b, "chan", size, 1) for k, b in held.items()}


def solution(mesh):
    in_specs = (
        P("batch", None, None, "chan"),
        P(None, "chan"),
        P("chan"),
        P("chan"),
        P(None, None, None, "chan"),
        P("chan"),
        P("chan"),
        P("chan", None),
        P(),
        P(),
        P("batch", None, None, None),
        P("batch"),
        P("batch"),
    )
    out_specs = (
        P("batch", None, None, "chan"),
        P("batch", None, None, "chan"),
        P(None, "chan"),
        P("chan"),
        P("chan"),
        P(None, None, None, "chan"),
        P("chan"),
        P("chan"),
        P("chan", None),
        P("chan"),
        P("chan"),
    )
    n_batch, n_chan = mesh.shape["batch"], mesh.shape["chan"]

    def run(*args):
        return shards(n_batch, n_chan, *args)

    return jax.shard_map(run, mesh=mesh, in_specs=in_specs, out_specs=out_specs, check_vma=False)
```

```python
import functools

import jax
import jax.numpy as jnp
from jax import lax
from jax.experimental import pallas as pl
from jax.experimental.pallas import tpu as pltpu
from jax.sharding import PartitionSpec as P

EPSILON = 1e-05
ROOT = 0.7978845608028654
CUBE = 0.044715
F32 = jnp.float32
BF16 = jnp.bfloat16
STEP = 256
LANES = 128
LINES = 3
STEPS = 4
PIECES = 2
TN = (((0,), (0,)), ((), ()))
NT = (((1,), (1,)), ((), ()))
VM = pl.BlockSpec(memory_space=pltpu.VMEM)
SM = pl.BlockSpec(memory_space=pltpu.SMEM)


def dot(a, b):
    return jnp.dot(a, b, preferred_element_type=F32)


def dot_tn(a, b):
    return lax.dot_general(a, b, TN, preferred_element_type=F32)


def dot_nt(a, b):
    return lax.dot_general(a, b, NT, preferred_element_type=F32)


def bend(v):
    return jnp.tanh(v * (ROOT + (ROOT * CUBE) * (v * v)))


def act(v):
    half = 0.5 * v
    return half + half * bend(v)


def act_slope(v):
    t = bend(v)
    inner = v * (0.5 * ROOT + (1.5 * ROOT * CUBE) * (v * v))
    return 0.5 + 0.5 * t + inner * (1.0 - t * t)


def chunks(total, body, step=STEP):
    full = total // step

    def go(c, carry):
        body(pl.multiple_of(c * step, step), step)
        return carry

    if full:
        lax.fori_loop(0, full, go, 0)
    if total % step:
        body(full * step, total % step)


def fold(v):
    return jnp.sum(v.reshape(v.shape[0] // 8, 8, v.shape[1]), axis=0)


def widen(live, width):
    return jnp.concatenate([live] * (width // LANES), axis=1) if width > LANES else live


def norm_of(got, counts):
    s = jnp.sum(got[...], axis=0)
    share_of = 1.0 / jnp.sum(counts[...], axis=0)[2:3, 0:1]
    mu = s[0:1] * share_of
    return mu, lax.rsqrt(s[1:2] * share_of - mu * mu + EPSILON), share_of


def send_sums(out, acc):
    out[...] = jnp.broadcast_to(jnp.sum(acc[...], axis=1)[None], out.shape)


def start_sums(acc):
    @pl.when(pl.program_id(0) == 0)
    def _():
        acc[...] = jnp.zeros_like(acc)


def end_sums(out, acc):
    @pl.when(pl.program_id(0) == pl.num_programs(0) - 1)
    def _():
        send_sums(out, acc)


def near_kernel(dims, *refs):
    *feats, w, out = refs
    share = feats[0].shape[1]
    me = dims[2]
    ws = [w[pl.ds(pl.multiple_of((me ^ k) * share, share), share), :] for k in range(len(feats))]
    out[...] = sum(dot(f[...], wk) for f, wk in zip(feats, ws))


def part_far_kernel(dims, own, beside, *refs):
    n = len(refs) // 2
    share = own.shape[1]
    core = lax.bitwise_and(dims[2], 1)
    mine = pl.ds(pl.multiple_of(core * share, share), share)
    other = pl.ds(pl.multiple_of((1 - core) * share, share), share)
    for w, out in zip(refs[:n], refs[n:]):
        out[...] = (dot(own[...], w[mine, :]) + dot(beside[...], w[other, :])).astype(BF16)


def rows_kernel(dims, *refs):
    n = len(refs) // 3
    ws, rows, passed = (refs[i * n : (i + 1) * n] for i in range(3))
    share = rows[0].shape[0]
    core = lax.bitwise_and(dims[2], 1)
    for w, row, pass_on in zip(ws, rows, passed):
        row[...] = w[pl.ds(pl.multiple_of(core * share, share), share), :]
        pass_on[...] = w[pl.ds(pl.multiple_of((1 - core) * share, share), share), :]


def far_kernel(live, part, *refs):
    *got, out, spread, acc = refs
    start_sums(acc)
    z = part[...] + sum(g[...].astype(F32) for g in got)
    m = widen(live[...], z.shape[1])
    z = jnp.where(m > 0.0, z, 0.0)
    out[...] = z
    acc[0] += fold(z)
    acc[1] += fold(z * z)
    acc[2] += fold(m)
    end_sums(spread, acc)


def pad_edges(pad, side, line, wide, slots):
    width = pad.shape[1]
    pad[0:wide] = jnp.zeros((wide, width), F32)
    pad[(side + 1) * wide : (side + 2) * wide] = jnp.zeros((wide, width), F32)


def pad_line(pad, i, value, line, wide, slots):
    o = pl.multiple_of((i + 1) * wide, 8)
    edge = jnp.zeros((slots, pad.shape[1]), F32)
    pad[pl.ds(o, slots), :] = edge
    pad[pl.ds(o + slots, line), :] = value
    pad[pl.ds(o + slots + line, slots), :] = edge


def conv_lines(pad, first, count, taps, line, wide, slots, flip):
    total = None
    for t in range(9):
        a, b = divmod(t, 3)
        starts = [(first + i + a) * wide + b * slots for i in range(count)]
        x = jnp.concatenate([pad[o : o + line].astype(BF16) for o in starts], axis=0)
        d = dot_nt(x, taps[8 - t]) if flip else dot(x, taps[t])
        total = d if total is None else total + d
    return total


def taps_kernel(w, out):
    width, group_width = w.shape[2], w.shape[1]
    ids = [lax.broadcasted_iota(jnp.int32, (width, width), b) // group_width for b in range(2)]
    same = ids[0] == ids[1]
    for t in range(9):
        tiled = jnp.concatenate([w[t].astype(F32)] * (width // group_width), axis=0)
        out[t] = jnp.where(same, tiled, 0.0).astype(BF16)


def conv_kernel(side, slots, live, z, got, gain, shift, taps, out, spread, pad, acc):
    line, wide = side * slots, (side + 2) * slots
    rows, width = z.shape
    mu, r, _ = norm_of(got, got)
    a = r * gain[...]
    b = shift[...] - mu * a
    pad_edges(pad, side, line, wide, slots)
    acc[...] = jnp.zeros_like(acc)

    def fill(i, carry):
        here = pl.ds(pl.multiple_of(i * line, 8), line)
        h = widen(live[here, :], width) * act(z[here, :] * a + b)
        pad_line(pad, i, h.astype(BF16).astype(F32), line, wide, slots)
        return carry

    lax.fori_loop(0, side, fill, 0)

    for first in range(0, side, LINES):
        count = min(LINES, side - first)
        here = slice(first * line, (first + count) * line)
        total = conv_lines(pad, first, count, taps, line, wide, slots, False)
        out[here] = total
        m = widen(live[here], width) * total
        acc[0] += fold(m)
        acc[1] += fold(m * total)
    used = side * line
    out[used:rows] = jnp.zeros((rows - used, width), F32)
    send_sums(spread, acc)


def hidden_kernel(live, z, counts, got, gain, shift, out):
    mu, r, _ = norm_of(got, counts)
    a = r * gain[...]
    b = shift[...] - mu * a
    m = widen(live[...], z.shape[1])
    out[...] = (m * act(z[...] * a + b)).astype(BF16)


def slope_kernel(live, z, counts, got, gain, shift, out):
    mu, r, _ = norm_of(got, counts)
    a = r * gain[...]
    b = shift[...] - mu * a
    out[...] = widen(live[...], z.shape[1]) * act_slope(z[...] * a + b)


def expand_near_kernel(*refs):
    *ins, out = refs
    k = len(ins) // 2
    out[...] = sum(dot(h[...], w[...]) for h, w in zip(ins[:k], ins[k:]))


def expand_far_kernel(live, part, *refs):
    *ins, out, spread, acc = refs
    k = len(ins) // 2
    start_sums(acc)
    e = part[...] + sum(dot(h[...], w[...]) for h, w in zip(ins[:k], ins[k:]))
    out[...] = e
    m = widen(live[...], e.shape[1]) * e
    acc[0] += fold(m)
    acc[1] += fold(m * e)
    end_sums(spread, acc)


def third_kernel(live, e, counts, got, gain, shift, feats, cot, d_pre, spread, acc):
    mu, r, _ = norm_of(got, counts)
    start_sums(acc)
    zhat = (e[...] - mu) * r
    v = zhat * gain[...] + shift[...] + feats[...].astype(F32)
    m = widen(live[...], v.shape[1])
    d = m * cot[...].astype(F32) * act_slope(v)
    d_pre[...] = d
    acc[0] += fold(d)
    acc[1] += fold(d * zhat)
    end_sums(spread, acc)


def block_kernel(live, e, counts, got, gain, shift, feats, out):
    mu, r, _ = norm_of(got, counts)
    v = (e[...] - mu) * r * gain[...] + shift[...] + feats[...].astype(F32)
    out[...] = (widen(live[...], v.shape[1]) * act(v)).astype(BF16)


def d_expanded_kernel(live, e, d_pre, counts, got, totals, gain, w, d_exp, out, sums):
    mu, r, share_of = norm_of(got, counts)
    t = jnp.sum(totals[...], axis=0)
    sums[...] = t
    t = t * share_of
    scale = r * gain[...]
    zhat = (e[...] - mu) * r
    m = widen(live[...], zhat.shape[1])
    d = (m * scale * (d_pre[...] - t[0:1] - zhat * t[1:2])).astype(BF16)
    d_exp[...] = d
    out[...] = dot_nt(d, w[...]).astype(BF16)


def back_expand_kernel(d_exp, *refs):
    k = len(refs) // 2
    for w, out in zip(refs[:k], refs[k:]):
        out[...] = dot_nt(d_exp[...], w[...]).astype(out.dtype)


def merge_kernel(d_exp, w, *refs):
    *got, out = refs
    total = dot_nt(d_exp[...], w[...]) + sum(g[...].astype(F32) for g in got)
    out[...] = total.astype(BF16)


def expand_grad_kernel(d_exp, *refs):
    *hs, out = refs
    for k, h in enumerate(hs):
        out[k] = dot_tn(h[...], d_exp[...]).astype(BF16)


def d_two_kernel(slope, z, counts, got, *refs):
    *terms, d_out, spread, acc = refs
    mu, r, _ = norm_of(got, counts)
    start_sums(acc)
    d = sum(t[...].astype(F32) for t in terms) * slope[...]
    d_out[...] = d
    acc[0] += fold(d)
    acc[1] += fold(d * ((z[...] - mu) * r))
    end_sums(spread, acc)


def conv_back_kernel(
    side, slots, live, d_two, grouped, got_two, totals, gain, slope, z, got, taps,
    d_grouped, d_one, spread, sums, pad, acc,
):
    line, wide = side * slots, (side + 2) * slots
    rows, width = z.shape
    mu_two, r_two, share_of = norm_of(got_two, got)
    mu, r, _ = norm_of(got, got)
    t = jnp.sum(totals[...], axis=0)
    sums[...] = t
    t = t * share_of
    scale = r_two * gain[...]
    pad_edges(pad, side, line, wide, slots)
    acc[...] = jnp.zeros_like(acc)

    def fill(i, carry):
        here = pl.ds(pl.multiple_of(i * line, 8), line)
        zhat = (grouped[here, :] - mu_two) * r_two
        m = widen(live[here, :], width)
        d = m * scale * (d_two[here, :] - t[0:1] - zhat * t[1:2])
        d = d.astype(BF16).astype(F32)
        d_grouped[here, :] = d
        pad_line(pad, i, d, line, wide, slots)
        return carry

    lax.fori_loop(0, side, fill, 0)

    for first in range(0, side, LINES):
        count = min(LINES, side - first)
        here = slice(first * line, (first + count) * line)
        d = conv_lines(pad, first, count, taps, line, wide, slots, True) * slope[here]
        d_one[here] = d
        acc[0] += fold(d)
        acc[1] += fold(d * ((z[here] - mu) * r))
    used = side * line
    d_one[used:rows] = jnp.zeros((rows - used, width), F32)
    d_grouped[used:rows] = jnp.zeros((rows - used, width), F32)
    send_sums(spread, acc)


def d_reduced_kernel(live, d_one, z, got, totals, gain, out, sums):
    mu, r, share_of = norm_of(got, got)
    t = jnp.sum(totals[...], axis=0)
    sums[...] = t
    t = t * share_of
    zhat = (z[...] - mu) * r
    m = widen(live[...], zhat.shape[1])
    out[...] = (m * (r * gain[...]) * (d_one[...] - t[0:1] - zhat * t[1:2])).astype(BF16)


def group_grad_kernel(side, slots, group_width, live, z, got, gain, shift, d_grouped, out, pad):
    line, wide = side * slots, (side + 2) * slots
    width = z.shape[1]
    mu, r, _ = norm_of(got, got)
    scale = r * gain[...]
    offset = shift[...] - mu * scale
    pad_edges(pad, side, line, wide, slots)

    def fill(i, carry):
        here = pl.ds(pl.multiple_of(i * line, 8), line)
        h = widen(live[here, :], width) * act(z[here, :] * scale + offset)
        pad_line(pad, i, h.astype(BF16).astype(F32), line, wide, slots)
        return carry

    lax.fori_loop(0, side, fill, 0)
    d = d_grouped[0 : side * line].astype(BF16)
    ids = [lax.broadcasted_iota(jnp.int32, (width, width), b) // group_width for b in range(2)]
    same = ids[0] == ids[1]
    for t in range(9):
        a, b = divmod(t, 3)
        starts = [(i + a) * wide + b * slots for i in range(side)]
        x = jnp.concatenate([pad[o : o + line].astype(BF16) for o in starts], axis=0)
        dense = jnp.where(same, dot_tn(x, d), 0.0)
        picked = jnp.sum(dense.reshape(width // group_width, group_width, width), axis=0)
        out[t * group_width : (t + 1) * group_width] = picked.astype(BF16)


def reduce_grad_kernel(dims, d_red, *refs):
    *feats, out, rest = refs
    share = feats[0].shape[1]
    me = dims[2]
    for k in range(2):
        rows = pl.ds(pl.multiple_of((me ^ k) * share, share), share)
        out[rows, :] = dot_tn(feats[k][...], d_red[...]).astype(BF16)
    for k, f in enumerate(feats[2:]):
        rest[k] = dot_tn(f[...], d_red[0 : f.shape[0]])


def reduce_grad_rest_kernel(dims, d_red, near, rest, *refs):
    *feats, out = refs
    share = feats[0].shape[1]
    me = dims[2]
    for k in range(2):
        rows = pl.ds(pl.multiple_of((me ^ k) * share, share), share)
        out[rows, :] = near[rows, :]
    for k, f in enumerate(feats):
        rows = pl.ds(pl.multiple_of((me ^ (k + 2)) * share, share), share)
        first = d_red.shape[0] - f.shape[0]
        out[rows, :] = (rest[k] + dot_tn(f[...], d_red[first:])).astype(BF16)


def features_grad_kernel(part, *refs):
    *ins, out = refs
    k = len(ins) // 2
    out[...] = part[...] + sum(dot_nt(d[...], w[...]) for d, w in zip(ins[:k], ins[k:]))


def pick_kernel(dims, w_expand, w_reduce, gain, shift, cot, *outs):
    me = dims[2]
    n = len(outs) - 5
    cols, rows, rest = outs[:n], outs[n : n + 2], outs[n + 2 :]
    share = rows[0].shape[0]

    @pl.when(pl.program_id(0) == 0)
    def _():
        for k in range(n):
            at = pl.ds(pl.multiple_of((me ^ k) * share, share), share)
            cols[k][...] = w_expand[:, at]
            if k < 2:
                rows[k][...] = w_reduce[at, :]
        at = pl.ds(pl.multiple_of(me * share, share), share)
        rest[0][...] = gain[:, at]
        rest[1][...] = shift[:, at]

    at = pl.ds(pl.multiple_of(me * share, share), share)
    first = pl.program_id(0) * cot.shape[0]
    row = lax.broadcasted_iota(jnp.int32, (cot.shape[0], share), 0) + first
    rest[2][...] = jnp.where(row < dims[4], cot[:, at].astype(F32), 0.0).astype(BF16)


def bit_of(v, bit):
    return lax.bitwise_and(lax.shift_right_logical(v, bit), 1)


def add_terms(b, terms, order, step, last, base):
    total = None
    for first, (term, size) in enumerate(terms):
        rows, at = size, base if first == 0 else 0
        for t in range(first, step + (not last)):
            rows //= 2
            side = bit_of(b, order[t])
            at += rows * (side if t < step else 1 - side)
        here = pl.ds(at if isinstance(at, int) else pl.multiple_of(at, min(rows, 16)), rows)
        v = term[:, here, :] if len(term.shape) == 3 else term[here, :]
        total = v.astype(F32) if total is None else total + v.astype(F32)
    return total.astype(BF16)


def send_both_kernel(step, last, orders, dims, whole, *refs):
    half = whole.shape[-2] // 2
    n = step
    outs = refs[2 * n :]
    for i, order in enumerate(orders):
        terms = [(whole, half)] + [(r, r.shape[-2]) for r in refs[i * n : (i + 1) * n]]
        total = add_terms(dims[3], terms, order, step, last, i * half)
        rows = total.shape[-2]
        if last and len(whole.shape) == 3:
            outs[0][:, i * rows : (i + 1) * rows, :] = total
        elif last:
            outs[0][i * rows : (i + 1) * rows] = total
        else:
            outs[i][...] = total


def double_pair_kernel(bits, dims, sums, *refs):
    *ins, a, b = refs
    n = ins[0].shape[0]
    for i, (bit, out) in enumerate(zip(bits, (a, b))):
        mine = sums[i * n : (i + 1) * n] if len(ins) == 2 else (sums, ins[0])[i][...]
        other = ins[i] if len(ins) == 2 else ins[i + 1]
        upper = bit_of(dims[3], bit)
        out[pl.ds(pl.multiple_of(upper * n, min(n, 16)), n), :] = mine
        out[pl.ds(pl.multiple_of((1 - upper) * n, min(n, 16)), n), :] = other[...]


def finish_kernel(bits, dims, a, b, other_a, other_b, out):
    n = a.shape[0]
    for i, (bit, mine, other) in enumerate(zip(bits, (a, b), (other_a, other_b))):
        upper = bit_of(dims[3], bit)
        at = 2 * i * n
        out[pl.ds(pl.multiple_of(at + upper * n, min(n, 16)), n), :] = mine[...].astype(F32)
        out[pl.ds(pl.multiple_of(at + (1 - upper) * n, min(n, 16)), n), :] = other[...].astype(F32)


def arrange_kernel(dims, *refs):
    *cols, a, b = refs
    n, share = a.shape[0], cols[0].shape[1]
    for k, c in enumerate(cols):
        at = pl.ds(pl.multiple_of((dims[2] ^ k) * share, share), share)
        a[:, at] = c[0:n]
        b[:, at] = c[n:]


def split_kernel(a, b, *outs):
    for k, out in enumerate(outs):
        out[...] = (a[k].astype(F32) + b[k].astype(F32)).astype(BF16)


def add_kernel(a, b, out):
    out[...] = (a[...].astype(F32) + b[...].astype(F32)).astype(out.dtype)


def input_far_kernel(part, *refs):
    *ins, out = refs
    n = len(ins) // (PIECES + 1)
    ds, ws = ins[: n * PIECES], ins[n * PIECES :]
    for step in range(PIECES):

        @pl.when(pl.program_id(0) == step)
        def _(step=step):
            got = sum(dot_nt(ds[k * PIECES + step][...], w[...]) for k, w in enumerate(ws))
            out[...] = part[...] + got


def call(kernel, outs, ins, scratch=(), flops=0, name=None, smem=False, steps=0, size=0):
    moved = sum(x.size * x.dtype.itemsize for x in ins)
    moved += sum(int(o.size) * o.dtype.itemsize for o in outs)
    size = size or max(o.shape[0] for o in outs)
    block = -(-size // (16 * steps)) * 16 if steps else 0

    def spec(x):
        if not steps:
            return VM
        if len(x.shape) == 2 and steps * block - 64 < x.shape[0] <= steps * block:
            return pl.BlockSpec((block, x.shape[1]), lambda s: (s, 0))
        return pl.BlockSpec(x.shape, lambda s: (0,) * len(x.shape))

    specs = [spec(x) for x in ins]
    if smem:
        specs[0] = SM
    got = pl.pallas_call(
        kernel,
        out_shape=list(outs),
        grid=(steps,) if steps else (),
        in_specs=specs,
        out_specs=[spec(o) for o in outs],
        scratch_shapes=list(scratch),
        compiler_params=pltpu.CompilerParams(vmem_limit_bytes=16 << 20),
        cost_estimate=pl.CostEstimate(flops=flops, bytes_accessed=moved, transcendentals=0),
        name=name,
    )(*ins)
    return got[0] if len(outs) == 1 else got


def after(v, *others):
    return lax.optimization_barrier((v, *others))[0]


def swap(v, axis, size, k):
    return lax.ppermute(v, axis, [(i, i ^ k) for i in range(size)])


def batch_sum(spread):
    return lax.all_to_all(spread, "batch", 0, 0)


def pair_kernel(a, b, out):
    out[0:1] = a[...]
    out[1:2] = b[...]


def sum_kernel(*refs):
    *terms, out = refs
    out[...] = sum(t[...] for t in terms)


def batch_sum_stepwise(v, size):
    shape = jax.ShapeDtypeStruct(v.shape, v.dtype)
    got = [swap(v, "batch", size, k) for k in range(2, size, 2)]
    v = call(sum_kernel, [shape], [v, *got], name="sum")
    both = jax.ShapeDtypeStruct((2, *v.shape[1:]), v.dtype)
    return call(pair_kernel, [both], [v, swap(v, "batch", size, 1)], name="pair")


def gather_chan(v, size):
    held = {0: v}
    bit = size // 2
    while bit:
        held.update({k | bit: swap(b, "chan", size, bit) for k, b in list(held.items())})
        bit //= 2
    return [held[k] for k in range(size)]


def send_both(dims, whole, got, orders, step, last=False):
    shape = list(whole.shape)
    shape[-2] >>= step if last else step + 2
    return call(
        functools.partial(send_both_kernel, step, last, orders),
        [jax.ShapeDtypeStruct(tuple(shape), BF16)] * (1 if last else 2),
        [dims, whole, *got[0], *got[1]], name="send_both", smem=True,
    )


def double_pair(dims, pair, new, bits):
    n, columns = new[0].shape
    return call(
        functools.partial(double_pair_kernel, bits),
        [jax.ShapeDtypeStruct((2 * n, columns), BF16)] * 2, [dims, *pair, *new],
        name="double_pair", smem=True,
    )


def finish(dims, pair, new, bits):
    n, columns = new[0].shape
    return call(
        functools.partial(finish_kernel, bits), [jax.ShapeDtypeStruct((4 * n, columns), F32)],
        [dims, *pair, *new], name="finish", smem=True,
    )


def add(a, b, dtype=BF16):
    return call(add_kernel, [jax.ShapeDtypeStruct(a.shape, dtype)], [a, b], name="add")


def shards(n_batch, n_chan, *args):
    (features, w_reduce, gain_one, shift_one, w_group, gain_two, shift_two, w_expand,
     gain_three, shift_three, cotangent, resolution, crop_count) = args
    slots, side, _, share = features.shape
    width = w_reduce.shape[1]
    group_width = w_group.shape[2]
    rows = slots * side * side
    unit = 16 * STEPS
    padded = -(-rows // unit) * unit
    line, wide = side * slots, (side + 2) * slots
    me = lax.axis_index("chan")
    others = range(n_chan)
    shape = jax.ShapeDtypeStruct
    acc = lambda n, c: pltpu.VMEM((n, 8, c), F32)
    tall = pltpu.VMEM(((side + 2) * wide, width), F32)
    mm = 2 * padded * share * width

    feats = features.transpose(1, 2, 0, 3).reshape(rows, share)
    ends = ((0, padded - rows), (0, 0))
    even = [k for k in others[2:] if k % 2 == 0]
    at = [lax.bitwise_and(me ^ k, n_chan - 2) * share for k in even]
    w_far = [lax.dynamic_slice_in_dim(w_reduce, o, 2 * share, 0) for o in at]
    own = jnp.pad(after(feats, *w_far), ends)
    w_far = [swap(w, "chan", n_chan, k) for k, w in zip(even, w_far)]
    beside = swap(own, "chan", n_chan, 1)

    dims = jnp.stack(
        [resolution[0], crop_count[0], me, lax.axis_index("batch"), jnp.int32(rows)]
    )
    row = lax.broadcasted_iota(jnp.int32, (padded, LANES), 0)
    crop, j, i = row % slots, (row // slots) % side, row // line
    live = ((crop < crop_count[0]) & (i < resolution[0]) & (j < resolution[0])).astype(F32)
    taps = call(
        taps_kernel, [shape((9, width, width), BF16)], [w_group.reshape(9, group_width, width)],
        flops=mm, name="taps",
    )
    line_of = lambda v: v.reshape(1, -1)
    gain_one, shift_one, gain_two, shift_two = map(
        line_of, (gain_one, shift_one, gain_two, shift_two)
    )

    parts = call(
        part_far_kernel, [shape((padded, width), BF16)] * len(even), [dims, own, beside, *w_far],
        flops=2 * len(even) * mm, name="part_far", steps=2, smem=True,
    )
    parts = parts if len(even) > 1 else [parts]
    got = call(
        rows_kernel, [shape((share, width), BF16)] * 2 * len(even),
        [dims, *[after(w, *parts) for w in w_far]], name="rows", smem=True,
    )
    rows_far, passed = got[: len(even)], got[len(even) :]
    got = [swap(p, "chan", n_chan, k) for k, p in zip(even, parts)]

    *picked, gain_c, shift_c, cot = call(
        pick_kernel,
        [shape((width, share), BF16)] * n_chan + [shape((share, width), BF16)] * 2
        + [shape((1, share), F32)] * 2 + [shape((padded, share), BF16)],
        [dims, after(w_expand, *parts), w_reduce, line_of(gain_three), line_of(shift_three),
         cotangent.transpose(1, 2, 0, 3).reshape(rows, -1)],
        flops=mm, name="pick", smem=True, steps=STEPS,
    )
    part = call(
        near_kernel, [shape((padded, width), F32)], [dims, after(own, *parts), beside, w_reduce],
        flops=2 * mm, name="near", steps=STEPS, smem=True,
    )
    w_cols = [picked[0], swap(after(picked[1], part), "chan", n_chan, 1)]
    w_rows = [picked[n_chan], swap(after(picked[n_chan + 1], part), "chan", n_chan, 1)]
    for row, pass_on in zip(rows_far, passed):
        w_rows += [row, swap(after(pass_on, part), "chan", n_chan, 1)]
    ready = (part, live, cot, taps, gain_c, shift_c, w_cols[1], *w_rows, *picked)
    got = [after(v, *ready) for v in got]
    w_cols += [swap(after(picked[k], *got), "chan", n_chan, k) for k in others[2:]]
    z, spread = call(
        far_kernel, [shape((padded, width), F32), shape((1, 3, width), F32)],
        [live, part, *got], [acc(3, width)], flops=mm, name="far", steps=STEPS,
    )
    got_one = batch_sum_stepwise(spread, n_batch)

    grouped, spread = call(
        functools.partial(conv_kernel, side, slots),
        [shape((padded, width), F32), shape((n_batch, 2, width), F32)],
        [live, z, got_one, gain_one, shift_one, taps], [tall, acc(2, width)],
        flops=18 * padded * width * width, name="conv",
    )
    got_two = batch_sum(after(spread, *w_cols))
    hidden_two = call(
        hidden_kernel, [shape((padded, width), BF16)],
        [live, grouped, got_one, got_two, gain_two, shift_two], flops=mm, name="hidden", steps=STEPS,
    )
    half = padded * 42 // 64 // 16 * 16
    own_first = after(own, hidden_two)[:half]
    first = gather_y(hidden_two, n_chan)
    beside_two = swap(hidden_two, "chan", n_chan, 1)
    slope_two = call(
        slope_kernel, [shape((padded, width), F32)],
        [live, grouped, got_one, got_two, gain_two, shift_two], flops=mm, name="slope_two", steps=STEPS,
    )
    slope_one = call(
        slope_kernel, [shape((padded, width), F32)],
        [live, z, got_one, got_one, gain_one, shift_one], flops=mm, name="slope_one", steps=STEPS,
    )
    part = call(
        expand_near_kernel, [shape((padded, share), F32)], [hidden_two, beside_two, *w_cols[:2]],
        flops=2 * mm, name="expand_near", steps=2,
    )
    first = {k: after(v, part, slope_one, slope_two, own_first, *w_cols) for k, v in first.items()}
    far_halves = [gather_y(after(own_first, *first.values()), n_chan)]
    first = gather_core(first, n_chan)
    hidden_all = [hidden_two, beside_two] + [first[k] for k in others if k > 1]
    expanded, spread = call(
        expand_far_kernel, [shape((padded, share), F32), shape((n_batch, 2, share), F32)],
        [live, part, *hidden_all[2:], *w_cols[2:]], [acc(2, share)],
        flops=(n_chan - 2) * mm, name="expand_far", steps=STEPS,
    )
    got_three = batch_sum(spread)
    d_pre, spread = call(
        third_kernel, [shape((padded, share), F32), shape((n_batch, 2, share), F32)],
        [live, expanded, got_one, got_three, gain_c, shift_c, own, cot], [acc(2, share)],
        flops=4 * mm, name="third", steps=STEPS,
    )
    totals_three = batch_sum(spread)
    top = n_chan - 1
    d_expanded, sent, sums_three = call(
        d_expanded_kernel,
        [shape((padded, share), BF16), shape((padded, width), BF16), shape((2, share), F32)],
        [live, expanded, d_pre, got_one, got_three, totals_three, gain_c]
        + [w_cols[top]],
        flops=2 * mm, name="d_expanded", steps=STEPS,
    )
    early = [0, 1]
    far_halves[0] = {k: after(v, d_expanded) for k, v in far_halves[0].items()}
    d_zero, d_near = call(
        back_expand_kernel, [shape((padded, width), F32), shape((padded, width), BF16)],
        [after(d_expanded, sent, *far_halves[0].values())] + [w_cols[k] for k in early], flops=2 * mm,
        name="back_expand", steps=2,
    )

    def part_sum(k, below):
        if k == top:
            return sent
        if k == 1:
            return d_near
        got, bit = [], 1
        while bit < below:
            got.append(swap(part_sum(k | bit, bit), "chan", n_chan, bit))
            bit *= 2
        if k == 0:
            return [d_zero, *got]
        return call(
            merge_kernel, [shape((padded, width), BF16)],
            [after(d_expanded, d_near), w_cols[k], *got], flops=mm, name="merge", steps=2,
        )

    far_sum = part_sum(n_chan // 2, n_chan // 2)
    terms = [d_zero]
    bit = 1
    while bit < n_chan:
        mine = far_sum if bit == n_chan // 2 else part_sum(bit, bit)
        terms.append(swap(mine, "chan", n_chan, bit))
        bit *= 2
    expand_part = call(
        expand_grad_kernel, [shape((n_chan, width, share), BF16)],
        [after(d_expanded, far_sum), *hidden_all], flops=n_chan * mm, name="expand_grad",
    )
    bits = n_batch.bit_length() - 1
    top = bits - 1
    orders = [list(range(top)), [1, 0, *range(2, top)]]
    halves = [0, 1]
    got = [[], []]
    for s in range(top):
        send = send_both(dims, expand_part, got, orders, s)
        new = [swap(send[h], "batch", n_batch, 1 << orders[h][s]) for h in halves]
        if s == 0:
            block_out = call(
                block_kernel, [shape((rows, share), BF16)],
                [live, after(expanded, send[0]), got_one, got_three, gain_c, shift_c, own],
                flops=2 * mm, name="block", steps=STEPS,
            )
            new = [after(v, block_out) for v in new]
        got = [got[h] + [new[h]] for h in halves]
    mine = send_both(dims, expand_part, got, orders, top, True)
    expand_other = swap(mine, "batch", n_batch, 1 << (bits - 1))
    far_halves[0] = gather_core({k: after(v, far_sum) for k, v in far_halves[0].items()}, n_chan)
    terms[0] = after(d_zero, *far_halves[0].values())
    far_halves.append(gather_y(after(own, terms[-1], mine)[half:], n_chan))
    d_two, spread = call(
        d_two_kernel, [shape((padded, width), F32), shape((n_batch, 2, width), F32)],
        [slope_two, grouped, got_one, got_two, *terms], [acc(2, width)], flops=mm, name="d_two", steps=STEPS,
    )
    totals_two = batch_sum(spread)
    d_grouped, d_one, spread, sums_two = call(
        functools.partial(conv_back_kernel, side, slots),
        [shape((padded, width), F32)] * 2 + [shape((n_batch, 2, width), F32), shape((2, width), F32)],
        [live, d_two, grouped, got_two, totals_two, gain_two, slope_one, z, got_one, taps],
        [tall, acc(2, width)], flops=18 * padded * width * width, name="conv_back",
    )
    parts = call(
        split_kernel, [shape(mine.shape[1:], BF16)] * n_chan,
        [mine, after(expand_other, d_one)], name="split",
    )
    far_halves[1] = {k: after(v, d_one) for k, v in far_halves[1].items()}
    totals_one = batch_sum(after(spread, *parts, *far_halves[1].values()))
    d_reduced, sums_one = call(
        d_reduced_kernel, [shape((padded, width), BF16), shape((2, width), F32)],
        [live, d_one, z, got_one, totals_one, gain_one], flops=mm, name="d_reduced", steps=STEPS,
    )
    far_halves[1] = gather_core(far_halves[1], n_chan)
    firsts, lasts = ([far_halves[h][k] for k in others[2:]] for h in range(2))
    tail, rest = call(
        reduce_grad_kernel,
        [shape((n_chan * share, width), BF16), shape((n_chan - 2, share, width), F32)],
        [dims, d_reduced, own, beside, *firsts], flops=n_chan * mm, name="reduce_grad", smem=True,
    )
    tail = call(
        reduce_grad_rest_kernel, [shape((n_chan * share, width), BF16)],
        [dims, d_reduced, tail, rest, *lasts], flops=mm, name="reduce_grad_rest", smem=True,
    )
    d_beside = swap(d_reduced, "chan", n_chan, 1)
    tail = after(tail, d_beside)
    piece_rows = padded // PIECES
    d_far = []

    def far_rows(at, *ready):
        piece = after(d_reduced, *ready)[at * piece_rows : (at + 1) * piece_rows]
        d_far.append(gather_y(piece, n_chan))
        return list(d_far[at].values())

    def pass_on(at, *ready):
        d_far[at] = gather_core({k: after(v, *ready) for k, v in d_far[at].items()}, n_chan)
        return list(d_far[at].values())

    got = [[], []]
    for s in range(top):
        send = send_both(dims, tail, got, orders, s)
        new = [swap(send[h], "batch", n_batch, 1 << orders[h][s]) for h in halves]
        ties = []
        if s == 0:
            cols = [parts[0]]
            cols += [swap(after(parts[k], send[0]), "chan", n_chan, k) for k in others if k]
            cols = call(
                arrange_kernel, [shape((mine.shape[1] // 2, n_chan * share), BF16)] * 2, [dims, *cols],
                name="arrange", smem=True,
            )
            group_part = call(
                functools.partial(group_grad_kernel, side, slots, group_width),
                [shape((9 * group_width, width), BF16)],
                [live, z, got_one, gain_one, shift_one, after(d_grouped, *cols)],
                [tall], flops=mm, name="group_grad",
            )
            far_rows(0, *cols)
            ties = [group_part]
        elif s == 1:
            group_other = swap(after(group_part, send[0]), "batch", n_batch, 1)
            for t in reversed(range(1, top)):
                others_cols = [
                    swap(after(cols[h], send[0]), "batch", n_batch, 1 << orders[h][t])
                    for h in halves
                ]
                cols = double_pair(dims, cols, others_cols, [o[t] for o in orders])
            group_part = add(group_part, after(group_other, *cols))
            ties += [group_part, *d_far[0].values()]
            ties.append(cols)
        new = [after(v, *ties) for v in new]
        got = [got[i] + [new[i]] for i in range(2)]
    sums = send_both(dims, tail, got, orders, top, True)
    other = swap(sums, "batch", n_batch, 1 << top)
    others_cols = [
        swap(after(cols[h], sums), "batch", n_batch, 1 << orders[h][0]) for h in halves
    ]
    moved = [*far_rows(1, sums), *pass_on(0, sums)]
    part = call(
        features_grad_kernel, [shape((padded, share), F32)],
        [d_pre, after(d_reduced, sums), d_beside, *w_rows[:2]], flops=2 * mm,
        name="input_near", steps=STEPS,
    )
    others_cols[0] = after(others_cols[0], part)
    expand_grad = finish(dims, cols, others_cols, [o[0] for o in orders])
    sums = add(sums, after(other, expand_grad, *moved))
    pair = [sums]
    for s in reversed(range(top)):
        n = pair[0].shape[0] // (2 if len(pair) == 1 else 1)
        cut = [sums[:n], sums[n:]] if len(pair) == 1 else pair
        new = [swap(cut[i], "batch", n_batch, 1 << orders[i][s]) for i in range(2)]
        if s == top - 1:
            group_other = swap(after(group_part, sums), "batch", n_batch, 2)
            group_part = add(group_part, group_other)
            before = (group_part, *pass_on(1, sums))
        if s == 0:
            for t in range(2, bits):
                group_part = after(group_part, cut[0])
                group_other = swap(group_part, "batch", n_batch, 1 << t)
                if t == 2:
                    features_grad = call(
                        input_far_kernel, [shape((rows, share), F32)],
                        [after(part, cut[0]), *[d[k] for k in others[2:] for d in d_far], *w_rows[2:]],
                        flops=(n_chan - 2) * mm, name="input_far", steps=PIECES, size=padded,
                    )
                    group_other = after(group_other, features_grad)
                group_part = add(group_part, group_other, BF16 if t + 1 < bits else F32)
            before = (group_part,)
        new = [after(v, *before) for v in new]
        if s:
            pair = double_pair(dims, pair, new, [o[s] for o in orders])
    tail = finish(dims, pair, new, [o[0] for o in orders])
    reduce_grad, group_grad = tail, group_part

    shaped = lambda v: v.reshape(side, side, slots, share).transpose(2, 0, 1, 3)
    return (
        shaped(block_out),
        shaped(features_grad),
        reduce_grad,
        sums_one[1],
        sums_one[0],
        group_grad.reshape(3, 3, group_width, width),
        sums_two[1],
        sums_two[0],
        expand_grad,
        sums_three[1],
        sums_three[0],
    )


def gather_y(v, size):
    held = {0: v}
    bit = size // 2
    while bit > 1:
        held.update({k | bit: swap(b, "chan", size, bit) for k, b in list(held.items())})
        bit //= 2
    return {k: b for k, b in held.items() if k}


def gather_core(held, size):
    return held | {k | 1: swap(b, "chan", size, 1) for k, b in held.items()}


def solution(mesh):
    in_specs = (
        P("batch", None, None, "chan"),
        P(None, "chan"),
        P("chan"),
        P("chan"),
        P(None, None, None, "chan"),
        P("chan"),
        P("chan"),
        P("chan", None),
        P(),
        P(),
        P("batch", None, None, None),
        P("batch"),
        P("batch"),
    )
    out_specs = (
        P("batch", None, None, "chan"),
        P("batch", None, None, "chan"),
        P(None, "chan"),
        P("chan"),
        P("chan"),
        P(None, None, None, "chan"),
        P("chan"),
        P("chan"),
        P("chan", None),
        P("chan"),
        P("chan"),
    )
    n_batch, n_chan = mesh.shape["batch"], mesh.shape["chan"]

    def run(*args):
        return shards(n_batch, n_chan, *args)

    return jax.shard_map(run, mesh=mesh, in_specs=in_specs, out_specs=out_specs, check_vma=False)
```

```python
import functools

import jax
import jax.numpy as jnp
from jax import lax
from jax.experimental import pallas as pl
from jax.experimental.pallas import tpu as pltpu
from jax.sharding import PartitionSpec as P

EPSILON = 1e-05
ROOT = 0.7978845608028654
CUBE = 0.044715
F32 = jnp.float32
BF16 = jnp.bfloat16
STEP = 256
LANES = 128
LINES = 3
STEPS = 4
PIECES = 2
TN = (((0,), (0,)), ((), ()))
NT = (((1,), (1,)), ((), ()))
VM = pl.BlockSpec(memory_space=pltpu.VMEM)
SM = pl.BlockSpec(memory_space=pltpu.SMEM)


def dot(a, b):
    return jnp.dot(a, b, preferred_element_type=F32)


def dot_tn(a, b):
    return lax.dot_general(a, b, TN, preferred_element_type=F32)


def dot_nt(a, b):
    return lax.dot_general(a, b, NT, preferred_element_type=F32)


def bend(v):
    return jnp.tanh(v * (ROOT + (ROOT * CUBE) * (v * v)))


def act(v):
    half = 0.5 * v
    return half + half * bend(v)


def act_slope(v):
    t = bend(v)
    inner = v * (0.5 * ROOT + (1.5 * ROOT * CUBE) * (v * v))
    return 0.5 + 0.5 * t + inner * (1.0 - t * t)


def chunks(total, body, step=STEP):
    full = total // step

    def go(c, carry):
        body(pl.multiple_of(c * step, step), step)
        return carry

    if full:
        lax.fori_loop(0, full, go, 0)
    if total % step:
        body(full * step, total % step)


def fold(v):
    return jnp.sum(v.reshape(v.shape[0] // 8, 8, v.shape[1]), axis=0)


def widen(live, width):
    return jnp.concatenate([live] * (width // LANES), axis=1) if width > LANES else live


def norm_of(got, counts):
    s = jnp.sum(got[...], axis=0)
    share_of = 1.0 / jnp.sum(counts[...], axis=0)[2:3, 0:1]
    mu = s[0:1] * share_of
    return mu, lax.rsqrt(s[1:2] * share_of - mu * mu + EPSILON), share_of


def send_sums(out, acc):
    out[...] = jnp.broadcast_to(jnp.sum(acc[...], axis=1)[None], out.shape)


def start_sums(acc):
    @pl.when(pl.program_id(0) == 0)
    def _():
        acc[...] = jnp.zeros_like(acc)


def end_sums(out, acc):
    @pl.when(pl.program_id(0) == pl.num_programs(0) - 1)
    def _():
        send_sums(out, acc)


def near_kernel(dims, *refs):
    *feats, w, out = refs
    share = feats[0].shape[1]
    me = dims[2]
    ws = [w[pl.ds(pl.multiple_of((me ^ k) * share, share), share), :] for k in range(len(feats))]
    out[...] = sum(dot(f[...], wk) for f, wk in zip(feats, ws))


def part_far_kernel(dims, own, beside, *refs):
    n = len(refs) // 2
    share = own.shape[1]
    core = lax.bitwise_and(dims[2], 1)
    mine = pl.ds(pl.multiple_of(core * share, share), share)
    other = pl.ds(pl.multiple_of((1 - core) * share, share), share)
    for w, out in zip(refs[:n], refs[n:]):
        out[...] = (dot(own[...], w[mine, :]) + dot(beside[...], w[other, :])).astype(BF16)


def rows_kernel(dims, *refs):
    n = len(refs) // 3
    ws, rows, passed = (refs[i * n : (i + 1) * n] for i in range(3))
    share = rows[0].shape[0]
    core = lax.bitwise_and(dims[2], 1)
    for w, row, pass_on in zip(ws, rows, passed):
        row[...] = w[pl.ds(pl.multiple_of(core * share, share), share), :]
        pass_on[...] = w[pl.ds(pl.multiple_of((1 - core) * share, share), share), :]


def far_kernel(live, part, *refs):
    *got, out, spread, acc = refs
    start_sums(acc)
    z = part[...] + sum(g[...].astype(F32) for g in got)
    m = widen(live[...], z.shape[1])
    z = jnp.where(m > 0.0, z, 0.0)
    out[...] = z
    acc[0] += fold(z)
    acc[1] += fold(z * z)
    acc[2] += fold(m)
    end_sums(spread, acc)


def pad_edges(pad, side, line, wide, slots):
    width = pad.shape[1]
    pad[0:wide] = jnp.zeros((wide, width), F32)
    pad[(side + 1) * wide : (side + 2) * wide] = jnp.zeros((wide, width), F32)


def pad_line(pad, i, value, line, wide, slots):
    o = pl.multiple_of((i + 1) * wide, 8)
    edge = jnp.zeros((slots, pad.shape[1]), F32)
    pad[pl.ds(o, slots), :] = edge
    pad[pl.ds(o + slots, line), :] = value
    pad[pl.ds(o + slots + line, slots), :] = edge


def conv_lines(pad, first, count, taps, line, wide, slots, flip):
    total = None
    for t in range(9):
        a, b = divmod(t, 3)
        starts = [(first + i + a) * wide + b * slots for i in range(count)]
        x = jnp.concatenate([pad[o : o + line].astype(BF16) for o in starts], axis=0)
        d = dot_nt(x, taps[8 - t]) if flip else dot(x, taps[t])
        total = d if total is None else total + d
    return total


def taps_kernel(w, out):
    width, group_width = w.shape[2], w.shape[1]
    ids = [lax.broadcasted_iota(jnp.int32, (width, width), b) // group_width for b in range(2)]
    same = ids[0] == ids[1]
    for t in range(9):
        tiled = jnp.concatenate([w[t].astype(F32)] * (width // group_width), axis=0)
        out[t] = jnp.where(same, tiled, 0.0).astype(BF16)


def conv_kernel(side, slots, live, z, got, gain, shift, taps, out, spread, pad, acc):
    line, wide = side * slots, (side + 2) * slots
    rows, width = z.shape
    mu, r, _ = norm_of(got, got)
    a = r * gain[...]
    b = shift[...] - mu * a
    pad_edges(pad, side, line, wide, slots)
    acc[...] = jnp.zeros_like(acc)

    def fill(i, carry):
        here = pl.ds(pl.multiple_of(i * line, 8), line)
        h = widen(live[here, :], width) * act(z[here, :] * a + b)
        pad_line(pad, i, h.astype(BF16).astype(F32), line, wide, slots)
        return carry

    lax.fori_loop(0, side, fill, 0)

    for first in range(0, side, LINES):
        count = min(LINES, side - first)
        here = slice(first * line, (first + count) * line)
        total = conv_lines(pad, first, count, taps, line, wide, slots, False)
        out[here] = total
        m = widen(live[here], width) * total
        acc[0] += fold(m)
        acc[1] += fold(m * total)
    used = side * line
    out[used:rows] = jnp.zeros((rows - used, width), F32)
    send_sums(spread, acc)


def hidden_kernel(live, z, counts, got, gain, shift, out):
    mu, r, _ = norm_of(got, counts)
    a = r * gain[...]
    b = shift[...] - mu * a
    m = widen(live[...], z.shape[1])
    out[...] = (m * act(z[...] * a + b)).astype(BF16)


def slope_kernel(live, z, counts, got, gain, shift, out):
    mu, r, _ = norm_of(got, counts)
    a = r * gain[...]
    b = shift[...] - mu * a
    out[...] = widen(live[...], z.shape[1]) * act_slope(z[...] * a + b)


def expand_near_kernel(*refs):
    *ins, out = refs
    k = len(ins) // 2
    out[...] = sum(dot(h[...], w[...]) for h, w in zip(ins[:k], ins[k:]))


def expand_far_kernel(live, part, *refs):
    *ins, out, spread, acc = refs
    k = len(ins) // 2
    start_sums(acc)
    e = part[...] + sum(dot(h[...], w[...]) for h, w in zip(ins[:k], ins[k:]))
    out[...] = e
    m = widen(live[...], e.shape[1]) * e
    acc[0] += fold(m)
    acc[1] += fold(m * e)
    end_sums(spread, acc)


def third_kernel(live, e, counts, got, gain, shift, feats, cot, d_pre, spread, acc):
    mu, r, _ = norm_of(got, counts)
    start_sums(acc)
    zhat = (e[...] - mu) * r
    v = zhat * gain[...] + shift[...] + feats[...].astype(F32)
    m = widen(live[...], v.shape[1])
    d = m * cot[...].astype(F32) * act_slope(v)
    d_pre[...] = d
    acc[0] += fold(d)
    acc[1] += fold(d * zhat)
    end_sums(spread, acc)


def block_kernel(live, e, counts, got, gain, shift, feats, out):
    mu, r, _ = norm_of(got, counts)
    v = (e[...] - mu) * r * gain[...] + shift[...] + feats[...].astype(F32)
    out[...] = (widen(live[...], v.shape[1]) * act(v)).astype(BF16)


def d_expanded_kernel(live, e, d_pre, counts, got, totals, gain, w, d_exp, out, sums):
    mu, r, share_of = norm_of(got, counts)
    t = jnp.sum(totals[...], axis=0)
    sums[...] = t
    t = t * share_of
    scale = r * gain[...]
    zhat = (e[...] - mu) * r
    m = widen(live[...], zhat.shape[1])
    d = (m * scale * (d_pre[...] - t[0:1] - zhat * t[1:2])).astype(BF16)
    d_exp[...] = d
    out[...] = dot_nt(d, w[...]).astype(BF16)


def back_expand_kernel(d_exp, *refs):
    k = len(refs) // 2
    for w, out in zip(refs[:k], refs[k:]):
        out[...] = dot_nt(d_exp[...], w[...]).astype(out.dtype)


def merge_kernel(d_exp, w, *refs):
    *got, out = refs
    total = dot_nt(d_exp[...], w[...]) + sum(g[...].astype(F32) for g in got)
    out[...] = total.astype(BF16)


def expand_grad_kernel(d_exp, *refs):
    *hs, out = refs
    for k, h in enumerate(hs):
        out[k] = dot_tn(h[...], d_exp[...]).astype(BF16)


def d_two_kernel(slope, z, counts, got, *refs):
    *terms, d_out, spread, acc = refs
    mu, r, _ = norm_of(got, counts)
    start_sums(acc)
    d = sum(t[...].astype(F32) for t in terms) * slope[...]
    d_out[...] = d
    acc[0] += fold(d)
    acc[1] += fold(d * ((z[...] - mu) * r))
    end_sums(spread, acc)


def conv_back_kernel(
    side, slots, live, d_two, grouped, got_two, totals, gain, slope, z, got, taps,
    d_grouped, d_one, spread, sums, pad, acc,
):
    line, wide = side * slots, (side + 2) * slots
    rows, width = z.shape
    mu_two, r_two, share_of = norm_of(got_two, got)
    mu, r, _ = norm_of(got, got)
    t = jnp.sum(totals[...], axis=0)
    sums[...] = t
    t = t * share_of
    scale = r_two * gain[...]
    pad_edges(pad, side, line, wide, slots)
    acc[...] = jnp.zeros_like(acc)

    def fill(i, carry):
        here = pl.ds(pl.multiple_of(i * line, 8), line)
        zhat = (grouped[here, :] - mu_two) * r_two
        m = widen(live[here, :], width)
        d = m * scale * (d_two[here, :] - t[0:1] - zhat * t[1:2])
        d = d.astype(BF16).astype(F32)
        d_grouped[here, :] = d
        pad_line(pad, i, d, line, wide, slots)
        return carry

    lax.fori_loop(0, side, fill, 0)

    for first in range(0, side, LINES):
        count = min(LINES, side - first)
        here = slice(first * line, (first + count) * line)
        d = conv_lines(pad, first, count, taps, line, wide, slots, True) * slope[here]
        d_one[here] = d
        acc[0] += fold(d)
        acc[1] += fold(d * ((z[here] - mu) * r))
    used = side * line
    d_one[used:rows] = jnp.zeros((rows - used, width), F32)
    d_grouped[used:rows] = jnp.zeros((rows - used, width), F32)
    send_sums(spread, acc)


def d_reduced_kernel(live, d_one, z, got, totals, gain, out, sums):
    mu, r, share_of = norm_of(got, got)
    t = jnp.sum(totals[...], axis=0)
    sums[...] = t
    t = t * share_of
    zhat = (z[...] - mu) * r
    m = widen(live[...], zhat.shape[1])
    out[...] = (m * (r * gain[...]) * (d_one[...] - t[0:1] - zhat * t[1:2])).astype(BF16)


def group_grad_kernel(side, slots, group_width, live, z, got, gain, shift, d_grouped, out, pad):
    line, wide = side * slots, (side + 2) * slots
    width = z.shape[1]
    mu, r, _ = norm_of(got, got)
    scale = r * gain[...]
    offset = shift[...] - mu * scale
    pad_edges(pad, side, line, wide, slots)

    def fill(i, carry):
        here = pl.ds(pl.multiple_of(i * line, 8), line)
        h = widen(live[here, :], width) * act(z[here, :] * scale + offset)
        pad_line(pad, i, h.astype(BF16).astype(F32), line, wide, slots)
        return carry

    lax.fori_loop(0, side, fill, 0)
    d = d_grouped[0 : side * line].astype(BF16)
    ids = [lax.broadcasted_iota(jnp.int32, (width, width), b) // group_width for b in range(2)]
    same = ids[0] == ids[1]
    for t in range(9):
        a, b = divmod(t, 3)
        starts = [(i + a) * wide + b * slots for i in range(side)]
        x = jnp.concatenate([pad[o : o + line].astype(BF16) for o in starts], axis=0)
        dense = jnp.where(same, dot_tn(x, d), 0.0)
        picked = jnp.sum(dense.reshape(width // group_width, group_width, width), axis=0)
        out[t * group_width : (t + 1) * group_width] = picked.astype(BF16)


def reduce_grad_kernel(dims, d_red, *refs):
    *feats, out, rest = refs
    share = feats[0].shape[1]
    me = dims[2]
    for k in range(2):
        rows = pl.ds(pl.multiple_of((me ^ k) * share, share), share)
        out[rows, :] = dot_tn(feats[k][...], d_red[...]).astype(BF16)
    for k, f in enumerate(feats[2:]):
        rest[k] = dot_tn(f[...], d_red[0 : f.shape[0]])


def reduce_grad_rest_kernel(dims, d_red, near, rest, *refs):
    *feats, out = refs
    share = feats[0].shape[1]
    me = dims[2]
    for k in range(2):
        rows = pl.ds(pl.multiple_of((me ^ k) * share, share), share)
        out[rows, :] = near[rows, :]
    for k, f in enumerate(feats):
        rows = pl.ds(pl.multiple_of((me ^ (k + 2)) * share, share), share)
        first = d_red.shape[0] - f.shape[0]
        out[rows, :] = (rest[k] + dot_tn(f[...], d_red[first:])).astype(BF16)


def features_grad_kernel(part, *refs):
    *ins, out = refs
    k = len(ins) // 2
    out[...] = part[...] + sum(dot_nt(d[...], w[...]) for d, w in zip(ins[:k], ins[k:]))


def pick_kernel(dims, w_expand, w_reduce, gain, shift, cot, *outs):
    me = dims[2]
    n = len(outs) - 5
    cols, rows, rest = outs[:n], outs[n : n + 2], outs[n + 2 :]
    share = rows[0].shape[0]

    @pl.when(pl.program_id(0) == 0)
    def _():
        for k in range(n):
            at = pl.ds(pl.multiple_of((me ^ k) * share, share), share)
            cols[k][...] = w_expand[:, at]
            if k < 2:
                rows[k][...] = w_reduce[at, :]
        at = pl.ds(pl.multiple_of(me * share, share), share)
        rest[0][...] = gain[:, at]
        rest[1][...] = shift[:, at]

    at = pl.ds(pl.multiple_of(me * share, share), share)
    first = pl.program_id(0) * cot.shape[0]
    row = lax.broadcasted_iota(jnp.int32, (cot.shape[0], share), 0) + first
    rest[2][...] = jnp.where(row < dims[4], cot[:, at].astype(F32), 0.0).astype(BF16)


def bit_of(v, bit):
    return lax.bitwise_and(lax.shift_right_logical(v, bit), 1)


def add_terms(b, terms, order, step, last, base):
    total = None
    for first, (term, size) in enumerate(terms):
        rows, at = size, base if first == 0 else 0
        for t in range(first, step + (not last)):
            rows //= 2
            side = bit_of(b, order[t])
            at += rows * (side if t < step else 1 - side)
        here = pl.ds(at if isinstance(at, int) else pl.multiple_of(at, min(rows, 16)), rows)
        v = term[:, here, :] if len(term.shape) == 3 else term[here, :]
        total = v.astype(F32) if total is None else total + v.astype(F32)
    return total.astype(BF16)


def send_both_kernel(step, last, orders, dims, whole, *refs):
    half = whole.shape[-2] // 2
    n = step
    outs = refs[2 * n :]
    for i, order in enumerate(orders):
        terms = [(whole, half)] + [(r, r.shape[-2]) for r in refs[i * n : (i + 1) * n]]
        total = add_terms(dims[3], terms, order, step, last, i * half)
        rows = total.shape[-2]
        if last and len(whole.shape) == 3:
            outs[0][:, i * rows : (i + 1) * rows, :] = total
        elif last:
            outs[0][i * rows : (i + 1) * rows] = total
        else:
            outs[i][...] = total


def double_pair_kernel(bits, dims, sums, *refs):
    *ins, a, b = refs
    n = ins[0].shape[0]
    for i, (bit, out) in enumerate(zip(bits, (a, b))):
        mine = sums[i * n : (i + 1) * n] if len(ins) == 2 else (sums, ins[0])[i][...]
        other = ins[i] if len(ins) == 2 else ins[i + 1]
        upper = bit_of(dims[3], bit)
        out[pl.ds(pl.multiple_of(upper * n, min(n, 16)), n), :] = mine
        out[pl.ds(pl.multiple_of((1 - upper) * n, min(n, 16)), n), :] = other[...]


def finish_kernel(bits, dims, a, b, other_a, other_b, out):
    n = a.shape[0]
    for i, (bit, mine, other) in enumerate(zip(bits, (a, b), (other_a, other_b))):
        upper = bit_of(dims[3], bit)
        at = 2 * i * n
        out[pl.ds(pl.multiple_of(at + upper * n, min(n, 16)), n), :] = mine[...].astype(F32)
        out[pl.ds(pl.multiple_of(at + (1 - upper) * n, min(n, 16)), n), :] = other[...].astype(F32)


def arrange_kernel(dims, *refs):
    *cols, a, b = refs
    n, share = a.shape[0], cols[0].shape[1]
    for k, c in enumerate(cols):
        at = pl.ds(pl.multiple_of((dims[2] ^ k) * share, share), share)
        a[:, at] = c[0:n]
        b[:, at] = c[n:]


def split_kernel(a, b, *outs):
    for k, out in enumerate(outs):
        out[...] = (a[k].astype(F32) + b[k].astype(F32)).astype(BF16)


def add_kernel(a, b, out):
    out[...] = (a[...].astype(F32) + b[...].astype(F32)).astype(out.dtype)


def input_far_kernel(part, *refs):
    *ins, out = refs
    n = len(ins) // (PIECES + 1)
    ds, ws = ins[: n * PIECES], ins[n * PIECES :]
    for step in range(PIECES):

        @pl.when(pl.program_id(0) == step)
        def _(step=step):
            got = sum(dot_nt(ds[k * PIECES + step][...], w[...]) for k, w in enumerate(ws))
            out[...] = part[...] + got


def call(kernel, outs, ins, scratch=(), flops=0, name=None, smem=False, steps=0, size=0):
    moved = sum(x.size * x.dtype.itemsize for x in ins)
    moved += sum(int(o.size) * o.dtype.itemsize for o in outs)
    size = size or max(o.shape[0] for o in outs)
    block = -(-size // (16 * steps)) * 16 if steps else 0

    def spec(x):
        if not steps:
            return VM
        if len(x.shape) == 2 and steps * block - 64 < x.shape[0] <= steps * block:
            return pl.BlockSpec((block, x.shape[1]), lambda s: (s, 0))
        return pl.BlockSpec(x.shape, lambda s: (0,) * len(x.shape))

    specs = [spec(x) for x in ins]
    if smem:
        specs[0] = SM
    got = pl.pallas_call(
        kernel,
        out_shape=list(outs),
        grid=(steps,) if steps else (),
        in_specs=specs,
        out_specs=[spec(o) for o in outs],
        scratch_shapes=list(scratch),
        compiler_params=pltpu.CompilerParams(vmem_limit_bytes=16 << 20),
        cost_estimate=pl.CostEstimate(flops=flops, bytes_accessed=moved, transcendentals=0),
        name=name,
    )(*ins)
    return got[0] if len(outs) == 1 else got


def after(v, *others):
    return lax.optimization_barrier((v, *others))[0]


def swap(v, axis, size, k):
    return lax.ppermute(v, axis, [(i, i ^ k) for i in range(size)])


def batch_sum(spread):
    return lax.all_to_all(spread, "batch", 0, 0)


def pair_kernel(a, b, out):
    out[0:1] = a[...]
    out[1:2] = b[...]


def sum_kernel(*refs):
    *terms, out = refs
    out[...] = sum(t[...] for t in terms)


def batch_sum_stepwise(v, size):
    shape = jax.ShapeDtypeStruct(v.shape, v.dtype)
    got = [swap(v, "batch", size, k) for k in range(2, size, 2)]
    v = call(sum_kernel, [shape], [v, *got], name="sum")
    both = jax.ShapeDtypeStruct((2, *v.shape[1:]), v.dtype)
    return call(pair_kernel, [both], [v, swap(v, "batch", size, 1)], name="pair")


def gather_chan(v, size):
    held = {0: v}
    bit = size // 2
    while bit:
        held.update({k | bit: swap(b, "chan", size, bit) for k, b in list(held.items())})
        bit //= 2
    return [held[k] for k in range(size)]


def send_both(dims, whole, got, orders, step, last=False):
    shape = list(whole.shape)
    shape[-2] >>= step if last else step + 2
    return call(
        functools.partial(send_both_kernel, step, last, orders),
        [jax.ShapeDtypeStruct(tuple(shape), BF16)] * (1 if last else 2),
        [dims, whole, *got[0], *got[1]], name="send_both", smem=True,
    )


def double_pair(dims, pair, new, bits):
    n, columns = new[0].shape
    return call(
        functools.partial(double_pair_kernel, bits),
        [jax.ShapeDtypeStruct((2 * n, columns), BF16)] * 2, [dims, *pair, *new],
        name="double_pair", smem=True,
    )


def finish(dims, pair, new, bits):
    n, columns = new[0].shape
    return call(
        functools.partial(finish_kernel, bits), [jax.ShapeDtypeStruct((4 * n, columns), F32)],
        [dims, *pair, *new], name="finish", smem=True,
    )


def add(a, b, dtype=BF16):
    return call(add_kernel, [jax.ShapeDtypeStruct(a.shape, dtype)], [a, b], name="add")


def shards(n_batch, n_chan, *args):
    (features, w_reduce, gain_one, shift_one, w_group, gain_two, shift_two, w_expand,
     gain_three, shift_three, cotangent, resolution, crop_count) = args
    slots, side, _, share = features.shape
    width = w_reduce.shape[1]
    group_width = w_group.shape[2]
    rows = slots * side * side
    unit = 16 * STEPS
    padded = -(-rows // unit) * unit
    line, wide = side * slots, (side + 2) * slots
    me = lax.axis_index("chan")
    others = range(n_chan)
    shape = jax.ShapeDtypeStruct
    acc = lambda n, c: pltpu.VMEM((n, 8, c), F32)
    tall = pltpu.VMEM(((side + 2) * wide, width), F32)
    mm = 2 * padded * share * width

    feats = features.transpose(1, 2, 0, 3).reshape(rows, share)
    ends = ((0, padded - rows), (0, 0))
    even = [k for k in others[2:] if k % 2 == 0]
    at = [lax.bitwise_and(me ^ k, n_chan - 2) * share for k in even]
    w_far = [lax.dynamic_slice_in_dim(w_reduce, o, 2 * share, 0) for o in at]
    own = jnp.pad(after(feats, *w_far), ends)
    w_far = [swap(w, "chan", n_chan, k) for k, w in zip(even, w_far)]
    beside = swap(own, "chan", n_chan, 1)

    dims = jnp.stack(
        [resolution[0], crop_count[0], me, lax.axis_index("batch"), jnp.int32(rows)]
    )
    row = lax.broadcasted_iota(jnp.int32, (padded, LANES), 0)
    crop, j, i = row % slots, (row // slots) % side, row // line
    live = ((crop < crop_count[0]) & (i < resolution[0]) & (j < resolution[0])).astype(F32)
    taps = call(
        taps_kernel, [shape((9, width, width), BF16)], [w_group.reshape(9, group_width, width)],
        flops=mm, name="taps",
    )
    line_of = lambda v: v.reshape(1, -1)
    gain_one, shift_one, gain_two, shift_two = map(
        line_of, (gain_one, shift_one, gain_two, shift_two)
    )

    parts = call(
        part_far_kernel, [shape((padded, width), BF16)] * len(even), [dims, own, beside, *w_far],
        flops=2 * len(even) * mm, name="part_far", steps=2, smem=True,
    )
    parts = parts if len(even) > 1 else [parts]
    got = call(
        rows_kernel, [shape((share, width), BF16)] * 2 * len(even),
        [dims, *[after(w, *parts) for w in w_far]], name="rows", smem=True,
    )
    rows_far, passed = got[: len(even)], got[len(even) :]
    got = [swap(p, "chan", n_chan, k) for k, p in zip(even, parts)]

    *picked, gain_c, shift_c, cot = call(
        pick_kernel,
        [shape((width, share), BF16)] * n_chan + [shape((share, width), BF16)] * 2
        + [shape((1, share), F32)] * 2 + [shape((padded, share), BF16)],
        [dims, after(w_expand, *parts), w_reduce, line_of(gain_three), line_of(shift_three),
         cotangent.transpose(1, 2, 0, 3).reshape(rows, -1)],
        flops=mm, name="pick", smem=True, steps=STEPS,
    )
    part = call(
        near_kernel, [shape((padded, width), F32)], [dims, after(own, *parts), beside, w_reduce],
        flops=2 * mm, name="near", steps=STEPS, smem=True,
    )
    w_cols = [picked[0], swap(after(picked[1], part), "chan", n_chan, 1)]
    w_rows = [picked[n_chan], swap(after(picked[n_chan + 1], part), "chan", n_chan, 1)]
    for row, pass_on in zip(rows_far, passed):
        w_rows += [row, swap(after(pass_on, part), "chan", n_chan, 1)]
    ready = (part, live, cot, taps, gain_c, shift_c, w_cols[1], *w_rows, *picked)
    got = [after(v, *ready) for v in got]
    w_cols += [swap(after(picked[k], *got), "chan", n_chan, k) for k in others[2:]]
    z, spread = call(
        far_kernel, [shape((padded, width), F32), shape((1, 3, width), F32)],
        [live, part, *got], [acc(3, width)], flops=mm, name="far", steps=STEPS,
    )
    got_one = batch_sum_stepwise(spread, n_batch)

    grouped, spread = call(
        functools.partial(conv_kernel, side, slots),
        [shape((padded, width), F32), shape((n_batch, 2, width), F32)],
        [live, z, got_one, gain_one, shift_one, taps], [tall, acc(2, width)],
        flops=18 * padded * width * width, name="conv",
    )
    got_two = batch_sum(after(spread, *w_cols))
    hidden_two = call(
        hidden_kernel, [shape((padded, width), BF16)],
        [live, grouped, got_one, got_two, gain_two, shift_two], flops=mm, name="hidden", steps=STEPS,
    )
    half = padded * 42 // 64 // 16 * 16
    own_first = after(own, hidden_two)[:half]
    first = gather_y(hidden_two, n_chan)
    beside_two = swap(hidden_two, "chan", n_chan, 1)
    slope_two = call(
        slope_kernel, [shape((padded, width), F32)],
        [live, grouped, got_one, got_two, gain_two, shift_two], flops=mm, name="slope_two", steps=STEPS,
    )
    slope_one = call(
        slope_kernel, [shape((padded, width), F32)],
        [live, z, got_one, got_one, gain_one, shift_one], flops=mm, name="slope_one", steps=STEPS,
    )
    part = call(
        expand_near_kernel, [shape((padded, share), F32)], [hidden_two, beside_two, *w_cols[:2]],
        flops=2 * mm, name="expand_near", steps=2,
    )
    first = {k: after(v, part, slope_one, slope_two, own_first, *w_cols) for k, v in first.items()}
    far_halves = [gather_y(after(own_first, *first.values()), n_chan)]
    first = gather_core(first, n_chan)
    hidden_all = [hidden_two, beside_two] + [first[k] for k in others if k > 1]
    expanded, spread = call(
        expand_far_kernel, [shape((padded, share), F32), shape((n_batch, 2, share), F32)],
        [live, part, *hidden_all[2:], *w_cols[2:]], [acc(2, share)],
        flops=(n_chan - 2) * mm, name="expand_far", steps=STEPS,
    )
    got_three = batch_sum(spread)
    d_pre, spread = call(
        third_kernel, [shape((padded, share), F32), shape((n_batch, 2, share), F32)],
        [live, expanded, got_one, got_three, gain_c, shift_c, own, cot], [acc(2, share)],
        flops=4 * mm, name="third", steps=STEPS,
    )
    totals_three = batch_sum(spread)
    top = n_chan - 1
    d_expanded, sent, sums_three = call(
        d_expanded_kernel,
        [shape((padded, share), BF16), shape((padded, width), BF16), shape((2, share), F32)],
        [live, expanded, d_pre, got_one, got_three, totals_three, gain_c]
        + [w_cols[top]],
        flops=2 * mm, name="d_expanded", steps=STEPS,
    )
    early = [0, 1]
    far_halves[0] = {k: after(v, d_expanded) for k, v in far_halves[0].items()}
    d_zero, d_near = call(
        back_expand_kernel, [shape((padded, width), F32), shape((padded, width), BF16)],
        [after(d_expanded, sent, *far_halves[0].values())] + [w_cols[k] for k in early], flops=2 * mm,
        name="back_expand", steps=2,
    )

    def part_sum(k, below):
        if k == top:
            return sent
        if k == 1:
            return d_near
        got, bit = [], 1
        while bit < below:
            got.append(swap(part_sum(k | bit, bit), "chan", n_chan, bit))
            bit *= 2
        if k == 0:
            return [d_zero, *got]
        return call(
            merge_kernel, [shape((padded, width), BF16)],
            [after(d_expanded, d_near), w_cols[k], *got], flops=mm, name="merge", steps=2,
        )

    far_sum = part_sum(n_chan // 2, n_chan // 2)
    terms = [d_zero]
    bit = 1
    while bit < n_chan:
        mine = far_sum if bit == n_chan // 2 else part_sum(bit, bit)
        terms.append(swap(mine, "chan", n_chan, bit))
        bit *= 2
    expand_part = call(
        expand_grad_kernel, [shape((n_chan, width, share), BF16)],
        [after(d_expanded, far_sum), *hidden_all], flops=n_chan * mm, name="expand_grad",
    )
    bits = n_batch.bit_length() - 1
    top = bits - 1
    orders = [list(range(top)), [1, 0, *range(2, top)]]
    halves = [0, 1]
    got = [[], []]
    for s in range(top):
        send = send_both(dims, expand_part, got, orders, s)
        new = [swap(send[h], "batch", n_batch, 1 << orders[h][s]) for h in halves]
        if s == 0:
            block_out = call(
                block_kernel, [shape((rows, share), BF16)],
                [live, after(expanded, send[0]), got_one, got_three, gain_c, shift_c, own],
                flops=2 * mm, name="block", steps=STEPS,
            )
            new = [after(v, block_out) for v in new]
        got = [got[h] + [new[h]] for h in halves]
    mine = send_both(dims, expand_part, got, orders, top, True)
    expand_other = swap(mine, "batch", n_batch, 1 << (bits - 1))
    far_halves[0] = gather_core({k: after(v, far_sum) for k, v in far_halves[0].items()}, n_chan)
    terms[0] = after(d_zero, *far_halves[0].values())
    far_halves.append(gather_y(after(own, terms[-1], mine)[half:], n_chan))
    d_two, spread = call(
        d_two_kernel, [shape((padded, width), F32), shape((n_batch, 2, width), F32)],
        [slope_two, grouped, got_one, got_two, *terms], [acc(2, width)], flops=mm, name="d_two", steps=STEPS,
    )
    totals_two = batch_sum(spread)
    d_grouped, d_one, spread, sums_two = call(
        functools.partial(conv_back_kernel, side, slots),
        [shape((padded, width), F32)] * 2 + [shape((n_batch, 2, width), F32), shape((2, width), F32)],
        [live, d_two, grouped, got_two, totals_two, gain_two, slope_one, z, got_one, taps],
        [tall, acc(2, width)], flops=18 * padded * width * width, name="conv_back",
    )
    parts = call(
        split_kernel, [shape(mine.shape[1:], BF16)] * n_chan,
        [mine, after(expand_other, d_one)], name="split",
    )
    far_halves[1] = {k: after(v, d_one) for k, v in far_halves[1].items()}
    totals_one = batch_sum(after(spread, *parts, *far_halves[1].values()))
    d_reduced, sums_one = call(
        d_reduced_kernel, [shape((padded, width), BF16), shape((2, width), F32)],
        [live, d_one, z, got_one, totals_one, gain_one], flops=mm, name="d_reduced", steps=STEPS,
    )
    far_halves[1] = gather_core(far_halves[1], n_chan)
    firsts, lasts = ([far_halves[h][k] for k in others[2:]] for h in range(2))
    tail, rest = call(
        reduce_grad_kernel,
        [shape((n_chan * share, width), BF16), shape((n_chan - 2, share, width), F32)],
        [dims, d_reduced, own, beside, *firsts], flops=n_chan * mm, name="reduce_grad", smem=True,
    )
    tail = call(
        reduce_grad_rest_kernel, [shape((n_chan * share, width), BF16)],
        [dims, d_reduced, tail, rest, *lasts], flops=mm, name="reduce_grad_rest", smem=True,
    )
    d_beside = swap(d_reduced, "chan", n_chan, 1)
    tail = after(tail, d_beside)
    piece_rows = padded // PIECES
    d_far = []

    def far_rows(at, *ready):
        piece = after(d_reduced, *ready)[at * piece_rows : (at + 1) * piece_rows]
        d_far.append(gather_y(piece, n_chan))
        return list(d_far[at].values())

    def pass_on(at, *ready):
        d_far[at] = gather_core({k: after(v, *ready) for k, v in d_far[at].items()}, n_chan)
        return list(d_far[at].values())

    got = [[], []]
    for s in range(top):
        send = send_both(dims, tail, got, orders, s)
        new = [swap(send[h], "batch", n_batch, 1 << orders[h][s]) for h in halves]
        ties = []
        if s == 0:
            cols = [parts[0]]
            cols += [swap(after(parts[k], send[0]), "chan", n_chan, k) for k in others if k]
            cols = call(
                arrange_kernel, [shape((mine.shape[1] // 2, n_chan * share), BF16)] * 2, [dims, *cols],
                name="arrange", smem=True,
            )
            group_part = call(
                functools.partial(group_grad_kernel, side, slots, group_width),
                [shape((9 * group_width, width), BF16)],
                [live, z, got_one, gain_one, shift_one, after(d_grouped, *cols)],
                [tall], flops=mm, name="group_grad",
            )
            far_rows(0, *cols)
            ties = [group_part]
        elif s == 1:
            group_other = swap(after(group_part, send[0]), "batch", n_batch, 1)
            others_cols = [
                swap(after(cols[h], send[0]), "batch", n_batch, 1 << orders[h][top - 1])
                for h in halves
            ]
        new = [after(v, *ties) for v in new]
        got = [got[i] + [new[i]] for i in range(2)]
    sums = send_both(dims, tail, got, orders, top, True)
    other = swap(sums, "batch", n_batch, 1 << top)
    others_cols = [after(v, sums) for v in others_cols]
    cols = double_pair(dims, cols, others_cols, [o[top - 1] for o in orders])
    for t in reversed(range(1, top - 1)):
        others_cols = [swap(cols[h], "batch", n_batch, 1 << orders[h][t]) for h in halves]
        cols = double_pair(dims, cols, others_cols, [o[t] for o in orders])
    group_part = add(group_part, after(group_other, *cols))
    others_cols = [
        swap(after(cols[h], sums), "batch", n_batch, 1 << orders[h][0]) for h in halves
    ]
    moved = [*far_rows(1, sums), *pass_on(0, sums)]
    part = call(
        features_grad_kernel, [shape((padded, share), F32)],
        [d_pre, after(d_reduced, group_part), d_beside, *w_rows[:2]], flops=2 * mm,
        name="input_near", steps=STEPS,
    )
    sums = add(sums, after(other, part))
    others_cols = [after(v, sums) for v in others_cols]
    moved = [after(v, sums) for v in moved]
    expand_grad = finish(dims, cols, others_cols, [o[0] for o in orders])
    pair = [sums]
    for s in reversed(range(top)):
        n = pair[0].shape[0] // (2 if len(pair) == 1 else 1)
        cut = [sums[:n], sums[n:]] if len(pair) == 1 else pair
        new = [swap(cut[i], "batch", n_batch, 1 << orders[i][s]) for i in range(2)]
        if s == top - 1:
            group_other = swap(after(group_part, sums), "batch", n_batch, 2)
            group_part = add(group_part, after(group_other, expand_grad))
            before = (group_part,)
        if s == 0:
            pass_on(1, cut[0])
            for t in range(2, bits):
                group_part = after(group_part, cut[0])
                group_other = swap(group_part, "batch", n_batch, 1 << t)
                if t == 2:
                    features_grad = call(
                        input_far_kernel, [shape((rows, share), F32)],
                        [after(part, cut[0]), *[d[k] for k in others[2:] for d in d_far], *w_rows[2:]],
                        flops=(n_chan - 2) * mm, name="input_far", steps=PIECES, size=padded,
                    )
                    group_other = after(group_other, features_grad)
                group_part = add(group_part, group_other, BF16 if t + 1 < bits else F32)
            before = (group_part,)
        new = [after(v, *before) for v in new]
        if s:
            pair = double_pair(dims, pair, new, [o[s] for o in orders])
    tail = finish(dims, pair, new, [o[0] for o in orders])
    reduce_grad, group_grad = tail, group_part

    shaped = lambda v: v.reshape(side, side, slots, share).transpose(2, 0, 1, 3)
    return (
        shaped(block_out),
        shaped(features_grad),
        reduce_grad,
        sums_one[1],
        sums_one[0],
        group_grad.reshape(3, 3, group_width, width),
        sums_two[1],
        sums_two[0],
        expand_grad,
        sums_three[1],
        sums_three[0],
    )


def gather_y(v, size):
    held = {0: v}
    bit = size // 2
    while bit > 1:
        held.update({k | bit: swap(b, "chan", size, bit) for k, b in list(held.items())})
        bit //= 2
    return {k: b for k, b in held.items() if k}


def gather_core(held, size):
    return held | {k | 1: swap(b, "chan", size, 1) for k, b in held.items()}


def solution(mesh):
    in_specs = (
        P("batch", None, None, "chan"),
        P(None, "chan"),
        P("chan"),
        P("chan"),
        P(None, None, None, "chan"),
        P("chan"),
        P("chan"),
        P("chan", None),
        P(),
        P(),
        P("batch", None, None, None),
        P("batch"),
        P("batch"),
    )
    out_specs = (
        P("batch", None, None, "chan"),
        P("batch", None, None, "chan"),
        P(None, "chan"),
        P("chan"),
        P("chan"),
        P(None, None, None, "chan"),
        P("chan"),
        P("chan"),
        P("chan", None),
        P("chan"),
        P("chan"),
    )
    n_batch, n_chan = mesh.shape["batch"], mesh.shape["chan"]

    def run(*args):
        return shards(n_batch, n_chan, *args)

    return jax.shard_map(run, mesh=mesh, in_specs=in_specs, out_specs=out_specs, check_vma=False)
```

```python
import functools

import jax
import jax.numpy as jnp
from jax import lax
from jax.experimental import pallas as pl
from jax.experimental.pallas import tpu as pltpu
from jax.sharding import PartitionSpec as P

EPSILON = 1e-05
ROOT = 0.7978845608028654
CUBE = 0.044715
F32 = jnp.float32
BF16 = jnp.bfloat16
STEP = 256
LANES = 128
LINES = 3
STEPS = 4
PIECES = 2
TN = (((0,), (0,)), ((), ()))
NT = (((1,), (1,)), ((), ()))
VM = pl.BlockSpec(memory_space=pltpu.VMEM)
SM = pl.BlockSpec(memory_space=pltpu.SMEM)


def dot(a, b):
    return jnp.dot(a, b, preferred_element_type=F32)


def dot_tn(a, b):
    return lax.dot_general(a, b, TN, preferred_element_type=F32)


def dot_nt(a, b):
    return lax.dot_general(a, b, NT, preferred_element_type=F32)


def bend(v):
    return jnp.tanh(v * (ROOT + (ROOT * CUBE) * (v * v)))


def act(v):
    half = 0.5 * v
    return half + half * bend(v)


def act_slope(v):
    t = bend(v)
    inner = v * (0.5 * ROOT + (1.5 * ROOT * CUBE) * (v * v))
    return 0.5 + 0.5 * t + inner * (1.0 - t * t)


def chunks(total, body, step=STEP):
    full = total // step

    def go(c, carry):
        body(pl.multiple_of(c * step, step), step)
        return carry

    if full:
        lax.fori_loop(0, full, go, 0)
    if total % step:
        body(full * step, total % step)


def fold(v):
    return jnp.sum(v.reshape(v.shape[0] // 8, 8, v.shape[1]), axis=0)


def widen(live, width):
    return jnp.concatenate([live] * (width // LANES), axis=1) if width > LANES else live


def norm_of(got, counts):
    s = jnp.sum(got[...], axis=0)
    share_of = 1.0 / jnp.sum(counts[...], axis=0)[2:3, 0:1]
    mu = s[0:1] * share_of
    return mu, lax.rsqrt(s[1:2] * share_of - mu * mu + EPSILON), share_of


def send_sums(out, acc):
    out[...] = jnp.broadcast_to(jnp.sum(acc[...], axis=1)[None], out.shape)


def start_sums(acc):
    @pl.when(pl.program_id(0) == 0)
    def _():
        acc[...] = jnp.zeros_like(acc)


def end_sums(out, acc):
    @pl.when(pl.program_id(0) == pl.num_programs(0) - 1)
    def _():
        send_sums(out, acc)


def near_kernel(dims, *refs):
    *feats, w, out = refs
    share = feats[0].shape[1]
    me = dims[2]
    ws = [w[pl.ds(pl.multiple_of((me ^ k) * share, share), share), :] for k in range(len(feats))]
    out[...] = sum(dot(f[...], wk) for f, wk in zip(feats, ws))


def part_far_kernel(dims, own, beside, *refs):
    n = len(refs) // 2
    share = own.shape[1]
    core = lax.bitwise_and(dims[2], 1)
    mine = pl.ds(pl.multiple_of(core * share, share), share)
    other = pl.ds(pl.multiple_of((1 - core) * share, share), share)
    for w, out in zip(refs[:n], refs[n:]):
        out[...] = (dot(own[...], w[mine, :]) + dot(beside[...], w[other, :])).astype(BF16)


def rows_kernel(dims, *refs):
    n = len(refs) // 3
    ws, rows, passed = (refs[i * n : (i + 1) * n] for i in range(3))
    share = rows[0].shape[0]
    core = lax.bitwise_and(dims[2], 1)
    for w, row, pass_on in zip(ws, rows, passed):
        row[...] = w[pl.ds(pl.multiple_of(core * share, share), share), :]
        pass_on[...] = w[pl.ds(pl.multiple_of((1 - core) * share, share), share), :]


def far_kernel(live, part, *refs):
    *got, out, spread, acc = refs
    start_sums(acc)
    z = part[...] + sum(g[...].astype(F32) for g in got)
    m = widen(live[...], z.shape[1])
    z = jnp.where(m > 0.0, z, 0.0)
    out[...] = z
    acc[0] += fold(z)
    acc[1] += fold(z * z)
    acc[2] += fold(m)
    end_sums(spread, acc)


def pad_edges(pad, side, line, wide, slots):
    width = pad.shape[1]
    pad[0:wide] = jnp.zeros((wide, width), F32)
    pad[(side + 1) * wide : (side + 2) * wide] = jnp.zeros((wide, width), F32)


def pad_line(pad, i, value, line, wide, slots):
    o = pl.multiple_of((i + 1) * wide, 8)
    edge = jnp.zeros((slots, pad.shape[1]), F32)
    pad[pl.ds(o, slots), :] = edge
    pad[pl.ds(o + slots, line), :] = value
    pad[pl.ds(o + slots + line, slots), :] = edge


def conv_lines(pad, first, count, taps, line, wide, slots, flip):
    total = None
    for t in range(9):
        a, b = divmod(t, 3)
        starts = [(first + i + a) * wide + b * slots for i in range(count)]
        x = jnp.concatenate([pad[o : o + line].astype(BF16) for o in starts], axis=0)
        d = dot_nt(x, taps[8 - t]) if flip else dot(x, taps[t])
        total = d if total is None else total + d
    return total


def taps_kernel(w, out):
    width, group_width = w.shape[2], w.shape[1]
    ids = [lax.broadcasted_iota(jnp.int32, (width, width), b) // group_width for b in range(2)]
    same = ids[0] == ids[1]
    for t in range(9):
        tiled = jnp.concatenate([w[t].astype(F32)] * (width // group_width), axis=0)
        out[t] = jnp.where(same, tiled, 0.0).astype(BF16)


def conv_kernel(side, slots, live, z, got, gain, shift, taps, out, spread, pad, acc):
    line, wide = side * slots, (side + 2) * slots
    rows, width = z.shape
    mu, r, _ = norm_of(got, got)
    a = r * gain[...]
    b = shift[...] - mu * a
    pad_edges(pad, side, line, wide, slots)
    acc[...] = jnp.zeros_like(acc)

    def fill(i, carry):
        here = pl.ds(pl.multiple_of(i * line, 8), line)
        h = widen(live[here, :], width) * act(z[here, :] * a + b)
        pad_line(pad, i, h.astype(BF16).astype(F32), line, wide, slots)
        return carry

    lax.fori_loop(0, side, fill, 0)

    for first in range(0, side, LINES):
        count = min(LINES, side - first)
        here = slice(first * line, (first + count) * line)
        total = conv_lines(pad, first, count, taps, line, wide, slots, False)
        out[here] = total
        m = widen(live[here], width) * total
        acc[0] += fold(m)
        acc[1] += fold(m * total)
    used = side * line
    out[used:rows] = jnp.zeros((rows - used, width), F32)
    send_sums(spread, acc)


def hidden_kernel(live, z, counts, got, gain, shift, out):
    mu, r, _ = norm_of(got, counts)
    a = r * gain[...]
    b = shift[...] - mu * a
    m = widen(live[...], z.shape[1])
    out[...] = (m * act(z[...] * a + b)).astype(BF16)


def slope_kernel(live, z, counts, got, gain, shift, out):
    mu, r, _ = norm_of(got, counts)
    a = r * gain[...]
    b = shift[...] - mu * a
    out[...] = widen(live[...], z.shape[1]) * act_slope(z[...] * a + b)


def expand_near_kernel(*refs):
    *ins, out = refs
    k = len(ins) // 2
    out[...] = sum(dot(h[...], w[...]) for h, w in zip(ins[:k], ins[k:]))


def expand_far_kernel(live, part, *refs):
    *ins, out, spread, acc = refs
    k = len(ins) // 2
    start_sums(acc)
    e = part[...] + sum(dot(h[...], w[...]) for h, w in zip(ins[:k], ins[k:]))
    out[...] = e
    m = widen(live[...], e.shape[1]) * e
    acc[0] += fold(m)
    acc[1] += fold(m * e)
    end_sums(spread, acc)


def third_kernel(live, e, counts, got, gain, shift, feats, cot, d_pre, spread, acc):
    mu, r, _ = norm_of(got, counts)
    start_sums(acc)
    zhat = (e[...] - mu) * r
    v = zhat * gain[...] + shift[...] + feats[...].astype(F32)
    m = widen(live[...], v.shape[1])
    d = m * cot[...].astype(F32) * act_slope(v)
    d_pre[...] = d
    acc[0] += fold(d)
    acc[1] += fold(d * zhat)
    end_sums(spread, acc)


def block_kernel(live, e, counts, got, gain, shift, feats, out):
    mu, r, _ = norm_of(got, counts)
    v = (e[...] - mu) * r * gain[...] + shift[...] + feats[...].astype(F32)
    out[...] = (widen(live[...], v.shape[1]) * act(v)).astype(BF16)


def d_expanded_kernel(live, e, d_pre, counts, got, totals, gain, w, d_exp, out, sums):
    mu, r, share_of = norm_of(got, counts)
    t = jnp.sum(totals[...], axis=0)
    sums[...] = t
    t = t * share_of
    scale = r * gain[...]
    zhat = (e[...] - mu) * r
    m = widen(live[...], zhat.shape[1])
    d = (m * scale * (d_pre[...] - t[0:1] - zhat * t[1:2])).astype(BF16)
    d_exp[...] = d
    out[...] = dot_nt(d, w[...]).astype(BF16)


def back_expand_kernel(d_exp, *refs):
    k = len(refs) // 2
    for w, out in zip(refs[:k], refs[k:]):
        out[...] = dot_nt(d_exp[...], w[...]).astype(out.dtype)


def merge_kernel(d_exp, w, *refs):
    *got, out = refs
    total = dot_nt(d_exp[...], w[...]) + sum(g[...].astype(F32) for g in got)
    out[...] = total.astype(BF16)


def expand_grad_kernel(d_exp, *refs):
    *hs, out = refs
    for k, h in enumerate(hs):
        out[k] = dot_tn(h[...], d_exp[...]).astype(BF16)


def d_two_kernel(slope, z, counts, got, *refs):
    *terms, d_out, spread, acc = refs
    mu, r, _ = norm_of(got, counts)
    start_sums(acc)
    d = sum(t[...].astype(F32) for t in terms) * slope[...]
    d_out[...] = d
    acc[0] += fold(d)
    acc[1] += fold(d * ((z[...] - mu) * r))
    end_sums(spread, acc)


def conv_back_kernel(
    side, slots, live, d_two, grouped, got_two, totals, gain, slope, z, got, taps,
    d_grouped, d_one, spread, sums, pad, acc,
):
    line, wide = side * slots, (side + 2) * slots
    rows, width = z.shape
    mu_two, r_two, share_of = norm_of(got_two, got)
    mu, r, _ = norm_of(got, got)
    t = jnp.sum(totals[...], axis=0)
    sums[...] = t
    t = t * share_of
    scale = r_two * gain[...]
    pad_edges(pad, side, line, wide, slots)
    acc[...] = jnp.zeros_like(acc)

    def fill(i, carry):
        here = pl.ds(pl.multiple_of(i * line, 8), line)
        zhat = (grouped[here, :] - mu_two) * r_two
        m = widen(live[here, :], width)
        d = m * scale * (d_two[here, :] - t[0:1] - zhat * t[1:2])
        d = d.astype(BF16).astype(F32)
        d_grouped[here, :] = d
        pad_line(pad, i, d, line, wide, slots)
        return carry

    lax.fori_loop(0, side, fill, 0)

    for first in range(0, side, LINES):
        count = min(LINES, side - first)
        here = slice(first * line, (first + count) * line)
        d = conv_lines(pad, first, count, taps, line, wide, slots, True) * slope[here]
        d_one[here] = d
        acc[0] += fold(d)
        acc[1] += fold(d * ((z[here] - mu) * r))
    used = side * line
    d_one[used:rows] = jnp.zeros((rows - used, width), F32)
    d_grouped[used:rows] = jnp.zeros((rows - used, width), F32)
    send_sums(spread, acc)


def d_reduced_kernel(live, d_one, z, got, totals, gain, out, sums):
    mu, r, share_of = norm_of(got, got)
    t = jnp.sum(totals[...], axis=0)
    sums[...] = t
    t = t * share_of
    zhat = (z[...] - mu) * r
    m = widen(live[...], zhat.shape[1])
    out[...] = (m * (r * gain[...]) * (d_one[...] - t[0:1] - zhat * t[1:2])).astype(BF16)


def group_grad_kernel(side, slots, group_width, live, z, got, gain, shift, d_grouped, out, pad):
    line, wide = side * slots, (side + 2) * slots
    width = z.shape[1]
    mu, r, _ = norm_of(got, got)
    scale = r * gain[...]
    offset = shift[...] - mu * scale
    pad_edges(pad, side, line, wide, slots)

    def fill(i, carry):
        here = pl.ds(pl.multiple_of(i * line, 8), line)
        h = widen(live[here, :], width) * act(z[here, :] * scale + offset)
        pad_line(pad, i, h.astype(BF16).astype(F32), line, wide, slots)
        return carry

    lax.fori_loop(0, side, fill, 0)
    d = d_grouped[0 : side * line].astype(BF16)
    ids = [lax.broadcasted_iota(jnp.int32, (width, width), b) // group_width for b in range(2)]
    same = ids[0] == ids[1]
    for t in range(9):
        a, b = divmod(t, 3)
        starts = [(i + a) * wide + b * slots for i in range(side)]
        x = jnp.concatenate([pad[o : o + line].astype(BF16) for o in starts], axis=0)
        dense = jnp.where(same, dot_tn(x, d), 0.0)
        picked = jnp.sum(dense.reshape(width // group_width, group_width, width), axis=0)
        out[t * group_width : (t + 1) * group_width] = picked.astype(BF16)


def reduce_grad_kernel(dims, d_red, *refs):
    *feats, out, rest = refs
    share = feats[0].shape[1]
    me = dims[2]
    for k in range(2):
        rows = pl.ds(pl.multiple_of((me ^ k) * share, share), share)
        out[rows, :] = dot_tn(feats[k][...], d_red[...]).astype(BF16)
    for k, f in enumerate(feats[2:]):
        rest[k] = dot_tn(f[...], d_red[0 : f.shape[0]])


def reduce_grad_rest_kernel(dims, d_red, near, rest, *refs):
    *feats, out = refs
    share = feats[0].shape[1]
    me = dims[2]
    for k in range(2):
        rows = pl.ds(pl.multiple_of((me ^ k) * share, share), share)
        out[rows, :] = near[rows, :]
    for k, f in enumerate(feats):
        rows = pl.ds(pl.multiple_of((me ^ (k + 2)) * share, share), share)
        first = d_red.shape[0] - f.shape[0]
        out[rows, :] = (rest[k] + dot_tn(f[...], d_red[first:])).astype(BF16)


def features_grad_kernel(part, *refs):
    *ins, out = refs
    k = len(ins) // 2
    out[...] = part[...] + sum(dot_nt(d[...], w[...]) for d, w in zip(ins[:k], ins[k:]))


def pick_kernel(dims, w_expand, w_reduce, gain, shift, cot, *outs):
    me = dims[2]
    n = len(outs) - 5
    cols, rows, rest = outs[:n], outs[n : n + 2], outs[n + 2 :]
    share = rows[0].shape[0]

    @pl.when(pl.program_id(0) == 0)
    def _():
        for k in range(n):
            at = pl.ds(pl.multiple_of((me ^ k) * share, share), share)
            cols[k][...] = w_expand[:, at]
            if k < 2:
                rows[k][...] = w_reduce[at, :]
        at = pl.ds(pl.multiple_of(me * share, share), share)
        rest[0][...] = gain[:, at]
        rest[1][...] = shift[:, at]

    at = pl.ds(pl.multiple_of(me * share, share), share)
    first = pl.program_id(0) * cot.shape[0]
    row = lax.broadcasted_iota(jnp.int32, (cot.shape[0], share), 0) + first
    rest[2][...] = jnp.where(row < dims[4], cot[:, at].astype(F32), 0.0).astype(BF16)


def bit_of(v, bit):
    return lax.bitwise_and(lax.shift_right_logical(v, bit), 1)


def add_terms(b, terms, order, step, last, base):
    total = None
    for first, (term, size) in enumerate(terms):
        rows, at = size, base if first == 0 else 0
        for t in range(first, step + (not last)):
            rows //= 2
            side = bit_of(b, order[t])
            at += rows * (side if t < step else 1 - side)
        here = pl.ds(at if isinstance(at, int) else pl.multiple_of(at, min(rows, 16)), rows)
        v = term[:, here, :] if len(term.shape) == 3 else term[here, :]
        total = v.astype(F32) if total is None else total + v.astype(F32)
    return total.astype(BF16)


def send_both_kernel(step, last, orders, dims, whole, *refs):
    half = whole.shape[-2] // 2
    n = step
    outs = refs[2 * n :]
    for i, order in enumerate(orders):
        terms = [(whole, half)] + [(r, r.shape[-2]) for r in refs[i * n : (i + 1) * n]]
        total = add_terms(dims[3], terms, order, step, last, i * half)
        rows = total.shape[-2]
        if last and len(whole.shape) == 3:
            outs[0][:, i * rows : (i + 1) * rows, :] = total
        elif last:
            outs[0][i * rows : (i + 1) * rows] = total
        else:
            outs[i][...] = total


def double_pair_kernel(bits, dims, sums, *refs):
    *ins, a, b = refs
    n = ins[0].shape[0]
    for i, (bit, out) in enumerate(zip(bits, (a, b))):
        mine = sums[i * n : (i + 1) * n] if len(ins) == 2 else (sums, ins[0])[i][...]
        other = ins[i] if len(ins) == 2 else ins[i + 1]
        upper = bit_of(dims[3], bit)
        out[pl.ds(pl.multiple_of(upper * n, min(n, 16)), n), :] = mine
        out[pl.ds(pl.multiple_of((1 - upper) * n, min(n, 16)), n), :] = other[...]


def finish_kernel(bits, dims, a, b, other_a, other_b, out):
    n = a.shape[0]
    for i, (bit, mine, other) in enumerate(zip(bits, (a, b), (other_a, other_b))):
        upper = bit_of(dims[3], bit)
        at = 2 * i * n
        out[pl.ds(pl.multiple_of(at + upper * n, min(n, 16)), n), :] = mine[...].astype(F32)
        out[pl.ds(pl.multiple_of(at + (1 - upper) * n, min(n, 16)), n), :] = other[...].astype(F32)


def arrange_kernel(dims, *refs):
    *cols, a, b = refs
    n, share = a.shape[0], cols[0].shape[1]
    for k, c in enumerate(cols):
        at = pl.ds(pl.multiple_of((dims[2] ^ k) * share, share), share)
        a[:, at] = c[0:n]
        b[:, at] = c[n:]


def split_kernel(a, b, *outs):
    for k, out in enumerate(outs):
        out[...] = (a[k].astype(F32) + b[k].astype(F32)).astype(BF16)


def add_kernel(a, b, out):
    out[...] = (a[...].astype(F32) + b[...].astype(F32)).astype(out.dtype)


def input_far_kernel(part, *refs):
    *ins, out = refs
    n = len(ins) // (PIECES + 1)
    ds, ws = ins[: n * PIECES], ins[n * PIECES :]
    for step in range(PIECES):

        @pl.when(pl.program_id(0) == step)
        def _(step=step):
            got = sum(dot_nt(ds[k * PIECES + step][...], w[...]) for k, w in enumerate(ws))
            out[...] = part[...] + got


def call(kernel, outs, ins, scratch=(), flops=0, name=None, smem=False, steps=0, size=0):
    moved = sum(x.size * x.dtype.itemsize for x in ins)
    moved += sum(int(o.size) * o.dtype.itemsize for o in outs)
    size = size or max(o.shape[0] for o in outs)
    block = -(-size // (16 * steps)) * 16 if steps else 0

    def spec(x):
        if not steps:
            return VM
        if len(x.shape) == 2 and steps * block - 64 < x.shape[0] <= steps * block:
            return pl.BlockSpec((block, x.shape[1]), lambda s: (s, 0))
        return pl.BlockSpec(x.shape, lambda s: (0,) * len(x.shape))

    specs = [spec(x) for x in ins]
    if smem:
        specs[0] = SM
    got = pl.pallas_call(
        kernel,
        out_shape=list(outs),
        grid=(steps,) if steps else (),
        in_specs=specs,
        out_specs=[spec(o) for o in outs],
        scratch_shapes=list(scratch),
        compiler_params=pltpu.CompilerParams(vmem_limit_bytes=16 << 20),
        cost_estimate=pl.CostEstimate(flops=flops, bytes_accessed=moved, transcendentals=0),
        name=name,
    )(*ins)
    return got[0] if len(outs) == 1 else got


def after(v, *others):
    return lax.optimization_barrier((v, *others))[0]


def swap(v, axis, size, k):
    return lax.ppermute(v, axis, [(i, i ^ k) for i in range(size)])


def batch_sum(spread):
    return lax.all_to_all(spread, "batch", 0, 0)


def pair_kernel(a, b, out):
    out[0:1] = a[...]
    out[1:2] = b[...]


def sum_kernel(*refs):
    *terms, out = refs
    out[...] = sum(t[...] for t in terms)


def batch_sum_stepwise(v, size):
    shape = jax.ShapeDtypeStruct(v.shape, v.dtype)
    got = [swap(v, "batch", size, k) for k in range(2, size, 2)]
    v = call(sum_kernel, [shape], [v, *got], name="sum")
    both = jax.ShapeDtypeStruct((2, *v.shape[1:]), v.dtype)
    return call(pair_kernel, [both], [v, swap(v, "batch", size, 1)], name="pair")


def gather_chan(v, size):
    held = {0: v}
    bit = size // 2
    while bit:
        held.update({k | bit: swap(b, "chan", size, bit) for k, b in list(held.items())})
        bit //= 2
    return [held[k] for k in range(size)]


def send_both(dims, whole, got, orders, step, last=False):
    shape = list(whole.shape)
    shape[-2] >>= step if last else step + 2
    return call(
        functools.partial(send_both_kernel, step, last, orders),
        [jax.ShapeDtypeStruct(tuple(shape), BF16)] * (1 if last else 2),
        [dims, whole, *got[0], *got[1]], name="send_both", smem=True,
    )


def double_pair(dims, pair, new, bits):
    n, columns = new[0].shape
    return call(
        functools.partial(double_pair_kernel, bits),
        [jax.ShapeDtypeStruct((2 * n, columns), BF16)] * 2, [dims, *pair, *new],
        name="double_pair", smem=True,
    )


def finish(dims, pair, new, bits):
    n, columns = new[0].shape
    return call(
        functools.partial(finish_kernel, bits), [jax.ShapeDtypeStruct((4 * n, columns), F32)],
        [dims, *pair, *new], name="finish", smem=True,
    )


def add(a, b, dtype=BF16):
    return call(add_kernel, [jax.ShapeDtypeStruct(a.shape, dtype)], [a, b], name="add")


def shards(n_batch, n_chan, *args):
    (features, w_reduce, gain_one, shift_one, w_group, gain_two, shift_two, w_expand,
     gain_three, shift_three, cotangent, resolution, crop_count) = args
    slots, side, _, share = features.shape
    width = w_reduce.shape[1]
    group_width = w_group.shape[2]
    rows = slots * side * side
    unit = 16 * STEPS
    padded = -(-rows // unit) * unit
    line, wide = side * slots, (side + 2) * slots
    me = lax.axis_index("chan")
    others = range(n_chan)
    shape = jax.ShapeDtypeStruct
    acc = lambda n, c: pltpu.VMEM((n, 8, c), F32)
    tall = pltpu.VMEM(((side + 2) * wide, width), F32)
    mm = 2 * padded * share * width

    feats = features.transpose(1, 2, 0, 3).reshape(rows, share)
    ends = ((0, padded - rows), (0, 0))
    even = [k for k in others[2:] if k % 2 == 0]
    at = [lax.bitwise_and(me ^ k, n_chan - 2) * share for k in even]
    w_far = [lax.dynamic_slice_in_dim(w_reduce, o, 2 * share, 0) for o in at]
    own = jnp.pad(after(feats, *w_far), ends)
    w_far = [swap(w, "chan", n_chan, k) for k, w in zip(even, w_far)]
    beside = swap(own, "chan", n_chan, 1)

    dims = jnp.stack(
        [resolution[0], crop_count[0], me, lax.axis_index("batch"), jnp.int32(rows)]
    )
    row = lax.broadcasted_iota(jnp.int32, (padded, LANES), 0)
    crop, j, i = row % slots, (row // slots) % side, row // line
    live = ((crop < crop_count[0]) & (i < resolution[0]) & (j < resolution[0])).astype(F32)
    taps = call(
        taps_kernel, [shape((9, width, width), BF16)], [w_group.reshape(9, group_width, width)],
        flops=mm, name="taps",
    )
    line_of = lambda v: v.reshape(1, -1)
    gain_one, shift_one, gain_two, shift_two = map(
        line_of, (gain_one, shift_one, gain_two, shift_two)
    )

    parts = call(
        part_far_kernel, [shape((padded, width), BF16)] * len(even), [dims, own, beside, *w_far],
        flops=2 * len(even) * mm, name="part_far", steps=2, smem=True,
    )
    parts = parts if len(even) > 1 else [parts]
    got = call(
        rows_kernel, [shape((share, width), BF16)] * 2 * len(even),
        [dims, *[after(w, *parts) for w in w_far]], name="rows", smem=True,
    )
    rows_far, passed = got[: len(even)], got[len(even) :]
    got = [swap(p, "chan", n_chan, k) for k, p in zip(even, parts)]

    *picked, gain_c, shift_c, cot = call(
        pick_kernel,
        [shape((width, share), BF16)] * n_chan + [shape((share, width), BF16)] * 2
        + [shape((1, share), F32)] * 2 + [shape((padded, share), BF16)],
        [dims, after(w_expand, *parts), w_reduce, line_of(gain_three), line_of(shift_three),
         cotangent.transpose(1, 2, 0, 3).reshape(rows, -1)],
        flops=mm, name="pick", smem=True, steps=STEPS,
    )
    part = call(
        near_kernel, [shape((padded, width), F32)], [dims, after(own, *parts), beside, w_reduce],
        flops=2 * mm, name="near", steps=STEPS, smem=True,
    )
    w_cols = [picked[0], swap(after(picked[1], part), "chan", n_chan, 1)]
    w_rows = [picked[n_chan], swap(after(picked[n_chan + 1], part), "chan", n_chan, 1)]
    for row, pass_on in zip(rows_far, passed):
        w_rows += [row, swap(after(pass_on, part), "chan", n_chan, 1)]
    ready = (part, live, cot, taps, gain_c, shift_c, w_cols[1], *w_rows, *picked)
    got = [after(v, *ready) for v in got]
    w_cols += [swap(after(picked[k], *got), "chan", n_chan, k) for k in others[2:]]
    z, spread = call(
        far_kernel, [shape((padded, width), F32), shape((1, 3, width), F32)],
        [live, part, *got], [acc(3, width)], flops=mm, name="far", steps=STEPS,
    )
    got_one = batch_sum_stepwise(spread, n_batch)

    grouped, spread = call(
        functools.partial(conv_kernel, side, slots),
        [shape((padded, width), F32), shape((n_batch, 2, width), F32)],
        [live, z, got_one, gain_one, shift_one, taps], [tall, acc(2, width)],
        flops=18 * padded * width * width, name="conv",
    )
    got_two = batch_sum(after(spread, *w_cols))
    hidden_two = call(
        hidden_kernel, [shape((padded, width), BF16)],
        [live, grouped, got_one, got_two, gain_two, shift_two], flops=mm, name="hidden", steps=STEPS,
    )
    half = padded * 42 // 64 // 16 * 16
    own_first = after(own, hidden_two)[:half]
    first = gather_y(hidden_two, n_chan)
    beside_two = swap(hidden_two, "chan", n_chan, 1)
    slope_two = call(
        slope_kernel, [shape((padded, width), F32)],
        [live, grouped, got_one, got_two, gain_two, shift_two], flops=mm, name="slope_two", steps=STEPS,
    )
    slope_one = call(
        slope_kernel, [shape((padded, width), F32)],
        [live, z, got_one, got_one, gain_one, shift_one], flops=mm, name="slope_one", steps=STEPS,
    )
    part = call(
        expand_near_kernel, [shape((padded, share), F32)], [hidden_two, beside_two, *w_cols[:2]],
        flops=2 * mm, name="expand_near", steps=2,
    )
    first = {k: after(v, part, slope_one, slope_two, own_first, *w_cols) for k, v in first.items()}
    far_halves = [gather_y(after(own_first, *first.values()), n_chan)]
    first = gather_core(first, n_chan)
    hidden_all = [hidden_two, beside_two] + [first[k] for k in others if k > 1]
    expanded, spread = call(
        expand_far_kernel, [shape((padded, share), F32), shape((n_batch, 2, share), F32)],
        [live, part, *hidden_all[2:], *w_cols[2:]], [acc(2, share)],
        flops=(n_chan - 2) * mm, name="expand_far", steps=STEPS,
    )
    got_three = batch_sum(spread)
    d_pre, spread = call(
        third_kernel, [shape((padded, share), F32), shape((n_batch, 2, share), F32)],
        [live, expanded, got_one, got_three, gain_c, shift_c, own, cot], [acc(2, share)],
        flops=4 * mm, name="third", steps=STEPS,
    )
    totals_three = batch_sum(spread)
    top = n_chan - 1
    d_expanded, sent, sums_three = call(
        d_expanded_kernel,
        [shape((padded, share), BF16), shape((padded, width), BF16), shape((2, share), F32)],
        [live, expanded, d_pre, got_one, got_three, totals_three, gain_c]
        + [w_cols[top]],
        flops=2 * mm, name="d_expanded", steps=STEPS,
    )
    early = [0, 1]
    far_halves[0] = {k: after(v, d_expanded) for k, v in far_halves[0].items()}
    d_zero, d_near = call(
        back_expand_kernel, [shape((padded, width), F32), shape((padded, width), BF16)],
        [after(d_expanded, sent, *far_halves[0].values())] + [w_cols[k] for k in early], flops=2 * mm,
        name="back_expand", steps=2,
    )

    def part_sum(k, below):
        if k == top:
            return sent
        if k == 1:
            return d_near
        got, bit = [], 1
        while bit < below:
            got.append(swap(part_sum(k | bit, bit), "chan", n_chan, bit))
            bit *= 2
        if k == 0:
            return [d_zero, *got]
        return call(
            merge_kernel, [shape((padded, width), BF16)],
            [after(d_expanded, d_near), w_cols[k], *got], flops=mm, name="merge", steps=2,
        )

    far_sum = part_sum(n_chan // 2, n_chan // 2)
    terms = [d_zero]
    bit = 1
    while bit < n_chan:
        mine = far_sum if bit == n_chan // 2 else part_sum(bit, bit)
        terms.append(swap(mine, "chan", n_chan, bit))
        bit *= 2
    expand_part = call(
        expand_grad_kernel, [shape((n_chan, width, share), BF16)],
        [after(d_expanded, far_sum), *hidden_all], flops=n_chan * mm, name="expand_grad",
    )
    bits = n_batch.bit_length() - 1
    top = bits - 1
    orders = [list(range(top)), [1, 0, *range(2, top)]]
    halves = [0, 1]
    got = [[], []]
    for s in range(top):
        send = send_both(dims, expand_part, got, orders, s)
        new = [swap(send[h], "batch", n_batch, 1 << orders[h][s]) for h in halves]
        if s == 0:
            block_out = call(
                block_kernel, [shape((rows, share), BF16)],
                [live, after(expanded, send[0]), got_one, got_three, gain_c, shift_c, own],
                flops=2 * mm, name="block", steps=STEPS,
            )
            new = [after(v, block_out) for v in new]
        got = [got[h] + [new[h]] for h in halves]
    mine = send_both(dims, expand_part, got, orders, top, True)
    expand_other = swap(mine, "batch", n_batch, 1 << (bits - 1))
    far_halves[0] = gather_core({k: after(v, far_sum) for k, v in far_halves[0].items()}, n_chan)
    terms[0] = after(d_zero, *far_halves[0].values())
    far_halves.append(gather_y(after(own, terms[-1], mine)[half:], n_chan))
    d_two, spread = call(
        d_two_kernel, [shape((padded, width), F32), shape((n_batch, 2, width), F32)],
        [slope_two, grouped, got_one, got_two, *terms], [acc(2, width)], flops=mm, name="d_two", steps=STEPS,
    )
    totals_two = batch_sum(spread)
    d_grouped, d_one, spread, sums_two = call(
        functools.partial(conv_back_kernel, side, slots),
        [shape((padded, width), F32)] * 2 + [shape((n_batch, 2, width), F32), shape((2, width), F32)],
        [live, d_two, grouped, got_two, totals_two, gain_two, slope_one, z, got_one, taps],
        [tall, acc(2, width)], flops=18 * padded * width * width, name="conv_back",
    )
    parts = call(
        split_kernel, [shape(mine.shape[1:], BF16)] * n_chan,
        [mine, after(expand_other, d_one)], name="split",
    )
    far_halves[1] = {k: after(v, d_one) for k, v in far_halves[1].items()}
    totals_one = batch_sum(after(spread, *parts, *far_halves[1].values()))
    d_reduced, sums_one = call(
        d_reduced_kernel, [shape((padded, width), BF16), shape((2, width), F32)],
        [live, d_one, z, got_one, totals_one, gain_one], flops=mm, name="d_reduced", steps=STEPS,
    )
    far_halves[1] = gather_core(far_halves[1], n_chan)
    firsts, lasts = ([far_halves[h][k] for k in others[2:]] for h in range(2))
    tail, rest = call(
        reduce_grad_kernel,
        [shape((n_chan * share, width), BF16), shape((n_chan - 2, share, width), F32)],
        [dims, d_reduced, own, beside, *firsts], flops=n_chan * mm, name="reduce_grad", smem=True,
    )
    tail = call(
        reduce_grad_rest_kernel, [shape((n_chan * share, width), BF16)],
        [dims, d_reduced, tail, rest, *lasts], flops=mm, name="reduce_grad_rest", smem=True,
    )
    d_beside = swap(d_reduced, "chan", n_chan, 1)
    tail = after(tail, d_beside)
    piece_rows = padded // PIECES
    d_far = []

    def far_rows(at, *ready):
        piece = after(d_reduced, *ready)[at * piece_rows : (at + 1) * piece_rows]
        d_far.append(gather_y(piece, n_chan))
        return list(d_far[at].values())

    def pass_on(at, *ready):
        d_far[at] = gather_core({k: after(v, *ready) for k, v in d_far[at].items()}, n_chan)
        return list(d_far[at].values())

    got = [[], []]
    for s in range(top):
        send = send_both(dims, tail, got, orders, s)
        new = [swap(send[h], "batch", n_batch, 1 << orders[h][s]) for h in halves]
        ties = []
        if s == 0:
            cols = [parts[0]]
            cols += [swap(after(parts[k], send[0]), "chan", n_chan, k) for k in others if k]
            cols = call(
                arrange_kernel, [shape((mine.shape[1] // 2, n_chan * share), BF16)] * 2, [dims, *cols],
                name="arrange", smem=True,
            )
            far_rows(0, *cols)
            ties = cols
        elif s == 1:
            group_part = call(
                functools.partial(group_grad_kernel, side, slots, group_width),
                [shape((9 * group_width, width), BF16)],
                [live, z, got_one, gain_one, shift_one, after(d_grouped, send[0])],
                [tall], flops=mm, name="group_grad",
            )
            group_other = swap(group_part, "batch", n_batch, 1)
            ties = [group_part]
            others_cols = [
                swap(after(cols[h], send[0]), "batch", n_batch, 1 << orders[h][top - 1])
                for h in halves
            ]
        new = [after(v, *ties) for v in new]
        got = [got[i] + [new[i]] for i in range(2)]
    sums = send_both(dims, tail, got, orders, top, True)
    other = swap(sums, "batch", n_batch, 1 << top)
    others_cols = [after(v, sums) for v in others_cols]
    cols = double_pair(dims, cols, others_cols, [o[top - 1] for o in orders])
    for t in reversed(range(1, top - 1)):
        others_cols = [swap(cols[h], "batch", n_batch, 1 << orders[h][t]) for h in halves]
        cols = double_pair(dims, cols, others_cols, [o[t] for o in orders])
    group_part = add(group_part, after(group_other, *cols))
    others_cols = [
        swap(after(cols[h], sums), "batch", n_batch, 1 << orders[h][0]) for h in halves
    ]
    moved = [*far_rows(1, sums), *pass_on(0, sums)]
    part = call(
        features_grad_kernel, [shape((padded, share), F32)],
        [d_pre, after(d_reduced, group_part), d_beside, *w_rows[:2]], flops=2 * mm,
        name="input_near", steps=STEPS,
    )
    sums = add(sums, after(other, part))
    others_cols = [after(v, sums) for v in others_cols]
    moved = [after(v, sums) for v in moved]
    expand_grad = finish(dims, cols, others_cols, [o[0] for o in orders])
    pair = [sums]
    for s in reversed(range(top)):
        n = pair[0].shape[0] // (2 if len(pair) == 1 else 1)
        cut = [sums[:n], sums[n:]] if len(pair) == 1 else pair
        new = [swap(cut[i], "batch", n_batch, 1 << orders[i][s]) for i in range(2)]
        if s == top - 1:
            group_other = swap(after(group_part, sums), "batch", n_batch, 2)
            group_part = add(group_part, after(group_other, expand_grad))
            before = (group_part,)
        if s == 0:
            pass_on(1, cut[0])
            for t in range(2, bits):
                group_part = after(group_part, cut[0])
                group_other = swap(group_part, "batch", n_batch, 1 << t)
                if t == 2:
                    features_grad = call(
                        input_far_kernel, [shape((rows, share), F32)],
                        [after(part, cut[0]), *[d[k] for k in others[2:] for d in d_far], *w_rows[2:]],
                        flops=(n_chan - 2) * mm, name="input_far", steps=PIECES, size=padded,
                    )
                    group_other = after(group_other, features_grad)
                group_part = add(group_part, group_other, BF16 if t + 1 < bits else F32)
            before = (group_part,)
        new = [after(v, *before) for v in new]
        if s:
            pair = double_pair(dims, pair, new, [o[s] for o in orders])
    tail = finish(dims, pair, new, [o[0] for o in orders])
    reduce_grad, group_grad = tail, group_part

    shaped = lambda v: v.reshape(side, side, slots, share).transpose(2, 0, 1, 3)
    return (
        shaped(block_out),
        shaped(features_grad),
        reduce_grad,
        sums_one[1],
        sums_one[0],
        group_grad.reshape(3, 3, group_width, width),
        sums_two[1],
        sums_two[0],
        expand_grad,
        sums_three[1],
        sums_three[0],
    )


def gather_y(v, size):
    held = {0: v}
    bit = size // 2
    while bit > 1:
        held.update({k | bit: swap(b, "chan", size, bit) for k, b in list(held.items())})
        bit //= 2
    return {k: b for k, b in held.items() if k}


def gather_core(held, size):
    return held | {k | 1: swap(b, "chan", size, 1) for k, b in held.items()}


def solution(mesh):
    in_specs = (
        P("batch", None, None, "chan"),
        P(None, "chan"),
        P("chan"),
        P("chan"),
        P(None, None, None, "chan"),
        P("chan"),
        P("chan"),
        P("chan", None),
        P(),
        P(),
        P("batch", None, None, None),
        P("batch"),
        P("batch"),
    )
    out_specs = (
        P("batch", None, None, "chan"),
        P("batch", None, None, "chan"),
        P(None, "chan"),
        P("chan"),
        P("chan"),
        P(None, None, None, "chan"),
        P("chan"),
        P("chan"),
        P("chan", None),
        P("chan"),
        P("chan"),
    )
    n_batch, n_chan = mesh.shape["batch"], mesh.shape["chan"]

    def run(*args):
        return shards(n_batch, n_chan, *args)

    return jax.shard_map(run, mesh=mesh, in_specs=in_specs, out_specs=out_specs, check_vma=False)
```

```python
import functools

import jax
import jax.numpy as jnp
from jax import lax
from jax.experimental import pallas as pl
from jax.experimental.pallas import tpu as pltpu
from jax.sharding import PartitionSpec as P

EPSILON = 1e-05
ROOT = 0.7978845608028654
CUBE = 0.044715
F32 = jnp.float32
BF16 = jnp.bfloat16
STEP = 256
LANES = 128
LINES = 3
STEPS = 4
PIECES = 2
TN = (((0,), (0,)), ((), ()))
NT = (((1,), (1,)), ((), ()))
VM = pl.BlockSpec(memory_space=pltpu.VMEM)
SM = pl.BlockSpec(memory_space=pltpu.SMEM)


def dot(a, b):
    return jnp.dot(a, b, preferred_element_type=F32)


def dot_tn(a, b):
    return lax.dot_general(a, b, TN, preferred_element_type=F32)


def dot_nt(a, b):
    return lax.dot_general(a, b, NT, preferred_element_type=F32)


def bend(v):
    return jnp.tanh(v * (ROOT + (ROOT * CUBE) * (v * v)))


def act(v):
    half = 0.5 * v
    return half + half * bend(v)


def act_slope(v):
    t = bend(v)
    inner = v * (0.5 * ROOT + (1.5 * ROOT * CUBE) * (v * v))
    return 0.5 + 0.5 * t + inner * (1.0 - t * t)


def chunks(total, body, step=STEP):
    full = total // step

    def go(c, carry):
        body(pl.multiple_of(c * step, step), step)
        return carry

    if full:
        lax.fori_loop(0, full, go, 0)
    if total % step:
        body(full * step, total % step)


def fold(v):
    return jnp.sum(v.reshape(v.shape[0] // 8, 8, v.shape[1]), axis=0)


def widen(live, width):
    return jnp.concatenate([live] * (width // LANES), axis=1) if width > LANES else live


def norm_of(got, counts):
    s = jnp.sum(got[...], axis=0)
    share_of = 1.0 / jnp.sum(counts[...], axis=0)[2:3, 0:1]
    mu = s[0:1] * share_of
    return mu, lax.rsqrt(s[1:2] * share_of - mu * mu + EPSILON), share_of


def send_sums(out, acc):
    out[...] = jnp.broadcast_to(jnp.sum(acc[...], axis=1)[None], out.shape)


def start_sums(acc):
    @pl.when(pl.program_id(0) == 0)
    def _():
        acc[...] = jnp.zeros_like(acc)


def end_sums(out, acc):
    @pl.when(pl.program_id(0) == pl.num_programs(0) - 1)
    def _():
        send_sums(out, acc)


def near_kernel(dims, *refs):
    *feats, w, out = refs
    share = feats[0].shape[1]
    me = dims[2]
    ws = [w[pl.ds(pl.multiple_of((me ^ k) * share, share), share), :] for k in range(len(feats))]
    out[...] = sum(dot(f[...], wk) for f, wk in zip(feats, ws))


def part_far_kernel(dims, own, beside, *refs):
    n = len(refs) // 2
    share = own.shape[1]
    core = lax.bitwise_and(dims[2], 1)
    mine = pl.ds(pl.multiple_of(core * share, share), share)
    other = pl.ds(pl.multiple_of((1 - core) * share, share), share)
    for w, out in zip(refs[:n], refs[n:]):
        out[...] = (dot(own[...], w[mine, :]) + dot(beside[...], w[other, :])).astype(BF16)


def rows_kernel(dims, *refs):
    n = len(refs) // 3
    ws, rows, passed = (refs[i * n : (i + 1) * n] for i in range(3))
    share = rows[0].shape[0]
    core = lax.bitwise_and(dims[2], 1)
    for w, row, pass_on in zip(ws, rows, passed):
        row[...] = w[pl.ds(pl.multiple_of(core * share, share), share), :]
        pass_on[...] = w[pl.ds(pl.multiple_of((1 - core) * share, share), share), :]


def far_kernel(live, part, *refs):
    *got, out, spread, acc = refs
    start_sums(acc)
    z = part[...] + sum(g[...].astype(F32) for g in got)
    m = widen(live[...], z.shape[1])
    z = jnp.where(m > 0.0, z, 0.0)
    out[...] = z
    acc[0] += fold(z)
    acc[1] += fold(z * z)
    acc[2] += fold(m)
    end_sums(spread, acc)


def pad_edges(pad, side, line, wide, slots):
    width = pad.shape[1]
    pad[0:wide] = jnp.zeros((wide, width), F32)
    pad[(side + 1) * wide : (side + 2) * wide] = jnp.zeros((wide, width), F32)


def pad_line(pad, i, value, line, wide, slots):
    o = pl.multiple_of((i + 1) * wide, 8)
    edge = jnp.zeros((slots, pad.shape[1]), F32)
    pad[pl.ds(o, slots), :] = edge
    pad[pl.ds(o + slots, line), :] = value
    pad[pl.ds(o + slots + line, slots), :] = edge


def conv_lines(pad, first, count, taps, line, wide, slots, flip):
    total = None
    for t in range(9):
        a, b = divmod(t, 3)
        starts = [(first + i + a) * wide + b * slots for i in range(count)]
        x = jnp.concatenate([pad[o : o + line].astype(BF16) for o in starts], axis=0)
        d = dot_nt(x, taps[8 - t]) if flip else dot(x, taps[t])
        total = d if total is None else total + d
    return total


def taps_kernel(w, out):
    width, group_width = w.shape[2], w.shape[1]
    ids = [lax.broadcasted_iota(jnp.int32, (width, width), b) // group_width for b in range(2)]
    same = ids[0] == ids[1]
    for t in range(9):
        tiled = jnp.concatenate([w[t].astype(F32)] * (width // group_width), axis=0)
        out[t] = jnp.where(same, tiled, 0.0).astype(BF16)


def conv_kernel(side, slots, live, z, got, gain, shift, taps, out, spread, pad, acc):
    line, wide = side * slots, (side + 2) * slots
    rows, width = z.shape
    mu, r, _ = norm_of(got, got)
    a = r * gain[...]
    b = shift[...] - mu * a
    pad_edges(pad, side, line, wide, slots)
    acc[...] = jnp.zeros_like(acc)

    def fill(i, carry):
        here = pl.ds(pl.multiple_of(i * line, 8), line)
        h = widen(live[here, :], width) * act(z[here, :] * a + b)
        pad_line(pad, i, h.astype(BF16).astype(F32), line, wide, slots)
        return carry

    lax.fori_loop(0, side, fill, 0)

    for first in range(0, side, LINES):
        count = min(LINES, side - first)
        here = slice(first * line, (first + count) * line)
        total = conv_lines(pad, first, count, taps, line, wide, slots, False)
        out[here] = total
        m = widen(live[here], width) * total
        acc[0] += fold(m)
        acc[1] += fold(m * total)
    used = side * line
    out[used:rows] = jnp.zeros((rows - used, width), F32)
    send_sums(spread, acc)


def hidden_kernel(live, z, counts, got, gain, shift, out):
    mu, r, _ = norm_of(got, counts)
    a = r * gain[...]
    b = shift[...] - mu * a
    m = widen(live[...], z.shape[1])
    out[...] = (m * act(z[...] * a + b)).astype(BF16)


def slope_kernel(live, z, counts, got, gain, shift, out):
    mu, r, _ = norm_of(got, counts)
    a = r * gain[...]
    b = shift[...] - mu * a
    out[...] = widen(live[...], z.shape[1]) * act_slope(z[...] * a + b)


def expand_near_kernel(*refs):
    *ins, out = refs
    k = len(ins) // 2
    out[...] = sum(dot(h[...], w[...]) for h, w in zip(ins[:k], ins[k:]))


def expand_far_kernel(live, part, *refs):
    *ins, out, spread, acc = refs
    k = len(ins) // 2
    start_sums(acc)
    e = part[...] + sum(dot(h[...], w[...]) for h, w in zip(ins[:k], ins[k:]))
    out[...] = e
    m = widen(live[...], e.shape[1]) * e
    acc[0] += fold(m)
    acc[1] += fold(m * e)
    end_sums(spread, acc)


def third_kernel(live, e, counts, got, gain, shift, feats, cot, d_pre, spread, acc):
    mu, r, _ = norm_of(got, counts)
    start_sums(acc)
    zhat = (e[...] - mu) * r
    v = zhat * gain[...] + shift[...] + feats[...].astype(F32)
    m = widen(live[...], v.shape[1])
    d = m * cot[...].astype(F32) * act_slope(v)
    d_pre[...] = d
    acc[0] += fold(d)
    acc[1] += fold(d * zhat)
    end_sums(spread, acc)


def block_kernel(live, e, counts, got, gain, shift, feats, out):
    mu, r, _ = norm_of(got, counts)
    v = (e[...] - mu) * r * gain[...] + shift[...] + feats[...].astype(F32)
    out[...] = (widen(live[...], v.shape[1]) * act(v)).astype(BF16)


def d_expanded_kernel(live, e, d_pre, counts, got, totals, gain, w, d_exp, out, sums):
    mu, r, share_of = norm_of(got, counts)
    t = jnp.sum(totals[...], axis=0)
    sums[...] = t
    t = t * share_of
    scale = r * gain[...]
    zhat = (e[...] - mu) * r
    m = widen(live[...], zhat.shape[1])
    d = (m * scale * (d_pre[...] - t[0:1] - zhat * t[1:2])).astype(BF16)
    d_exp[...] = d
    out[...] = dot_nt(d, w[...]).astype(BF16)


def back_expand_kernel(d_exp, *refs):
    k = len(refs) // 2
    for w, out in zip(refs[:k], refs[k:]):
        out[...] = dot_nt(d_exp[...], w[...]).astype(out.dtype)


def merge_kernel(d_exp, w, *refs):
    *got, out = refs
    total = dot_nt(d_exp[...], w[...]) + sum(g[...].astype(F32) for g in got)
    out[...] = total.astype(BF16)


def expand_grad_kernel(d_exp, *refs):
    *hs, out = refs
    for k, h in enumerate(hs):
        out[k] = dot_tn(h[...], d_exp[...]).astype(BF16)


def d_two_kernel(slope, z, counts, got, *refs):
    *terms, d_out, spread, acc = refs
    mu, r, _ = norm_of(got, counts)
    start_sums(acc)
    d = sum(t[...].astype(F32) for t in terms) * slope[...]
    d_out[...] = d
    acc[0] += fold(d)
    acc[1] += fold(d * ((z[...] - mu) * r))
    end_sums(spread, acc)


def conv_back_kernel(
    side, slots, live, d_two, grouped, got_two, totals, gain, slope, z, got, taps,
    d_grouped, d_one, spread, sums, pad, acc,
):
    line, wide = side * slots, (side + 2) * slots
    rows, width = z.shape
    mu_two, r_two, share_of = norm_of(got_two, got)
    mu, r, _ = norm_of(got, got)
    t = jnp.sum(totals[...], axis=0)
    sums[...] = t
    t = t * share_of
    scale = r_two * gain[...]
    pad_edges(pad, side, line, wide, slots)
    acc[...] = jnp.zeros_like(acc)

    def fill(i, carry):
        here = pl.ds(pl.multiple_of(i * line, 8), line)
        zhat = (grouped[here, :] - mu_two) * r_two
        m = widen(live[here, :], width)
        d = m * scale * (d_two[here, :] - t[0:1] - zhat * t[1:2])
        d = d.astype(BF16).astype(F32)
        d_grouped[here, :] = d
        pad_line(pad, i, d, line, wide, slots)
        return carry

    lax.fori_loop(0, side, fill, 0)

    for first in range(0, side, LINES):
        count = min(LINES, side - first)
        here = slice(first * line, (first + count) * line)
        d = conv_lines(pad, first, count, taps, line, wide, slots, True) * slope[here]
        d_one[here] = d
        acc[0] += fold(d)
        acc[1] += fold(d * ((z[here] - mu) * r))
    used = side * line
    d_one[used:rows] = jnp.zeros((rows - used, width), F32)
    d_grouped[used:rows] = jnp.zeros((rows - used, width), F32)
    send_sums(spread, acc)


def d_reduced_kernel(live, d_one, z, got, totals, gain, out, sums):
    mu, r, share_of = norm_of(got, got)
    t = jnp.sum(totals[...], axis=0)
    sums[...] = t
    t = t * share_of
    zhat = (z[...] - mu) * r
    m = widen(live[...], zhat.shape[1])
    out[...] = (m * (r * gain[...]) * (d_one[...] - t[0:1] - zhat * t[1:2])).astype(BF16)


def group_grad_kernel(side, slots, group_width, live, z, got, gain, shift, d_grouped, out, pad):
    line, wide = side * slots, (side + 2) * slots
    width = z.shape[1]
    mu, r, _ = norm_of(got, got)
    scale = r * gain[...]
    offset = shift[...] - mu * scale
    pad_edges(pad, side, line, wide, slots)

    def fill(i, carry):
        here = pl.ds(pl.multiple_of(i * line, 8), line)
        h = widen(live[here, :], width) * act(z[here, :] * scale + offset)
        pad_line(pad, i, h.astype(BF16).astype(F32), line, wide, slots)
        return carry

    lax.fori_loop(0, side, fill, 0)
    d = d_grouped[0 : side * line].astype(BF16)
    ids = [lax.broadcasted_iota(jnp.int32, (width, width), b) // group_width for b in range(2)]
    same = ids[0] == ids[1]
    for t in range(9):
        a, b = divmod(t, 3)
        starts = [(i + a) * wide + b * slots for i in range(side)]
        x = jnp.concatenate([pad[o : o + line].astype(BF16) for o in starts], axis=0)
        dense = jnp.where(same, dot_tn(x, d), 0.0)
        picked = jnp.sum(dense.reshape(width // group_width, group_width, width), axis=0)
        out[t * group_width : (t + 1) * group_width] = picked.astype(BF16)


def reduce_grad_kernel(dims, d_red, *refs):
    *feats, out, rest = refs
    share = feats[0].shape[1]
    me = dims[2]
    for k in range(2):
        rows = pl.ds(pl.multiple_of((me ^ k) * share, share), share)
        out[rows, :] = dot_tn(feats[k][...], d_red[...]).astype(BF16)
    for k, f in enumerate(feats[2:]):
        rest[k] = dot_tn(f[...], d_red[0 : f.shape[0]])


def reduce_grad_rest_kernel(dims, d_red, near, rest, *refs):
    *feats, out = refs
    share = feats[0].shape[1]
    me = dims[2]
    for k in range(2):
        rows = pl.ds(pl.multiple_of((me ^ k) * share, share), share)
        out[rows, :] = near[rows, :]
    for k, f in enumerate(feats):
        rows = pl.ds(pl.multiple_of((me ^ (k + 2)) * share, share), share)
        first = d_red.shape[0] - f.shape[0]
        out[rows, :] = (rest[k] + dot_tn(f[...], d_red[first:])).astype(BF16)


def features_grad_kernel(part, *refs):
    *ins, out = refs
    k = len(ins) // 2
    out[...] = part[...] + sum(dot_nt(d[...], w[...]) for d, w in zip(ins[:k], ins[k:]))


def pick_kernel(dims, w_expand, w_reduce, gain, shift, cot, *outs):
    me = dims[2]
    n = len(outs) - 5
    cols, rows, rest = outs[:n], outs[n : n + 2], outs[n + 2 :]
    share = rows[0].shape[0]

    @pl.when(pl.program_id(0) == 0)
    def _():
        for k in range(n):
            at = pl.ds(pl.multiple_of((me ^ k) * share, share), share)
            cols[k][...] = w_expand[:, at]
            if k < 2:
                rows[k][...] = w_reduce[at, :]
        at = pl.ds(pl.multiple_of(me * share, share), share)
        rest[0][...] = gain[:, at]
        rest[1][...] = shift[:, at]

    at = pl.ds(pl.multiple_of(me * share, share), share)
    first = pl.program_id(0) * cot.shape[0]
    row = lax.broadcasted_iota(jnp.int32, (cot.shape[0], share), 0) + first
    rest[2][...] = jnp.where(row < dims[4], cot[:, at].astype(F32), 0.0).astype(BF16)


def bit_of(v, bit):
    return lax.bitwise_and(lax.shift_right_logical(v, bit), 1)


def add_terms(b, terms, order, step, last, base):
    total = None
    for first, (term, size) in enumerate(terms):
        rows, at = size, base if first == 0 else 0
        for t in range(first, step + (not last)):
            rows //= 2
            side = bit_of(b, order[t])
            at += rows * (side if t < step else 1 - side)
        here = pl.ds(at if isinstance(at, int) else pl.multiple_of(at, min(rows, 16)), rows)
        v = term[:, here, :] if len(term.shape) == 3 else term[here, :]
        total = v.astype(F32) if total is None else total + v.astype(F32)
    return total.astype(BF16)


def send_both_kernel(step, last, orders, dims, whole, *refs):
    half = whole.shape[-2] // 2
    n = step
    outs = refs[2 * n :]
    for i, order in enumerate(orders):
        terms = [(whole, half)] + [(r, r.shape[-2]) for r in refs[i * n : (i + 1) * n]]
        total = add_terms(dims[3], terms, order, step, last, i * half)
        rows = total.shape[-2]
        if last and len(whole.shape) == 3:
            outs[0][:, i * rows : (i + 1) * rows, :] = total
        elif last:
            outs[0][i * rows : (i + 1) * rows] = total
        else:
            outs[i][...] = total


def double_pair_kernel(bits, dims, sums, *refs):
    *ins, a, b = refs
    n = ins[0].shape[0]
    for i, (bit, out) in enumerate(zip(bits, (a, b))):
        mine = sums[i * n : (i + 1) * n] if len(ins) == 2 else (sums, ins[0])[i][...]
        other = ins[i] if len(ins) == 2 else ins[i + 1]
        upper = bit_of(dims[3], bit)
        out[pl.ds(pl.multiple_of(upper * n, min(n, 16)), n), :] = mine
        out[pl.ds(pl.multiple_of((1 - upper) * n, min(n, 16)), n), :] = other[...]


def finish_kernel(bits, dims, a, b, other_a, other_b, out):
    n = a.shape[0]
    for i, (bit, mine, other) in enumerate(zip(bits, (a, b), (other_a, other_b))):
        upper = bit_of(dims[3], bit)
        at = 2 * i * n
        out[pl.ds(pl.multiple_of(at + upper * n, min(n, 16)), n), :] = mine[...].astype(F32)
        out[pl.ds(pl.multiple_of(at + (1 - upper) * n, min(n, 16)), n), :] = other[...].astype(F32)


def arrange_kernel(dims, *refs):
    *cols, a, b = refs
    n, share = a.shape[0], cols[0].shape[1]
    for k, c in enumerate(cols):
        at = pl.ds(pl.multiple_of((dims[2] ^ k) * share, share), share)
        a[:, at] = c[0:n]
        b[:, at] = c[n:]


def split_kernel(a, b, *outs):
    for k, out in enumerate(outs):
        out[...] = (a[k].astype(F32) + b[k].astype(F32)).astype(BF16)


def add_kernel(a, b, out):
    out[...] = (a[...].astype(F32) + b[...].astype(F32)).astype(out.dtype)


def input_far_kernel(part, *refs):
    *ins, out = refs
    n = len(ins) // (PIECES + 1)
    ds, ws = ins[: n * PIECES], ins[n * PIECES :]
    for step in range(PIECES):

        @pl.when(pl.program_id(0) == step)
        def _(step=step):
            got = sum(dot_nt(ds[k * PIECES + step][...], w[...]) for k, w in enumerate(ws))
            out[...] = part[...] + got


def call(kernel, outs, ins, scratch=(), flops=0, name=None, smem=False, steps=0, size=0):
    moved = sum(x.size * x.dtype.itemsize for x in ins)
    moved += sum(int(o.size) * o.dtype.itemsize for o in outs)
    size = size or max(o.shape[0] for o in outs)
    block = -(-size // (16 * steps)) * 16 if steps else 0

    def spec(x):
        if not steps:
            return VM
        if len(x.shape) == 2 and steps * block - 64 < x.shape[0] <= steps * block:
            return pl.BlockSpec((block, x.shape[1]), lambda s: (s, 0))
        return pl.BlockSpec(x.shape, lambda s: (0,) * len(x.shape))

    specs = [spec(x) for x in ins]
    if smem:
        specs[0] = SM
    got = pl.pallas_call(
        kernel,
        out_shape=list(outs),
        grid=(steps,) if steps else (),
        in_specs=specs,
        out_specs=[spec(o) for o in outs],
        scratch_shapes=list(scratch),
        compiler_params=pltpu.CompilerParams(vmem_limit_bytes=16 << 20),
        cost_estimate=pl.CostEstimate(flops=flops, bytes_accessed=moved, transcendentals=0),
        name=name,
    )(*ins)
    return got[0] if len(outs) == 1 else got


def after(v, *others):
    return lax.optimization_barrier((v, *others))[0]


def swap(v, axis, size, k):
    return lax.ppermute(v, axis, [(i, i ^ k) for i in range(size)])


def batch_sum(spread):
    return lax.all_to_all(spread, "batch", 0, 0)


def pair_kernel(a, b, out):
    out[0:1] = a[...]
    out[1:2] = b[...]


def sum_kernel(*refs):
    *terms, out = refs
    out[...] = sum(t[...] for t in terms)


def batch_sum_stepwise(v, size):
    shape = jax.ShapeDtypeStruct(v.shape, v.dtype)
    got = [swap(v, "batch", size, k) for k in range(2, size, 2)]
    v = call(sum_kernel, [shape], [v, *got], name="sum")
    both = jax.ShapeDtypeStruct((2, *v.shape[1:]), v.dtype)
    return call(pair_kernel, [both], [v, swap(v, "batch", size, 1)], name="pair")


def gather_chan(v, size):
    held = {0: v}
    bit = size // 2
    while bit:
        held.update({k | bit: swap(b, "chan", size, bit) for k, b in list(held.items())})
        bit //= 2
    return [held[k] for k in range(size)]


def send_both(dims, whole, got, orders, step, last=False):
    shape = list(whole.shape)
    shape[-2] >>= step if last else step + 2
    return call(
        functools.partial(send_both_kernel, step, last, orders),
        [jax.ShapeDtypeStruct(tuple(shape), BF16)] * (1 if last else 2),
        [dims, whole, *got[0], *got[1]], name="send_both", smem=True,
    )


def double_pair(dims, pair, new, bits):
    n, columns = new[0].shape
    return call(
        functools.partial(double_pair_kernel, bits),
        [jax.ShapeDtypeStruct((2 * n, columns), BF16)] * 2, [dims, *pair, *new],
        name="double_pair", smem=True,
    )


def finish(dims, pair, new, bits):
    n, columns = new[0].shape
    return call(
        functools.partial(finish_kernel, bits), [jax.ShapeDtypeStruct((4 * n, columns), F32)],
        [dims, *pair, *new], name="finish", smem=True,
    )


def add(a, b, dtype=BF16):
    return call(add_kernel, [jax.ShapeDtypeStruct(a.shape, dtype)], [a, b], name="add")


def shards(n_batch, n_chan, *args):
    (features, w_reduce, gain_one, shift_one, w_group, gain_two, shift_two, w_expand,
     gain_three, shift_three, cotangent, resolution, crop_count) = args
    slots, side, _, share = features.shape
    width = w_reduce.shape[1]
    group_width = w_group.shape[2]
    rows = slots * side * side
    unit = 16 * STEPS
    padded = -(-rows // unit) * unit
    line, wide = side * slots, (side + 2) * slots
    me = lax.axis_index("chan")
    others = range(n_chan)
    shape = jax.ShapeDtypeStruct
    acc = lambda n, c: pltpu.VMEM((n, 8, c), F32)
    tall = pltpu.VMEM(((side + 2) * wide, width), F32)
    mm = 2 * padded * share * width

    feats = features.transpose(1, 2, 0, 3).reshape(rows, share)
    ends = ((0, padded - rows), (0, 0))
    even = [k for k in others[2:] if k % 2 == 0]
    at = [lax.bitwise_and(me ^ k, n_chan - 2) * share for k in even]
    w_far = [lax.dynamic_slice_in_dim(w_reduce, o, 2 * share, 0) for o in at]
    own = jnp.pad(after(feats, *w_far), ends)
    w_far = [swap(w, "chan", n_chan, k) for k, w in zip(even, w_far)]
    beside = swap(own, "chan", n_chan, 1)

    dims = jnp.stack(
        [resolution[0], crop_count[0], me, lax.axis_index("batch"), jnp.int32(rows)]
    )
    row = lax.broadcasted_iota(jnp.int32, (padded, LANES), 0)
    crop, j, i = row % slots, (row // slots) % side, row // line
    live = ((crop < crop_count[0]) & (i < resolution[0]) & (j < resolution[0])).astype(F32)
    taps = call(
        taps_kernel, [shape((9, width, width), BF16)], [w_group.reshape(9, group_width, width)],
        flops=mm, name="taps",
    )
    line_of = lambda v: v.reshape(1, -1)
    gain_one, shift_one, gain_two, shift_two = map(
        line_of, (gain_one, shift_one, gain_two, shift_two)
    )

    parts = call(
        part_far_kernel, [shape((padded, width), BF16)] * len(even), [dims, own, beside, *w_far],
        flops=2 * len(even) * mm, name="part_far", steps=2, smem=True,
    )
    parts = parts if len(even) > 1 else [parts]
    got = call(
        rows_kernel, [shape((share, width), BF16)] * 2 * len(even),
        [dims, *[after(w, *parts) for w in w_far]], name="rows", smem=True,
    )
    rows_far, passed = got[: len(even)], got[len(even) :]
    got = [swap(p, "chan", n_chan, k) for k, p in zip(even, parts)]

    *picked, gain_c, shift_c, cot = call(
        pick_kernel,
        [shape((width, share), BF16)] * n_chan + [shape((share, width), BF16)] * 2
        + [shape((1, share), F32)] * 2 + [shape((padded, share), BF16)],
        [dims, after(w_expand, *parts), w_reduce, line_of(gain_three), line_of(shift_three),
         cotangent.transpose(1, 2, 0, 3).reshape(rows, -1)],
        flops=mm, name="pick", smem=True, steps=STEPS,
    )
    part = call(
        near_kernel, [shape((padded, width), F32)], [dims, after(own, *parts), beside, w_reduce],
        flops=2 * mm, name="near", steps=STEPS, smem=True,
    )
    w_cols = [picked[0], swap(after(picked[1], part), "chan", n_chan, 1)]
    w_rows = [picked[n_chan], swap(after(picked[n_chan + 1], part), "chan", n_chan, 1)]
    for row, pass_on in zip(rows_far, passed):
        w_rows += [row, swap(after(pass_on, part), "chan", n_chan, 1)]
    ready = (part, live, cot, taps, gain_c, shift_c, w_cols[1], *w_rows, *picked)
    got = [after(v, *ready) for v in got]
    w_cols += [swap(after(picked[k], *got), "chan", n_chan, k) for k in others[2:]]
    z, spread = call(
        far_kernel, [shape((padded, width), F32), shape((1, 3, width), F32)],
        [live, part, *got], [acc(3, width)], flops=mm, name="far", steps=STEPS,
    )
    got_one = batch_sum_stepwise(spread, n_batch)

    grouped, spread = call(
        functools.partial(conv_kernel, side, slots),
        [shape((padded, width), F32), shape((n_batch, 2, width), F32)],
        [live, z, got_one, gain_one, shift_one, taps], [tall, acc(2, width)],
        flops=18 * padded * width * width, name="conv",
    )
    got_two = batch_sum(after(spread, *w_cols))
    hidden_two = call(
        hidden_kernel, [shape((padded, width), BF16)],
        [live, grouped, got_one, got_two, gain_two, shift_two], flops=mm, name="hidden", steps=STEPS,
    )
    half = padded * 42 // 64 // 16 * 16
    own_first = after(own, hidden_two)[:half]
    first = gather_y(hidden_two, n_chan)
    beside_two = swap(hidden_two, "chan", n_chan, 1)
    slope_two = call(
        slope_kernel, [shape((padded, width), F32)],
        [live, grouped, got_one, got_two, gain_two, shift_two], flops=mm, name="slope_two", steps=STEPS,
    )
    slope_one = call(
        slope_kernel, [shape((padded, width), F32)],
        [live, z, got_one, got_one, gain_one, shift_one], flops=mm, name="slope_one", steps=STEPS,
    )
    part = call(
        expand_near_kernel, [shape((padded, share), F32)], [hidden_two, beside_two, *w_cols[:2]],
        flops=2 * mm, name="expand_near", steps=2,
    )
    first = {k: after(v, part, slope_one, slope_two, own_first, *w_cols) for k, v in first.items()}
    far_halves = [gather_y(after(own_first, *first.values()), n_chan)]
    first = gather_core(first, n_chan)
    hidden_all = [hidden_two, beside_two] + [first[k] for k in others if k > 1]
    expanded, spread = call(
        expand_far_kernel, [shape((padded, share), F32), shape((n_batch, 2, share), F32)],
        [live, part, *hidden_all[2:], *w_cols[2:]], [acc(2, share)],
        flops=(n_chan - 2) * mm, name="expand_far", steps=STEPS,
    )
    got_three = batch_sum(spread)
    d_pre, spread = call(
        third_kernel, [shape((padded, share), F32), shape((n_batch, 2, share), F32)],
        [live, expanded, got_one, got_three, gain_c, shift_c, own, cot], [acc(2, share)],
        flops=4 * mm, name="third", steps=STEPS,
    )
    totals_three = batch_sum(spread)
    top = n_chan - 1
    d_expanded, sent, sums_three = call(
        d_expanded_kernel,
        [shape((padded, share), BF16), shape((padded, width), BF16), shape((2, share), F32)],
        [live, expanded, d_pre, got_one, got_three, totals_three, gain_c]
        + [w_cols[top]],
        flops=2 * mm, name="d_expanded", steps=STEPS,
    )
    early = [0, 1]
    far_halves[0] = {k: after(v, d_expanded) for k, v in far_halves[0].items()}
    d_zero, d_near = call(
        back_expand_kernel, [shape((padded, width), F32), shape((padded, width), BF16)],
        [after(d_expanded, sent, *far_halves[0].values())] + [w_cols[k] for k in early], flops=2 * mm,
        name="back_expand", steps=2,
    )

    def part_sum(k, below):
        if k == top:
            return sent
        if k == 1:
            return d_near
        got, bit = [], 1
        while bit < below:
            got.append(swap(part_sum(k | bit, bit), "chan", n_chan, bit))
            bit *= 2
        if k == 0:
            return [d_zero, *got]
        return call(
            merge_kernel, [shape((padded, width), BF16)],
            [after(d_expanded, d_near), w_cols[k], *got], flops=mm, name="merge", steps=2,
        )

    far_sum = part_sum(n_chan // 2, n_chan // 2)
    terms = [d_zero]
    bit = 1
    while bit < n_chan:
        mine = far_sum if bit == n_chan // 2 else part_sum(bit, bit)
        terms.append(swap(mine, "chan", n_chan, bit))
        bit *= 2
    expand_part = call(
        expand_grad_kernel, [shape((n_chan, width, share), BF16)],
        [after(d_expanded, far_sum), *hidden_all], flops=n_chan * mm, name="expand_grad",
    )
    bits = n_batch.bit_length() - 1
    top = bits - 1
    orders = [list(range(top)), [1, 0, *range(2, top)]]
    halves = [0, 1]
    got = [[], []]
    for s in range(top):
        send = send_both(dims, expand_part, got, orders, s)
        new = [swap(send[h], "batch", n_batch, 1 << orders[h][s]) for h in halves]
        if s == 0:
            block_out = call(
                block_kernel, [shape((rows, share), BF16)],
                [live, after(expanded, send[0]), got_one, got_three, gain_c, shift_c, own],
                flops=2 * mm, name="block", steps=STEPS,
            )
            new = [after(v, block_out) for v in new]
        got = [got[h] + [new[h]] for h in halves]
    mine = send_both(dims, expand_part, got, orders, top, True)
    expand_other = swap(mine, "batch", n_batch, 1 << (bits - 1))
    far_halves[0] = gather_core({k: after(v, far_sum) for k, v in far_halves[0].items()}, n_chan)
    terms[0] = after(d_zero, *far_halves[0].values())
    far_halves.append(gather_y(after(own, terms[-1], mine)[half:], n_chan))
    d_two, spread = call(
        d_two_kernel, [shape((padded, width), F32), shape((n_batch, 2, width), F32)],
        [slope_two, grouped, got_one, got_two, *terms], [acc(2, width)], flops=mm, name="d_two", steps=STEPS,
    )
    totals_two = batch_sum(spread)
    d_grouped, d_one, spread, sums_two = call(
        functools.partial(conv_back_kernel, side, slots),
        [shape((padded, width), F32)] * 2 + [shape((n_batch, 2, width), F32), shape((2, width), F32)],
        [live, d_two, grouped, got_two, totals_two, gain_two, slope_one, z, got_one, taps],
        [tall, acc(2, width)], flops=18 * padded * width * width, name="conv_back",
    )
    parts = call(
        split_kernel, [shape(mine.shape[1:], BF16)] * n_chan,
        [mine, after(expand_other, d_one)], name="split",
    )
    far_halves[1] = {k: after(v, d_one) for k, v in far_halves[1].items()}
    totals_one = batch_sum(after(spread, *parts, *far_halves[1].values()))
    d_reduced, sums_one = call(
        d_reduced_kernel, [shape((padded, width), BF16), shape((2, width), F32)],
        [live, d_one, z, got_one, totals_one, gain_one], flops=mm, name="d_reduced", steps=STEPS,
    )
    far_halves[1] = gather_core(far_halves[1], n_chan)
    firsts, lasts = ([far_halves[h][k] for k in others[2:]] for h in range(2))
    tail, rest = call(
        reduce_grad_kernel,
        [shape((n_chan * share, width), BF16), shape((n_chan - 2, share, width), F32)],
        [dims, d_reduced, own, beside, *firsts], flops=n_chan * mm, name="reduce_grad", smem=True,
    )
    tail = call(
        reduce_grad_rest_kernel, [shape((n_chan * share, width), BF16)],
        [dims, d_reduced, tail, rest, *lasts], flops=mm, name="reduce_grad_rest", smem=True,
    )
    d_beside = swap(d_reduced, "chan", n_chan, 1)
    tail = after(tail, d_beside)
    piece_rows = padded // PIECES
    d_far = []

    def far_rows(at, *ready):
        piece = after(d_reduced, *ready)[at * piece_rows : (at + 1) * piece_rows]
        d_far.append(gather_y(piece, n_chan))
        return list(d_far[at].values())

    def pass_on(at, *ready):
        d_far[at] = gather_core({k: after(v, *ready) for k, v in d_far[at].items()}, n_chan)
        return list(d_far[at].values())

    got = [[], []]
    for s in range(top):
        send = send_both(dims, tail, got, orders, s)
        new = [swap(send[h], "batch", n_batch, 1 << orders[h][s]) for h in halves]
        ties = []
        if s == 0:
            cols = [parts[0]]
            cols += [swap(after(parts[k], send[0]), "chan", n_chan, k) for k in others if k]
            cols = call(
                arrange_kernel, [shape((mine.shape[1] // 2, n_chan * share), BF16)] * 2, [dims, *cols],
                name="arrange", smem=True,
            )
            far_rows(0, *cols)
            ties = cols
        elif s == 1:
            others_cols = [
                swap(after(cols[h], send[0]), "batch", n_batch, 1 << orders[h][top - 1])
                for h in halves
            ]
        new = [after(v, *ties) for v in new]
        got = [got[i] + [new[i]] for i in range(2)]
    sums = send_both(dims, tail, got, orders, top, True)
    other = swap(sums, "batch", n_batch, 1 << top)
    others_cols = [after(v, sums) for v in others_cols]
    cols = double_pair(dims, cols, others_cols, [o[top - 1] for o in orders])
    for t in reversed(range(1, top - 1)):
        others_cols = [swap(cols[h], "batch", n_batch, 1 << orders[h][t]) for h in halves]
        cols = double_pair(dims, cols, others_cols, [o[t] for o in orders])
    group_part = call(
        functools.partial(group_grad_kernel, side, slots, group_width),
        [shape((9 * group_width, width), BF16)],
        [live, z, got_one, gain_one, shift_one, after(d_grouped, *cols)],
        [tall], flops=mm, name="group_grad",
    )
    group_other = swap(group_part, "batch", n_batch, 1)
    others_cols = [
        swap(after(cols[h], sums), "batch", n_batch, 1 << orders[h][0]) for h in halves
    ]
    moved = [*far_rows(1, sums), *pass_on(0, sums)]
    part = call(
        features_grad_kernel, [shape((padded, share), F32)],
        [d_pre, after(d_reduced, group_part), d_beside, *w_rows[:2]], flops=2 * mm,
        name="input_near", steps=STEPS,
    )
    sums = add(sums, after(other, part))
    group_part = add(group_part, after(group_other, sums))
    others_cols = [after(v, sums) for v in others_cols]
    moved = [after(v, sums) for v in moved]
    expand_grad = finish(dims, cols, others_cols, [o[0] for o in orders])
    pair = [sums]
    for s in reversed(range(top)):
        n = pair[0].shape[0] // (2 if len(pair) == 1 else 1)
        cut = [sums[:n], sums[n:]] if len(pair) == 1 else pair
        new = [swap(cut[i], "batch", n_batch, 1 << orders[i][s]) for i in range(2)]
        if s == top - 1:
            group_other = swap(after(group_part, sums), "batch", n_batch, 2)
            group_part = add(group_part, after(group_other, expand_grad))
            before = (group_part,)
        if s == 0:
            pass_on(1, cut[0])
            for t in range(2, bits):
                group_part = after(group_part, cut[0])
                group_other = swap(group_part, "batch", n_batch, 1 << t)
                if t == 2:
                    features_grad = call(
                        input_far_kernel, [shape((rows, share), F32)],
                        [after(part, cut[0]), *[d[k] for k in others[2:] for d in d_far], *w_rows[2:]],
                        flops=(n_chan - 2) * mm, name="input_far", steps=PIECES, size=padded,
                    )
                    group_other = after(group_other, features_grad)
                group_part = add(group_part, group_other, BF16 if t + 1 < bits else F32)
            before = (group_part,)
        new = [after(v, *before) for v in new]
        if s:
            pair = double_pair(dims, pair, new, [o[s] for o in orders])
    tail = finish(dims, pair, new, [o[0] for o in orders])
    reduce_grad, group_grad = tail, group_part

    shaped = lambda v: v.reshape(side, side, slots, share).transpose(2, 0, 1, 3)
    return (
        shaped(block_out),
        shaped(features_grad),
        reduce_grad,
        sums_one[1],
        sums_one[0],
        group_grad.reshape(3, 3, group_width, width),
        sums_two[1],
        sums_two[0],
        expand_grad,
        sums_three[1],
        sums_three[0],
    )


def gather_y(v, size):
    held = {0: v}
    bit = size // 2
    while bit > 1:
        held.update({k | bit: swap(b, "chan", size, bit) for k, b in list(held.items())})
        bit //= 2
    return {k: b for k, b in held.items() if k}


def gather_core(held, size):
    return held | {k | 1: swap(b, "chan", size, 1) for k, b in held.items()}


def solution(mesh):
    in_specs = (
        P("batch", None, None, "chan"),
        P(None, "chan"),
        P("chan"),
        P("chan"),
        P(None, None, None, "chan"),
        P("chan"),
        P("chan"),
        P("chan", None),
        P(),
        P(),
        P("batch", None, None, None),
        P("batch"),
        P("batch"),
    )
    out_specs = (
        P("batch", None, None, "chan"),
        P("batch", None, None, "chan"),
        P(None, "chan"),
        P("chan"),
        P("chan"),
        P(None, None, None, "chan"),
        P("chan"),
        P("chan"),
        P("chan", None),
        P("chan"),
        P("chan"),
    )
    n_batch, n_chan = mesh.shape["batch"], mesh.shape["chan"]

    def run(*args):
        return shards(n_batch, n_chan, *args)

    return jax.shard_map(run, mesh=mesh, in_specs=in_specs, out_specs=out_specs, check_vma=False)
```

```python
import functools

import jax
import jax.numpy as jnp
from jax import lax
from jax.experimental import pallas as pl
from jax.experimental.pallas import tpu as pltpu
from jax.sharding import PartitionSpec as P

EPSILON = 1e-05
ROOT = 0.7978845608028654
CUBE = 0.044715
F32 = jnp.float32
BF16 = jnp.bfloat16
STEP = 256
LANES = 128
LINES = 3
STEPS = 4
PIECES = 2
TN = (((0,), (0,)), ((), ()))
NT = (((1,), (1,)), ((), ()))
VM = pl.BlockSpec(memory_space=pltpu.VMEM)
SM = pl.BlockSpec(memory_space=pltpu.SMEM)


def dot(a, b):
    return jnp.dot(a, b, preferred_element_type=F32)


def dot_tn(a, b):
    return lax.dot_general(a, b, TN, preferred_element_type=F32)


def dot_nt(a, b):
    return lax.dot_general(a, b, NT, preferred_element_type=F32)


def bend(v):
    return jnp.tanh(v * (ROOT + (ROOT * CUBE) * (v * v)))


def act(v):
    half = 0.5 * v
    return half + half * bend(v)


def act_slope(v):
    t = bend(v)
    inner = v * (0.5 * ROOT + (1.5 * ROOT * CUBE) * (v * v))
    return 0.5 + 0.5 * t + inner * (1.0 - t * t)


def chunks(total, body, step=STEP):
    full = total // step

    def go(c, carry):
        body(pl.multiple_of(c * step, step), step)
        return carry

    if full:
        lax.fori_loop(0, full, go, 0)
    if total % step:
        body(full * step, total % step)


def fold(v):
    return jnp.sum(v.reshape(v.shape[0] // 8, 8, v.shape[1]), axis=0)


def widen(live, width):
    return jnp.concatenate([live] * (width // LANES), axis=1) if width > LANES else live


def norm_of(got, counts):
    s = jnp.sum(got[...], axis=0)
    share_of = 1.0 / jnp.sum(counts[...], axis=0)[2:3, 0:1]
    mu = s[0:1] * share_of
    return mu, lax.rsqrt(s[1:2] * share_of - mu * mu + EPSILON), share_of


def send_sums(out, acc):
    out[...] = jnp.broadcast_to(jnp.sum(acc[...], axis=1)[None], out.shape)


def start_sums(acc):
    @pl.when(pl.program_id(0) == 0)
    def _():
        acc[...] = jnp.zeros_like(acc)


def end_sums(out, acc):
    @pl.when(pl.program_id(0) == pl.num_programs(0) - 1)
    def _():
        send_sums(out, acc)


def near_kernel(dims, *refs):
    *feats, w, out = refs
    share = feats[0].shape[1]
    me = dims[2]
    ws = [w[pl.ds(pl.multiple_of((me ^ k) * share, share), share), :] for k in range(len(feats))]
    out[...] = sum(dot(f[...], wk) for f, wk in zip(feats, ws))


def part_far_kernel(dims, own, beside, *refs):
    n = len(refs) // 2
    share = own.shape[1]
    core = lax.bitwise_and(dims[2], 1)
    mine = pl.ds(pl.multiple_of(core * share, share), share)
    other = pl.ds(pl.multiple_of((1 - core) * share, share), share)
    for w, out in zip(refs[:n], refs[n:]):
        out[...] = (dot(own[...], w[mine, :]) + dot(beside[...], w[other, :])).astype(BF16)


def rows_kernel(dims, *refs):
    n = len(refs) // 3
    ws, rows, passed = (refs[i * n : (i + 1) * n] for i in range(3))
    share = rows[0].shape[0]
    core = lax.bitwise_and(dims[2], 1)
    for w, row, pass_on in zip(ws, rows, passed):
        row[...] = w[pl.ds(pl.multiple_of(core * share, share), share), :]
        pass_on[...] = w[pl.ds(pl.multiple_of((1 - core) * share, share), share), :]


def far_kernel(live, part, *refs):
    *got, out, spread, acc = refs
    start_sums(acc)
    z = part[...] + sum(g[...].astype(F32) for g in got)
    m = widen(live[...], z.shape[1])
    z = jnp.where(m > 0.0, z, 0.0)
    out[...] = z
    acc[0] += fold(z)
    acc[1] += fold(z * z)
    acc[2] += fold(m)
    end_sums(spread, acc)


def pad_edges(pad, side, line, wide, slots):
    width = pad.shape[1]
    pad[0:wide] = jnp.zeros((wide, width), F32)
    pad[(side + 1) * wide : (side + 2) * wide] = jnp.zeros((wide, width), F32)


def pad_line(pad, i, value, line, wide, slots):
    o = pl.multiple_of((i + 1) * wide, 8)
    edge = jnp.zeros((slots, pad.shape[1]), F32)
    pad[pl.ds(o, slots), :] = edge
    pad[pl.ds(o + slots, line), :] = value
    pad[pl.ds(o + slots + line, slots), :] = edge


def conv_lines(pad, first, count, taps, line, wide, slots, flip):
    total = None
    for t in range(9):
        a, b = divmod(t, 3)
        starts = [(first + i + a) * wide + b * slots for i in range(count)]
        x = jnp.concatenate([pad[o : o + line].astype(BF16) for o in starts], axis=0)
        d = dot_nt(x, taps[8 - t]) if flip else dot(x, taps[t])
        total = d if total is None else total + d
    return total


def taps_kernel(w, out):
    width, group_width = w.shape[2], w.shape[1]
    ids = [lax.broadcasted_iota(jnp.int32, (width, width), b) // group_width for b in range(2)]
    same = ids[0] == ids[1]
    for t in range(9):
        tiled = jnp.concatenate([w[t].astype(F32)] * (width // group_width), axis=0)
        out[t] = jnp.where(same, tiled, 0.0).astype(BF16)


def conv_kernel(side, slots, live, z, got, gain, shift, taps, out, spread, pad, acc):
    line, wide = side * slots, (side + 2) * slots
    rows, width = z.shape
    mu, r, _ = norm_of(got, got)
    a = r * gain[...]
    b = shift[...] - mu * a
    pad_edges(pad, side, line, wide, slots)
    acc[...] = jnp.zeros_like(acc)

    def fill(i, carry):
        here = pl.ds(pl.multiple_of(i * line, 8), line)
        h = widen(live[here, :], width) * act(z[here, :] * a + b)
        pad_line(pad, i, h.astype(BF16).astype(F32), line, wide, slots)
        return carry

    lax.fori_loop(0, side, fill, 0)

    for first in range(0, side, LINES):
        count = min(LINES, side - first)
        here = slice(first * line, (first + count) * line)
        total = conv_lines(pad, first, count, taps, line, wide, slots, False)
        out[here] = total
        m = widen(live[here], width) * total
        acc[0] += fold(m)
        acc[1] += fold(m * total)
    used = side * line
    out[used:rows] = jnp.zeros((rows - used, width), F32)
    send_sums(spread, acc)


def hidden_kernel(live, z, counts, got, gain, shift, out):
    mu, r, _ = norm_of(got, counts)
    a = r * gain[...]
    b = shift[...] - mu * a
    m = widen(live[...], z.shape[1])
    out[...] = (m * act(z[...] * a + b)).astype(BF16)


def slope_kernel(live, z, counts, got, gain, shift, out):
    mu, r, _ = norm_of(got, counts)
    a = r * gain[...]
    b = shift[...] - mu * a
    out[...] = widen(live[...], z.shape[1]) * act_slope(z[...] * a + b)


def expand_near_kernel(*refs):
    *ins, out = refs
    k = len(ins) // 2
    out[...] = sum(dot(h[...], w[...]) for h, w in zip(ins[:k], ins[k:]))


def expand_far_kernel(live, part, *refs):
    *ins, out, spread, acc = refs
    k = len(ins) // 2
    start_sums(acc)
    e = part[...] + sum(dot(h[...], w[...]) for h, w in zip(ins[:k], ins[k:]))
    out[...] = e
    m = widen(live[...], e.shape[1]) * e
    acc[0] += fold(m)
    acc[1] += fold(m * e)
    end_sums(spread, acc)


def third_kernel(live, e, counts, got, gain, shift, feats, cot, d_pre, spread, acc):
    mu, r, _ = norm_of(got, counts)
    start_sums(acc)
    zhat = (e[...] - mu) * r
    v = zhat * gain[...] + shift[...] + feats[...].astype(F32)
    m = widen(live[...], v.shape[1])
    d = m * cot[...].astype(F32) * act_slope(v)
    d_pre[...] = d
    acc[0] += fold(d)
    acc[1] += fold(d * zhat)
    end_sums(spread, acc)


def block_kernel(live, e, counts, got, gain, shift, feats, out):
    mu, r, _ = norm_of(got, counts)
    v = (e[...] - mu) * r * gain[...] + shift[...] + feats[...].astype(F32)
    out[...] = (widen(live[...], v.shape[1]) * act(v)).astype(BF16)


def d_expanded_kernel(live, e, d_pre, counts, got, totals, gain, w, d_exp, out, sums):
    mu, r, share_of = norm_of(got, counts)
    t = jnp.sum(totals[...], axis=0)
    sums[...] = t
    t = t * share_of
    scale = r * gain[...]
    zhat = (e[...] - mu) * r
    m = widen(live[...], zhat.shape[1])
    d = (m * scale * (d_pre[...] - t[0:1] - zhat * t[1:2])).astype(BF16)
    d_exp[...] = d
    out[...] = dot_nt(d, w[...]).astype(BF16)


def back_expand_kernel(d_exp, *refs):
    k = len(refs) // 2
    for w, out in zip(refs[:k], refs[k:]):
        out[...] = dot_nt(d_exp[...], w[...]).astype(out.dtype)


def merge_kernel(d_exp, w, *refs):
    *got, out = refs
    total = dot_nt(d_exp[...], w[...]) + sum(g[...].astype(F32) for g in got)
    out[...] = total.astype(BF16)


def expand_grad_kernel(d_exp, *refs):
    *hs, out = refs
    for k, h in enumerate(hs):
        out[k] = dot_tn(h[...], d_exp[...]).astype(BF16)


def d_two_kernel(slope, z, counts, got, *refs):
    *terms, d_out, spread, acc = refs
    mu, r, _ = norm_of(got, counts)
    start_sums(acc)
    d = sum(t[...].astype(F32) for t in terms) * slope[...]
    d_out[...] = d
    acc[0] += fold(d)
    acc[1] += fold(d * ((z[...] - mu) * r))
    end_sums(spread, acc)


def conv_back_kernel(
    side, slots, live, d_two, grouped, got_two, totals, gain, slope, z, got, taps,
    d_grouped, d_one, spread, sums, pad, acc,
):
    line, wide = side * slots, (side + 2) * slots
    rows, width = z.shape
    mu_two, r_two, share_of = norm_of(got_two, got)
    mu, r, _ = norm_of(got, got)
    t = jnp.sum(totals[...], axis=0)
    sums[...] = t
    t = t * share_of
    scale = r_two * gain[...]
    pad_edges(pad, side, line, wide, slots)
    acc[...] = jnp.zeros_like(acc)

    def fill(i, carry):
        here = pl.ds(pl.multiple_of(i * line, 8), line)
        zhat = (grouped[here, :] - mu_two) * r_two
        m = widen(live[here, :], width)
        d = m * scale * (d_two[here, :] - t[0:1] - zhat * t[1:2])
        d = d.astype(BF16).astype(F32)
        d_grouped[here, :] = d
        pad_line(pad, i, d, line, wide, slots)
        return carry

    lax.fori_loop(0, side, fill, 0)

    for first in range(0, side, LINES):
        count = min(LINES, side - first)
        here = slice(first * line, (first + count) * line)
        d = conv_lines(pad, first, count, taps, line, wide, slots, True) * slope[here]
        d_one[here] = d
        acc[0] += fold(d)
        acc[1] += fold(d * ((z[here] - mu) * r))
    used = side * line
    d_one[used:rows] = jnp.zeros((rows - used, width), F32)
    d_grouped[used:rows] = jnp.zeros((rows - used, width), F32)
    send_sums(spread, acc)


def d_reduced_kernel(live, d_one, z, got, totals, gain, out, sums):
    mu, r, share_of = norm_of(got, got)
    t = jnp.sum(totals[...], axis=0)
    sums[...] = t
    t = t * share_of
    zhat = (z[...] - mu) * r
    m = widen(live[...], zhat.shape[1])
    out[...] = (m * (r * gain[...]) * (d_one[...] - t[0:1] - zhat * t[1:2])).astype(BF16)


def group_grad_kernel(side, slots, group_width, live, z, got, gain, shift, d_grouped, out, pad):
    line, wide = side * slots, (side + 2) * slots
    width = z.shape[1]
    mu, r, _ = norm_of(got, got)
    scale = r * gain[...]
    offset = shift[...] - mu * scale
    pad_edges(pad, side, line, wide, slots)

    def fill(i, carry):
        here = pl.ds(pl.multiple_of(i * line, 8), line)
        h = widen(live[here, :], width) * act(z[here, :] * scale + offset)
        pad_line(pad, i, h.astype(BF16).astype(F32), line, wide, slots)
        return carry

    lax.fori_loop(0, side, fill, 0)
    d = d_grouped[0 : side * line].astype(BF16)
    ids = [lax.broadcasted_iota(jnp.int32, (width, width), b) // group_width for b in range(2)]
    same = ids[0] == ids[1]
    for t in range(9):
        a, b = divmod(t, 3)
        starts = [(i + a) * wide + b * slots for i in range(side)]
        x = jnp.concatenate([pad[o : o + line].astype(BF16) for o in starts], axis=0)
        dense = jnp.where(same, dot_tn(x, d), 0.0)
        picked = jnp.sum(dense.reshape(width // group_width, group_width, width), axis=0)
        out[t * group_width : (t + 1) * group_width] = picked.astype(BF16)


def reduce_grad_kernel(dims, d_red, *refs):
    *feats, out, rest = refs
    share = feats[0].shape[1]
    me = dims[2]
    for k in range(2):
        rows = pl.ds(pl.multiple_of((me ^ k) * share, share), share)
        out[rows, :] = dot_tn(feats[k][...], d_red[...]).astype(BF16)
    for k, f in enumerate(feats[2:]):
        rest[k] = dot_tn(f[...], d_red[0 : f.shape[0]])


def reduce_grad_rest_kernel(firsts, dims, d_red, near, rest, *refs):
    *feats, out, send_a, send_b = refs
    share = feats[0].shape[1]
    me = dims[2]
    for k in range(2):
        rows = pl.ds(pl.multiple_of((me ^ k) * share, share), share)
        out[rows, :] = near[rows, :]
    for k, f in enumerate(feats):
        rows = pl.ds(pl.multiple_of((me ^ (k + 2)) * share, share), share)
        first = d_red.shape[0] - f.shape[0]
        out[rows, :] = (rest[k] + dot_tn(f[...], d_red[first:])).astype(BF16)
    n = send_a.shape[0]
    for h, send in enumerate((send_a, send_b)):
        at = 2 * h * n + (1 - bit_of(dims[3], firsts[h])) * n
        send[...] = out[pl.ds(pl.multiple_of(at, 16), n), :]


def features_grad_kernel(part, *refs):
    *ins, out = refs
    k = len(ins) // 2
    out[...] = part[...] + sum(dot_nt(d[...], w[...]) for d, w in zip(ins[:k], ins[k:]))


def pick_kernel(dims, w_expand, w_reduce, gain, shift, cot, *outs):
    me = dims[2]
    n = len(outs) - 5
    cols, rows, rest = outs[:n], outs[n : n + 2], outs[n + 2 :]
    share = rows[0].shape[0]

    @pl.when(pl.program_id(0) == 0)
    def _():
        for k in range(n):
            at = pl.ds(pl.multiple_of((me ^ k) * share, share), share)
            cols[k][...] = w_expand[:, at]
            if k < 2:
                rows[k][...] = w_reduce[at, :]
        at = pl.ds(pl.multiple_of(me * share, share), share)
        rest[0][...] = gain[:, at]
        rest[1][...] = shift[:, at]

    at = pl.ds(pl.multiple_of(me * share, share), share)
    first = pl.program_id(0) * cot.shape[0]
    row = lax.broadcasted_iota(jnp.int32, (cot.shape[0], share), 0) + first
    rest[2][...] = jnp.where(row < dims[4], cot[:, at].astype(F32), 0.0).astype(BF16)


def bit_of(v, bit):
    return lax.bitwise_and(lax.shift_right_logical(v, bit), 1)


def add_terms(b, terms, order, step, last, base):
    total = None
    for first, (term, size) in enumerate(terms):
        rows, at = size, base if first == 0 else 0
        for t in range(first, step + (not last)):
            rows //= 2
            side = bit_of(b, order[t])
            at += rows * (side if t < step else 1 - side)
        here = pl.ds(at if isinstance(at, int) else pl.multiple_of(at, min(rows, 16)), rows)
        v = term[:, here, :] if len(term.shape) == 3 else term[here, :]
        total = v.astype(F32) if total is None else total + v.astype(F32)
    return total.astype(BF16)


def send_both_kernel(step, last, orders, dims, whole, *refs):
    half = whole.shape[-2] // 2
    n = step
    outs = refs[2 * n :]
    for i, order in enumerate(orders):
        terms = [(whole, half)] + [(r, r.shape[-2]) for r in refs[i * n : (i + 1) * n]]
        total = add_terms(dims[3], terms, order, step, last, i * half)
        rows = total.shape[-2]
        if last and len(whole.shape) == 3:
            outs[0][:, i * rows : (i + 1) * rows, :] = total
        elif last:
            outs[0][i * rows : (i + 1) * rows] = total
        else:
            outs[i][...] = total


def double_pair_kernel(bits, dims, sums, *refs):
    *ins, a, b = refs
    n = ins[0].shape[0]
    for i, (bit, out) in enumerate(zip(bits, (a, b))):
        mine = sums[i * n : (i + 1) * n] if len(ins) == 2 else (sums, ins[0])[i][...]
        other = ins[i] if len(ins) == 2 else ins[i + 1]
        upper = bit_of(dims[3], bit)
        out[pl.ds(pl.multiple_of(upper * n, min(n, 16)), n), :] = mine
        out[pl.ds(pl.multiple_of((1 - upper) * n, min(n, 16)), n), :] = other[...]


def finish_kernel(bits, dims, a, b, other_a, other_b, out):
    n = a.shape[0]
    for i, (bit, mine, other) in enumerate(zip(bits, (a, b), (other_a, other_b))):
        upper = bit_of(dims[3], bit)
        at = 2 * i * n
        out[pl.ds(pl.multiple_of(at + upper * n, min(n, 16)), n), :] = mine[...].astype(F32)
        out[pl.ds(pl.multiple_of(at + (1 - upper) * n, min(n, 16)), n), :] = other[...].astype(F32)


def arrange_kernel(dims, *refs):
    *cols, a, b = refs
    n, share = a.shape[0], cols[0].shape[1]
    for k, c in enumerate(cols):
        at = pl.ds(pl.multiple_of((dims[2] ^ k) * share, share), share)
        a[:, at] = c[0:n]
        b[:, at] = c[n:]


def split_kernel(a, b, *outs):
    for k, out in enumerate(outs):
        out[...] = (a[k].astype(F32) + b[k].astype(F32)).astype(BF16)


def add_kernel(a, b, out):
    out[...] = (a[...].astype(F32) + b[...].astype(F32)).astype(out.dtype)


def input_far_kernel(part, *refs):
    *ins, out = refs
    n = len(ins) // (PIECES + 1)
    ds, ws = ins[: n * PIECES], ins[n * PIECES :]
    for step in range(PIECES):

        @pl.when(pl.program_id(0) == step)
        def _(step=step):
            got = sum(dot_nt(ds[k * PIECES + step][...], w[...]) for k, w in enumerate(ws))
            out[...] = part[...] + got


def call(kernel, outs, ins, scratch=(), flops=0, name=None, smem=False, steps=0, size=0):
    moved = sum(x.size * x.dtype.itemsize for x in ins)
    moved += sum(int(o.size) * o.dtype.itemsize for o in outs)
    size = size or max(o.shape[0] for o in outs)
    block = -(-size // (16 * steps)) * 16 if steps else 0

    def spec(x):
        if not steps:
            return VM
        if len(x.shape) == 2 and steps * block - 64 < x.shape[0] <= steps * block:
            return pl.BlockSpec((block, x.shape[1]), lambda s: (s, 0))
        return pl.BlockSpec(x.shape, lambda s: (0,) * len(x.shape))

    specs = [spec(x) for x in ins]
    if smem:
        specs[0] = SM
    got = pl.pallas_call(
        kernel,
        out_shape=list(outs),
        grid=(steps,) if steps else (),
        in_specs=specs,
        out_specs=[spec(o) for o in outs],
        scratch_shapes=list(scratch),
        compiler_params=pltpu.CompilerParams(vmem_limit_bytes=16 << 20),
        cost_estimate=pl.CostEstimate(flops=flops, bytes_accessed=moved, transcendentals=0),
        name=name,
    )(*ins)
    return got[0] if len(outs) == 1 else got


def after(v, *others):
    return lax.optimization_barrier((v, *others))[0]


def swap(v, axis, size, k):
    return lax.ppermute(v, axis, [(i, i ^ k) for i in range(size)])


def batch_sum(spread):
    return lax.all_to_all(spread, "batch", 0, 0)


def pair_kernel(a, b, out):
    out[0:1] = a[...]
    out[1:2] = b[...]


def sum_kernel(*refs):
    *terms, out = refs
    out[...] = sum(t[...] for t in terms)


def batch_sum_stepwise(v, size):
    shape = jax.ShapeDtypeStruct(v.shape, v.dtype)
    got = [swap(v, "batch", size, k) for k in range(2, size, 2)]
    v = call(sum_kernel, [shape], [v, *got], name="sum")
    both = jax.ShapeDtypeStruct((2, *v.shape[1:]), v.dtype)
    return call(pair_kernel, [both], [v, swap(v, "batch", size, 1)], name="pair")


def gather_chan(v, size):
    held = {0: v}
    bit = size // 2
    while bit:
        held.update({k | bit: swap(b, "chan", size, bit) for k, b in list(held.items())})
        bit //= 2
    return [held[k] for k in range(size)]


def send_both(dims, whole, got, orders, step, last=False):
    shape = list(whole.shape)
    shape[-2] >>= step if last else step + 2
    return call(
        functools.partial(send_both_kernel, step, last, orders),
        [jax.ShapeDtypeStruct(tuple(shape), BF16)] * (1 if last else 2),
        [dims, whole, *got[0], *got[1]], name="send_both", smem=True,
    )


def double_pair(dims, pair, new, bits):
    n, columns = new[0].shape
    return call(
        functools.partial(double_pair_kernel, bits),
        [jax.ShapeDtypeStruct((2 * n, columns), BF16)] * 2, [dims, *pair, *new],
        name="double_pair", smem=True,
    )


def finish(dims, pair, new, bits):
    n, columns = new[0].shape
    return call(
        functools.partial(finish_kernel, bits), [jax.ShapeDtypeStruct((4 * n, columns), F32)],
        [dims, *pair, *new], name="finish", smem=True,
    )


def add(a, b, dtype=BF16):
    return call(add_kernel, [jax.ShapeDtypeStruct(a.shape, dtype)], [a, b], name="add")


def shards(n_batch, n_chan, *args):
    (features, w_reduce, gain_one, shift_one, w_group, gain_two, shift_two, w_expand,
     gain_three, shift_three, cotangent, resolution, crop_count) = args
    slots, side, _, share = features.shape
    width = w_reduce.shape[1]
    group_width = w_group.shape[2]
    rows = slots * side * side
    unit = 16 * STEPS
    padded = -(-rows // unit) * unit
    line, wide = side * slots, (side + 2) * slots
    me = lax.axis_index("chan")
    others = range(n_chan)
    shape = jax.ShapeDtypeStruct
    acc = lambda n, c: pltpu.VMEM((n, 8, c), F32)
    tall = pltpu.VMEM(((side + 2) * wide, width), F32)
    mm = 2 * padded * share * width

    feats = features.transpose(1, 2, 0, 3).reshape(rows, share)
    ends = ((0, padded - rows), (0, 0))
    even = [k for k in others[2:] if k % 2 == 0]
    at = [lax.bitwise_and(me ^ k, n_chan - 2) * share for k in even]
    w_far = [lax.dynamic_slice_in_dim(w_reduce, o, 2 * share, 0) for o in at]
    own = jnp.pad(after(feats, *w_far), ends)
    w_far = [swap(w, "chan", n_chan, k) for k, w in zip(even, w_far)]
    beside = swap(own, "chan", n_chan, 1)

    dims = jnp.stack(
        [resolution[0], crop_count[0], me, lax.axis_index("batch"), jnp.int32(rows)]
    )
    row = lax.broadcasted_iota(jnp.int32, (padded, LANES), 0)
    crop, j, i = row % slots, (row // slots) % side, row // line
    live = ((crop < crop_count[0]) & (i < resolution[0]) & (j < resolution[0])).astype(F32)
    taps = call(
        taps_kernel, [shape((9, width, width), BF16)], [w_group.reshape(9, group_width, width)],
        flops=mm, name="taps",
    )
    line_of = lambda v: v.reshape(1, -1)
    gain_one, shift_one, gain_two, shift_two = map(
        line_of, (gain_one, shift_one, gain_two, shift_two)
    )

    parts = call(
        part_far_kernel, [shape((padded, width), BF16)] * len(even), [dims, own, beside, *w_far],
        flops=2 * len(even) * mm, name="part_far", steps=2, smem=True,
    )
    parts = parts if len(even) > 1 else [parts]
    got = call(
        rows_kernel, [shape((share, width), BF16)] * 2 * len(even),
        [dims, *[after(w, *parts) for w in w_far]], name="rows", smem=True,
    )
    rows_far, passed = got[: len(even)], got[len(even) :]
    got = [swap(p, "chan", n_chan, k) for k, p in zip(even, parts)]

    *picked, gain_c, shift_c, cot = call(
        pick_kernel,
        [shape((width, share), BF16)] * n_chan + [shape((share, width), BF16)] * 2
        + [shape((1, share), F32)] * 2 + [shape((padded, share), BF16)],
        [dims, after(w_expand, *parts), w_reduce, line_of(gain_three), line_of(shift_three),
         cotangent.transpose(1, 2, 0, 3).reshape(rows, -1)],
        flops=mm, name="pick", smem=True, steps=STEPS,
    )
    part = call(
        near_kernel, [shape((padded, width), F32)], [dims, after(own, *parts), beside, w_reduce],
        flops=2 * mm, name="near", steps=STEPS, smem=True,
    )
    w_cols = [picked[0], swap(after(picked[1], part), "chan", n_chan, 1)]
    w_rows = [picked[n_chan], swap(after(picked[n_chan + 1], part), "chan", n_chan, 1)]
    for row, pass_on in zip(rows_far, passed):
        w_rows += [row, swap(after(pass_on, part), "chan", n_chan, 1)]
    ready = (part, live, cot, taps, gain_c, shift_c, w_cols[1], *w_rows, *picked)
    got = [after(v, *ready) for v in got]
    w_cols += [swap(after(picked[k], *got), "chan", n_chan, k) for k in others[2:]]
    z, spread = call(
        far_kernel, [shape((padded, width), F32), shape((1, 3, width), F32)],
        [live, part, *got], [acc(3, width)], flops=mm, name="far", steps=STEPS,
    )
    got_one = batch_sum_stepwise(spread, n_batch)

    grouped, spread = call(
        functools.partial(conv_kernel, side, slots),
        [shape((padded, width), F32), shape((n_batch, 2, width), F32)],
        [live, z, got_one, gain_one, shift_one, taps], [tall, acc(2, width)],
        flops=18 * padded * width * width, name="conv",
    )
    got_two = batch_sum(after(spread, *w_cols))
    hidden_two = call(
        hidden_kernel, [shape((padded, width), BF16)],
        [live, grouped, got_one, got_two, gain_two, shift_two], flops=mm, name="hidden", steps=STEPS,
    )
    half = padded * 42 // 64 // 16 * 16
    own_first = after(own, hidden_two)[:half]
    first = gather_y(hidden_two, n_chan)
    beside_two = swap(hidden_two, "chan", n_chan, 1)
    slope_two = call(
        slope_kernel, [shape((padded, width), F32)],
        [live, grouped, got_one, got_two, gain_two, shift_two], flops=mm, name="slope_two", steps=STEPS,
    )
    slope_one = call(
        slope_kernel, [shape((padded, width), F32)],
        [live, z, got_one, got_one, gain_one, shift_one], flops=mm, name="slope_one", steps=STEPS,
    )
    part = call(
        expand_near_kernel, [shape((padded, share), F32)], [hidden_two, beside_two, *w_cols[:2]],
        flops=2 * mm, name="expand_near", steps=2,
    )
    first = {k: after(v, part, slope_one, slope_two, own_first, *w_cols) for k, v in first.items()}
    far_halves = [gather_y(after(own_first, *first.values()), n_chan)]
    first = gather_core(first, n_chan)
    hidden_all = [hidden_two, beside_two] + [first[k] for k in others if k > 1]
    expanded, spread = call(
        expand_far_kernel, [shape((padded, share), F32), shape((n_batch, 2, share), F32)],
        [live, part, *hidden_all[2:], *w_cols[2:]], [acc(2, share)],
        flops=(n_chan - 2) * mm, name="expand_far", steps=STEPS,
    )
    got_three = batch_sum(spread)
    d_pre, spread = call(
        third_kernel, [shape((padded, share), F32), shape((n_batch, 2, share), F32)],
        [live, expanded, got_one, got_three, gain_c, shift_c, own, cot], [acc(2, share)],
        flops=4 * mm, name="third", steps=STEPS,
    )
    totals_three = batch_sum(spread)
    top = n_chan - 1
    d_expanded, sent, sums_three = call(
        d_expanded_kernel,
        [shape((padded, share), BF16), shape((padded, width), BF16), shape((2, share), F32)],
        [live, expanded, d_pre, got_one, got_three, totals_three, gain_c]
        + [w_cols[top]],
        flops=2 * mm, name="d_expanded", steps=STEPS,
    )
    early = [0, 1]
    far_halves[0] = {k: after(v, d_expanded) for k, v in far_halves[0].items()}
    d_zero, d_near = call(
        back_expand_kernel, [shape((padded, width), F32), shape((padded, width), BF16)],
        [after(d_expanded, sent, *far_halves[0].values())] + [w_cols[k] for k in early], flops=2 * mm,
        name="back_expand", steps=2,
    )

    def part_sum(k, below):
        if k == top:
            return sent
        if k == 1:
            return d_near
        got, bit = [], 1
        while bit < below:
            got.append(swap(part_sum(k | bit, bit), "chan", n_chan, bit))
            bit *= 2
        if k == 0:
            return [d_zero, *got]
        return call(
            merge_kernel, [shape((padded, width), BF16)],
            [after(d_expanded, d_near), w_cols[k], *got], flops=mm, name="merge", steps=2,
        )

    far_sum = part_sum(n_chan // 2, n_chan // 2)
    terms = [d_zero]
    bit = 1
    while bit < n_chan:
        mine = far_sum if bit == n_chan // 2 else part_sum(bit, bit)
        terms.append(swap(mine, "chan", n_chan, bit))
        bit *= 2
    expand_part = call(
        expand_grad_kernel, [shape((n_chan, width, share), BF16)],
        [after(d_expanded, far_sum), *hidden_all], flops=n_chan * mm, name="expand_grad",
    )
    bits = n_batch.bit_length() - 1
    top = bits - 1
    orders = [list(range(top)), [1, 0, *range(2, top)]]
    halves = [0, 1]
    got = [[], []]
    for s in range(top):
        send = send_both(dims, expand_part, got, orders, s)
        new = [swap(send[h], "batch", n_batch, 1 << orders[h][s]) for h in halves]
        if s == 0:
            block_out = call(
                block_kernel, [shape((rows, share), BF16)],
                [live, after(expanded, send[0]), got_one, got_three, gain_c, shift_c, own],
                flops=2 * mm, name="block", steps=STEPS,
            )
            new = [after(v, block_out) for v in new]
        got = [got[h] + [new[h]] for h in halves]
    mine = send_both(dims, expand_part, got, orders, top, True)
    expand_other = swap(mine, "batch", n_batch, 1 << (bits - 1))
    far_halves[0] = gather_core({k: after(v, far_sum) for k, v in far_halves[0].items()}, n_chan)
    terms[0] = after(d_zero, *far_halves[0].values())
    far_halves.append(gather_y(after(own, terms[-1], mine)[half:], n_chan))
    d_two, spread = call(
        d_two_kernel, [shape((padded, width), F32), shape((n_batch, 2, width), F32)],
        [slope_two, grouped, got_one, got_two, *terms], [acc(2, width)], flops=mm, name="d_two", steps=STEPS,
    )
    totals_two = batch_sum(spread)
    d_grouped, d_one, spread, sums_two = call(
        functools.partial(conv_back_kernel, side, slots),
        [shape((padded, width), F32)] * 2 + [shape((n_batch, 2, width), F32), shape((2, width), F32)],
        [live, d_two, grouped, got_two, totals_two, gain_two, slope_one, z, got_one, taps],
        [tall, acc(2, width)], flops=18 * padded * width * width, name="conv_back",
    )
    parts = call(
        split_kernel, [shape(mine.shape[1:], BF16)] * n_chan,
        [mine, after(expand_other, d_one)], name="split",
    )
    far_halves[1] = {k: after(v, d_one) for k, v in far_halves[1].items()}
    totals_one = batch_sum(after(spread, *parts, *far_halves[1].values()))
    d_reduced, sums_one = call(
        d_reduced_kernel, [shape((padded, width), BF16), shape((2, width), F32)],
        [live, d_one, z, got_one, totals_one, gain_one], flops=mm, name="d_reduced", steps=STEPS,
    )
    far_halves[1] = gather_core(far_halves[1], n_chan)
    firsts, lasts = ([far_halves[h][k] for k in others[2:]] for h in range(2))
    tail, rest = call(
        reduce_grad_kernel,
        [shape((n_chan * share, width), BF16), shape((n_chan - 2, share, width), F32)],
        [dims, d_reduced, own, beside, *firsts], flops=n_chan * mm, name="reduce_grad", smem=True,
    )
    tail, *sends = call(
        functools.partial(reduce_grad_rest_kernel, [o[0] for o in orders]),
        [shape((n_chan * share, width), BF16)] + [shape((n_chan * share // 4, width), BF16)] * 2,
        [dims, d_reduced, tail, rest, *lasts], flops=mm, name="reduce_grad_rest", smem=True,
    )
    d_beside = swap(d_reduced, "chan", n_chan, 1)
    sends = [after(v, d_beside) for v in sends]
    piece_rows = padded // PIECES
    d_far = []

    def far_rows(at, *ready):
        piece = after(d_reduced, *ready)[at * piece_rows : (at + 1) * piece_rows]
        d_far.append(gather_y(piece, n_chan))
        return list(d_far[at].values())

    def pass_on(at, *ready):
        d_far[at] = gather_core({k: after(v, *ready) for k, v in d_far[at].items()}, n_chan)
        return list(d_far[at].values())

    got = [[], []]
    for s in range(top):
        send = send_both(dims, tail, got, orders, s) if s else sends
        new = [swap(send[h], "batch", n_batch, 1 << orders[h][s]) for h in halves]
        ties = []
        if s == 0:
            cols = [parts[0]]
            cols += [swap(after(parts[k], send[0]), "chan", n_chan, k) for k in others if k]
            cols = call(
                arrange_kernel, [shape((mine.shape[1] // 2, n_chan * share), BF16)] * 2, [dims, *cols],
                name="arrange", smem=True,
            )
            far_rows(0, *cols)
            ties = cols
        elif s == 1:
            others_cols = [
                swap(after(cols[h], send[0]), "batch", n_batch, 1 << orders[h][top - 1])
                for h in halves
            ]
        new = [after(v, *ties) for v in new]
        got = [got[i] + [new[i]] for i in range(2)]
    sums = send_both(dims, tail, got, orders, top, True)
    other = swap(sums, "batch", n_batch, 1 << top)
    others_cols = [after(v, sums) for v in others_cols]
    cols = double_pair(dims, cols, others_cols, [o[top - 1] for o in orders])
    for t in reversed(range(1, top - 1)):
        others_cols = [swap(cols[h], "batch", n_batch, 1 << orders[h][t]) for h in halves]
        cols = double_pair(dims, cols, others_cols, [o[t] for o in orders])
    group_part = call(
        functools.partial(group_grad_kernel, side, slots, group_width),
        [shape((9 * group_width, width), BF16)],
        [live, z, got_one, gain_one, shift_one, after(d_grouped, *cols)],
        [tall], flops=mm, name="group_grad",
    )
    group_other = swap(group_part, "batch", n_batch, 1)
    others_cols = [
        swap(after(cols[h], sums), "batch", n_batch, 1 << orders[h][0]) for h in halves
    ]
    moved = [*far_rows(1, sums), *pass_on(0, sums)]
    part = call(
        features_grad_kernel, [shape((padded, share), F32)],
        [d_pre, after(d_reduced, group_part), d_beside, *w_rows[:2]], flops=2 * mm,
        name="input_near", steps=STEPS,
    )
    sums = add(sums, after(other, part))
    group_part = add(group_part, after(group_other, sums))
    others_cols = [after(v, sums) for v in others_cols]
    moved = [after(v, sums) for v in moved]
    expand_grad = finish(dims, cols, others_cols, [o[0] for o in orders])
    pair = [sums]
    for s in reversed(range(top)):
        n = pair[0].shape[0] // (2 if len(pair) == 1 else 1)
        cut = [sums[:n], sums[n:]] if len(pair) == 1 else pair
        new = [swap(cut[i], "batch", n_batch, 1 << orders[i][s]) for i in range(2)]
        if s == top - 1:
            group_other = swap(after(group_part, sums), "batch", n_batch, 2)
            group_part = add(group_part, after(group_other, expand_grad))
            before = (group_part,)
        if s == 0:
            pass_on(1, cut[0])
            for t in range(2, bits):
                group_part = after(group_part, cut[0])
                group_other = swap(group_part, "batch", n_batch, 1 << t)
                if t == 2:
                    features_grad = call(
                        input_far_kernel, [shape((rows, share), F32)],
                        [after(part, cut[0]), *[d[k] for k in others[2:] for d in d_far], *w_rows[2:]],
                        flops=(n_chan - 2) * mm, name="input_far", steps=PIECES, size=padded,
                    )
                    group_other = after(group_other, features_grad)
                group_part = add(group_part, group_other, BF16 if t + 1 < bits else F32)
            before = (group_part,)
        new = [after(v, *before) for v in new]
        if s:
            pair = double_pair(dims, pair, new, [o[s] for o in orders])
    tail = finish(dims, pair, new, [o[0] for o in orders])
    reduce_grad, group_grad = tail, group_part

    shaped = lambda v: v.reshape(side, side, slots, share).transpose(2, 0, 1, 3)
    return (
        shaped(block_out),
        shaped(features_grad),
        reduce_grad,
        sums_one[1],
        sums_one[0],
        group_grad.reshape(3, 3, group_width, width),
        sums_two[1],
        sums_two[0],
        expand_grad,
        sums_three[1],
        sums_three[0],
    )


def gather_y(v, size):
    held = {0: v}
    bit = size // 2
    while bit > 1:
        held.update({k | bit: swap(b, "chan", size, bit) for k, b in list(held.items())})
        bit //= 2
    return {k: b for k, b in held.items() if k}


def gather_core(held, size):
    return held | {k | 1: swap(b, "chan", size, 1) for k, b in held.items()}


def solution(mesh):
    in_specs = (
        P("batch", None, None, "chan"),
        P(None, "chan"),
        P("chan"),
        P("chan"),
        P(None, None, None, "chan"),
        P("chan"),
        P("chan"),
        P("chan", None),
        P(),
        P(),
        P("batch", None, None, None),
        P("batch"),
        P("batch"),
    )
    out_specs = (
        P("batch", None, None, "chan"),
        P("batch", None, None, "chan"),
        P(None, "chan"),
        P("chan"),
        P("chan"),
        P(None, None, None, "chan"),
        P("chan"),
        P("chan"),
        P("chan", None),
        P("chan"),
        P("chan"),
    )
    n_batch, n_chan = mesh.shape["batch"], mesh.shape["chan"]

    def run(*args):
        return shards(n_batch, n_chan, *args)

    return jax.shard_map(run, mesh=mesh, in_specs=in_specs, out_specs=out_specs, check_vma=False)
```
